32 devices in a mesh: mp: 4 (over y, x), wide: 8 (over z, core).
Axes of the slice: x: 2, y: 2, z: 4, core: 2. Of those that a mesh axis runs over, the one named last changes fastest.
Arguments:
- tokens: bfloat16 [16384, 960], P(('mp', 'wide')), may hold values from -6 to 6
- cotangent: bfloat16 [16384, 960], P(('mp', 'wide')), may hold values from -6 to 6
- norm_gains: float32 [2, 960], replicated, may hold values from 0.5 to 1.5
- w_qkv: bfloat16 [960, 1600], P('mp', 'wide'), may hold values from -0.1875 to 0.1875
- w_out: bfloat16 [960, 960], P('wide', 'mp'), may hold values from -0.75 to 0.75
- w_gate: bfloat16 [960, 2560], P('mp', 'wide'), may hold values from -0.1875 to 0.1875
- w_up: bfloat16 [960, 2560], P('mp', 'wide'), may hold values from -0.1875 to 0.1875
- w_down: bfloat16 [2560, 960], P('wide', 'mp'), may hold values from -0.125 to 0.125
Outputs:
- block_out: float32 [16384, 960], P(('mp', 'wide'))
- input_grad: float32 [16384, 960], P(('mp', 'wide'))
- gain_grads: float32 [2, 960], replicated
- qkv_grad: float32 [960, 1600], P('mp', 'wide')
- out_grad: float32 [960, 960], P('wide', 'mp')
- gate_grad: float32 [960, 2560], P('mp', 'wide')
- up_grad: float32 [960, 2560], P('mp', 'wide')
- down_grad: float32 [2560, 960], P('wide', 'mp')
The draws below stay inside these ranges and needn't reach their ends.
All inputs are finite; a program needn't handle non-finite values.
Results may differ from the reference program's by a relative error of at most 0.025.
Values may be sent and summed in bfloat16 or wider, within the bound.
A program may use at most 192 MiB of HBM per device.

```python
import math
import jax
import jax.numpy as jnp
from jax import lax

D = 960
QUERY_HEADS = 15
KEY_HEADS = 5
HEAD_WIDTH = 64
FF = 2560
DEVICE_TOKENS = 512
GROUP_QUERIES = 3
QKV = 1600
TOKENS = 16384


def block_levels(rng, shape, shards, least, top_value):
    def one(dim, parts):
        heights = jax.random.uniform(jax.random.fold_in(jax.random.fold_in(rng, 6), dim), (parts,), jnp.float32, least / len(shards), top_value / len(shards))
        return jnp.repeat(jnp.exp(heights), shape[dim] // parts).reshape((-1,) + (1,) * (len(shape) - dim - 1))

    loudness = one(*shards[0])
    for cut in shards[1:]:
        loudness = loudness * one(*cut)
    return loudness


def noise(rng, dims, scale, limit, cuts=(), kind=jnp.bfloat16):
    values = scale * jax.random.normal(rng, dims, jnp.float32)
    if cuts:
        values = values * block_levels(rng, dims, cuts, -0.22, 0.18)
    return jnp.clip(values, -limit, limit).astype(kind)


def setup_inputs(seed: int = 0) -> dict:
    streams_of = jax.random.split(jax.random.key(seed), 9)
    return {
        "tokens": noise(streams_of[0], (TOKENS, D), 1.0, 6.0, ((0, 32),)),
        "cotangent": noise(streams_of[1], (TOKENS, D), 1.0, 6.0, ((0, 32),)),
        "norm_gains": jnp.clip(1.0 + 0.1 * jax.random.normal(streams_of[2], (2, D), jnp.float32), 0.5, 1.5),
        "w_qkv": noise(streams_of[3], (D, QKV), D ** -0.5, 0.1875, ((0, 4), (1, 8))),
        "w_out": noise(streams_of[4], (QUERY_HEADS * HEAD_WIDTH, D), (QUERY_HEADS * HEAD_WIDTH // 16) ** -0.5, 0.75, ((0, 8), (1, 4))),
        "w_gate": noise(streams_of[5], (D, FF), D ** -0.5, 0.1875, ((0, 4), (1, 8))),
        "w_up": noise(streams_of[6], (D, FF), D ** -0.5, 0.1875, ((0, 4), (1, 8))),
        "w_down": noise(streams_of[7], (FF, D), FF ** -0.5, 0.125, ((0, 8), (1, 4))),
    }


@jax.custom_vjp
def lower_precision(v):
    return lax.optimization_barrier(v.astype(jnp.bfloat16)).astype(jnp.float32)

@jax.custom_vjp
def low_back(v):
    return v

def low_keep(v):
    return (lower_precision(v), None)

def low_pass(kept, grad):
    return (grad,)

def back_keep(v):
    return (v, None)

def back_low(kept, grad):
    return (lower_precision(grad),)
lower_precision.defvjp(low_keep, low_pass)
low_back.defvjp(back_keep, back_low)
EPSILON = 1e-05
NEGATIVE = -1e+30
HIGHEST = lax.Precision.HIGHEST

def scale_rows(state, gain):
    factor = lax.rsqrt(lax.optimization_barrier(jnp.mean(state * state, axis=-1, keepdims=True)) + EPSILON)
    return state * factor * gain

def rotary_tables(count_of_rows):
    position = (jnp.arange(count_of_rows) % DEVICE_TOKENS).astype(jnp.float32)
    inverse = jnp.exp(jnp.arange(HEAD_WIDTH // 2).astype(jnp.float32) * (-2.0 * math.log(10000.0) / HEAD_WIDTH))
    angle = position[:, None] * inverse[None, :]
    return (jnp.cos(angle)[:, None, :], jnp.sin(angle)[:, None, :])

def apply_rotation(heads_in, cosine_table, sine_table):
    first = heads_in[..., :HEAD_WIDTH // 2]
    second = heads_in[..., HEAD_WIDTH // 2:]
    return jnp.concatenate([first * cosine_table - second * sine_table, second * cosine_table + first * sine_table], axis=-1)

def attend(operands):
    query_rows, rotated_keys, value_rows = operands
    keys_all = jnp.repeat(rotated_keys, GROUP_QUERIES, axis=1)
    values_all = jnp.repeat(value_rows, GROUP_QUERIES, axis=1)
    scores = jnp.einsum('qhd,khd->hqk', query_rows, keys_all, precision=HIGHEST) * (1.0 / math.sqrt(HEAD_WIDTH))
    causal = jnp.arange(DEVICE_TOKENS)[:, None] >= jnp.arange(DEVICE_TOKENS)[None, :]
    scores = low_back(jnp.where(causal[None], scores, NEGATIVE))
    probs = lower_precision(jax.nn.softmax(scores, axis=-1))
    return jnp.einsum('hqk,khd->qhd', probs, values_all, precision=HIGHEST)

def block(state, gains, weights):
    w_qkv, w_out, w_gate, w_up, w_down = weights
    count_of_rows = state.shape[0]
    normed = lower_precision(scale_rows(state, gains[0]))
    joined_parts = low_back(jnp.dot(normed, w_qkv, precision=HIGHEST))
    cosine_table, sine_table = rotary_tables(count_of_rows)
    query_rows = lower_precision(apply_rotation(joined_parts[:, :QUERY_HEADS * HEAD_WIDTH].reshape(count_of_rows, QUERY_HEADS, HEAD_WIDTH), cosine_table, sine_table))
    rotated_keys = lower_precision(apply_rotation(joined_parts[:, QUERY_HEADS * HEAD_WIDTH:(QUERY_HEADS + KEY_HEADS) * HEAD_WIDTH].reshape(count_of_rows, KEY_HEADS, HEAD_WIDTH), cosine_table, sine_table))
    value_rows = lower_precision(joined_parts[:, (QUERY_HEADS + KEY_HEADS) * HEAD_WIDTH:].reshape(count_of_rows, KEY_HEADS, HEAD_WIDTH))
    item_count = count_of_rows // DEVICE_TOKENS
    reshaped_input = (query_rows.reshape(item_count, DEVICE_TOKENS, QUERY_HEADS, HEAD_WIDTH), rotated_keys.reshape(item_count, DEVICE_TOKENS, KEY_HEADS, HEAD_WIDTH), value_rows.reshape(item_count, DEVICE_TOKENS, KEY_HEADS, HEAD_WIDTH))
    heads = lax.map(jax.checkpoint(attend), reshaped_input).reshape(count_of_rows, QUERY_HEADS * HEAD_WIDTH)
    heads = lower_precision(low_back(heads))
    middle = state + low_back(jnp.dot(heads, w_out, precision=HIGHEST))
    normed_two = lower_precision(scale_rows(middle, gains[1]))
    gate = low_back(jnp.dot(normed_two, w_gate, precision=HIGHEST))
    up_part = low_back(jnp.dot(normed_two, w_up, precision=HIGHEST))
    hidden = lower_precision(jax.nn.silu(gate) * up_part)
    return middle + low_back(jnp.dot(hidden, w_down, precision=HIGHEST))

def layer_pair(state, gains, weights):
    return block(block(state, gains, weights), gains, weights)

def reference(tokens, cotangent, norm_gains, w_qkv, w_out, w_gate, w_up, w_down):
    weights = tuple((item.astype(jnp.float32) for item in (w_qkv, w_out, w_gate, w_up, w_down)))
    gains = norm_gains.astype(jnp.float32)
    group_rows = 4 * DEVICE_TOKENS
    steps_count = TOKENS // group_rows
    inputs = tokens.astype(jnp.float32).reshape(steps_count, group_rows, D)
    upstream = cotangent.astype(jnp.float32).reshape(steps_count, group_rows, D)

    def step(carry, operands):
        state, incoming = operands
        result, pull = jax.vjp(layer_pair, state, gains, weights)
        state_grad, gain_part, weight_part = pull(incoming)
        gain_total = carry[0] + gain_part
        weight_total = tuple((jnp.add(first, second) for first, second in zip(carry[1], weight_part)))
        return ((gain_total, weight_total), (result, state_grad))
    start = (jnp.zeros((2, D), jnp.float32), tuple((jnp.zeros(item.shape, jnp.float32) for item in weights)))
    (gain_total, weight_total), (results, state_grads) = lax.scan(step, start, (inputs, upstream))
    return (results.reshape(TOKENS, D), state_grads.reshape(TOKENS, D), gain_total, weight_total[0], weight_total[1], weight_total[2], weight_total[3], weight_total[4])
```

```python
import functools
import math
import types

import jax
import jax.numpy as jnp
from jax import lax
from jax.experimental import pallas as pl
from jax.experimental.pallas import tpu as pltpu
from jax.sharding import PartitionSpec as P

EPSILON = 1e-05
NEGATIVE = -1e30
HEAD = 64
QUERY_HEADS = 15
KEY_HEADS = 5
GROUP = 3
LANES = 128
BLOCK = 256
BF = jnp.bfloat16
F32 = jnp.float32
MESH = pl.DeviceIdType.MESH
VMEM_BYTES = 62 * 2**20


def dot(a, b, contract):
    return lax.dot_general(a, b, ((contract[:1], contract[1:]), ((), ())), preferred_element_type=F32)


def nn(a, b):
    return dot(a, b, (1, 0))


def nt(a, b):
    return dot(a, b, (1, 1))


def tn(a, b):
    return dot(a, b, (0, 0))


def at(start, size):
    return pl.ds(pl.multiple_of(start, size), size)


def loop(count, body, **kw):
    def step(i, _):
        body(i)
        return 0

    lax.fori_loop(0, count, step, 0, **kw)


class Sizes:
    def __init__(self, tokens, width, qkv, heads, hidden, wide):
        self.tokens, self.width = tokens, width
        self.padded = 4 * BLOCK
        self.quarter = width // 4
        self.qkv, self.heads, self.hidden, self.wide = qkv, heads, hidden, wide
        up = lambda v: -(-v // 16) * 16
        self.rows_of = (qkv // wide, heads // wide, hidden // wide, hidden // wide, hidden // wide)
        self.blocks = tuple(up(v) for v in self.rows_of)
        self.starts = tuple(sum(self.blocks[:k]) for k in range(5))
        self.rows = sum(self.blocks)
        self.qkv_padded = -(-qkv // LANES) * LANES
        self.n = wide // 2
        self.group = 640 // self.rows_of[2]


def normalize(z, state, gain_row, out):
    def body(i):
        rows = at(i * 64, 64)
        s = state[rows, :].astype(F32)
        r = lax.rsqrt(jnp.sum(s * s, axis=1, keepdims=True) * (1.0 / z.width) + EPSILON)
        out[rows, :] = (s * r * gain_row).astype(BF)

    loop(z.tokens // 64, body)


def normalize_back(z, state, gain_row, incoming, passed, out, gain_out):
    def body(i):
        rows = at(i * 64, 64)
        s = state[rows, :].astype(F32)
        g = incoming[rows, :]
        r = lax.rsqrt(jnp.sum(s * s, axis=1, keepdims=True) * (1.0 / z.width) + EPSILON)
        n = s * r
        gn = g * n
        c = g * gain_row
        m = jnp.sum(gn * gain_row, axis=1, keepdims=True) * (1.0 / z.width)
        out[rows, :] = passed[rows, :].astype(F32) + r * (c - n * m)
        gain_out[...] += jnp.sum(gn.reshape(8, 8, z.padded), axis=0)

    loop(z.tokens // 64, body)


def half_mask(rows):
    return lax.broadcasted_iota(jnp.int32, (rows, LANES), 1) < HEAD


def swap_pairs(v):
    lane = lax.rem(lax.broadcasted_iota(jnp.int32, v.shape, 1), HEAD)
    return jnp.where(lane < HEAD // 2, pltpu.roll(v, LANES - HEAD // 2, 1), pltpu.roll(v, HEAD // 2, 1))


def project_qkv(z, normed, w_qkv, table, qkv, query, keys, values):
    cos, sin = table
    w = z.qkv
    half = 5 * LANES
    for start in (0, half, 2 * half):
        size = min(half, w - start)
        qkv[:, start : start + size] = nt(normed[...], w_qkv[start : start + size, :])

    def body(i):
        rows = at(i * 64, 64)
        lo = half_mask(64)
        c, s = cos[rows, :], sin[rows, :]
        zero = jnp.zeros((64, LANES), F32)

        def place(target, g, v, low):
            other = pltpu.roll(v, HEAD, 1)
            a, b = (v, other) if low else (other, v)
            target[0, g, rows, :] = jnp.where(lo, a, zero).astype(BF)
            target[1, g, rows, :] = jnp.where(lo, zero, b).astype(BF)

        for m in range(10):
            v = qkv[rows, m * LANES : (m + 1) * LANES]
            v = v * c + swap_pairs(v) * s
            if m < 7:
                query[rows, m * LANES : (m + 1) * LANES] = (v * (HEAD**-0.5)).astype(BF)
            elif m == 7:
                query[rows, m * LANES : (m + 1) * LANES] = jnp.where(lo, v * (HEAD**-0.5), zero).astype(BF)
                place(keys, 0, v, False)
            else:
                place(keys, 2 * (m - 8) + 1, v, True)
                place(keys, 2 * (m - 8) + 2, v, False)
        for m in range(2):
            v = qkv[rows, (10 + m) * LANES : (11 + m) * LANES]
            place(values, 2 * m, v, True)
            place(values, 2 * m + 1, v, False)
        v = qkv[rows, 12 * LANES : 13 * LANES]
        place(values, 4, v, True)

    loop(z.tokens // 64, body)


def causal(rows):
    return lax.broadcasted_iota(jnp.int32, (rows, rows), 0) >= lax.broadcasted_iota(jnp.int32, (rows, rows), 1)


def attend(z, r, first, count):
    t = z.tokens // 2
    query, keys, values, weights = r.query, r.keys, r.values, r.weights

    def one(m, parity):
        cols = at(m * LANES, LANES)
        h = 2 * m + parity
        g = h // GROUP
        mask = half_mask(z.tokens)
        own = mask if parity == 0 else jnp.logical_not(mask)
        value = jnp.where(own, values[parity, g], jnp.ones((), BF))
        s = nt(query[:t, cols], keys[parity, g, :t, :])
        s = jnp.where(causal(t), s, NEGATIVE)
        p = jnp.exp(s - jnp.max(s, axis=1, keepdims=True)).astype(BF)
        weights[h, 0] = p
        top = nn(p, value[:t])
        a = nt(query[t:, cols], keys[parity, g, :t, :])
        b = nt(query[t:, cols], keys[parity, g, t:, :])
        b = jnp.where(causal(t), b, NEGATIVE)
        high = jnp.max(jnp.maximum(a, b), axis=1, keepdims=True)
        pa = jnp.exp(a - high).astype(BF)
        pb = jnp.exp(b - high).astype(BF)
        weights[h, 1] = pa
        weights[h, 2] = pb
        return top, nn(pa, value[:t]) + nn(pb, value[t:])

    def finish(m, low, high):
        cols = at(m * LANES, LANES)
        lo = half_mask(t)
        for k in range(2):
            rows = slice(k * t, (k + 1) * t)
            inv = 1.0 / pltpu.roll(jnp.where(lo, high[k], low[k]), HEAD, 1)
            r.inverse[rows, cols] = inv
            r.heads[rows, cols] = (jnp.where(lo, low[k], high[k]) * inv).astype(BF)

    def pair(i):
        finish(first + i, one(first + i, 0), one(first + i, 1))

    last = QUERY_HEADS // 2
    loop(min(first + count, last) - first, pair)
    if first + count > last:
        empty = jnp.where(half_mask(t), 1.0, 0.0)
        finish(last, one(last, 0), (empty, empty))


def forward_steps(z, r):
    chunk = r.chunk

    def start():
        normalize(z, r.state, r.gains[0:1, :], r.normed)

    def qkv():
        r.need_qkv()
        project_qkv(z, r.normed, r.w_qkv, (r.cos, r.sin), r.qkv, r.query, r.keys, r.values)

    def heads(first):
        return lambda: attend(z, r, first, 2)

    def out():
        r.need_out()
        for n in range(2):
            cols = slice(n * 512, (n + 1) * 512)
            r.middle[:, cols] = r.state[:, cols].astype(F32) + nn(r.heads[:, : z.heads], r.w_out[:, cols])
        normalize(z, r.middle, r.gains[1:2, :], r.normed2)

    def gate_up(i):
        cols = at(i * chunk, chunk)
        gate = nt(r.normed2[...], r.gate_block(i))
        up = nt(r.normed2[...], r.up_block(i))
        r.gate[:, cols] = gate.astype(BF)
        r.up[:, cols] = up.astype(BF)
        r.hidden[:, cols] = (gate * jax.nn.sigmoid(gate) * up).astype(BF)

    def ffn():
        r.need_gate()
        loop(z.hidden // chunk, gate_up)

    def some(first, count):
        return lambda: loop(count, lambda i: gate_up(first + i))

    def down():
        r.need_down()
        r.down()

    if r.halves:
        half = z.hidden // chunk // 2
        return [start, qkv, heads(0), heads(2), heads(4), heads(6), out, some(0, half), some(half, half), down]
    return [start, qkv, lambda: attend(z, r, 0, 8), out, ffn, down]


def forward(z, r):
    for step in forward_steps(z, r):
        step()


def attend_back(z, r):
    t = z.tokens // 2
    query, keys, values, weights, scaled, heads = r.query, r.keys, r.values, r.weights, r.scaled, r.heads
    query_grad, key_grad, value_grad = r.query_grad, r.key_grad, r.value_grad
    key_grad[...] = jnp.zeros_like(key_grad)
    value_grad[...] = jnp.zeros_like(value_grad)

    first, second = slice(0, t), slice(t, 2 * t)

    def one(m, parity):
        h = 2 * m + parity
        g = h // GROUP
        cols = at(m * LANES, LANES)
        key = keys.at[parity, g]
        value = values.at[parity, g]
        mask = half_mask(2 * t)
        own = mask if parity == 0 else jnp.logical_not(mask)
        both = scaled[:, cols].astype(F32) * heads[:, cols].astype(F32)
        delta = jnp.sum(jnp.where(own, both, 0.0), axis=1, keepdims=True)

        def grad(tile, rows, other):
            w = weights[h, tile]
            dp = nt(scaled[rows, cols], value[other, :])
            return (w.astype(F32) * (dp - delta[rows])).astype(BF), w

        s00, w00 = grad(0, first, first)
        s10, w10 = grad(1, second, first)
        s11, w11 = grad(2, second, second)
        q1, q2 = query[first, cols], query[second, cols]
        d1, d2 = scaled[first, cols], scaled[second, cols]
        key_grad[parity, g, first, :] += tn(s00, q1) + tn(s10, q2)
        key_grad[parity, g, second, :] += tn(s11, q2)
        value_grad[parity, g, first, :] += tn(w00, d1) + tn(w10, d2)
        value_grad[parity, g, second, :] += tn(w11, d2)
        return nn(s00, key[first, :]), nn(s10, key[first, :]) + nn(s11, key[second, :])

    def pair(m):
        cols = at(m * LANES, LANES)
        a, b = one(m, 0), one(m, 1)
        query_grad[first, cols] = a[0] + b[0]
        query_grad[second, cols] = a[1] + b[1]

    m = QUERY_HEADS // 2
    loop(m, pair)
    cols = slice(m * LANES, (m + 1) * LANES)
    query_grad[first, cols], query_grad[second, cols] = one(m, 0)


def backward(z, r):
    ffn_grad = r.ffn_grad

    def rounded(i):
        rows = at(i * 64, 64)
        ffn_grad[rows, :] = r.grad[rows, :].astype(BF)

    if r.grad is not ffn_grad:
        loop(z.tokens // 64, rounded)
    r.need_down()
    r.need_kept()

    def ffn(n):
        cols = at(n * 512, 512)
        back = nt(ffn_grad[...], r.w_down[cols, :])
        gate = r.gate[:, cols].astype(F32)
        up = r.up[:, cols].astype(F32)
        s = jax.nn.sigmoid(gate)
        r.gate[:, cols] = (back * up * s * (1.0 + gate * (1.0 - s))).astype(BF)
        r.up[:, cols] = (back * gate * s).astype(BF)

    loop(z.hidden // 512, ffn)
    r.ffn_done()
    r.need_gate()

    def into(n):
        cols = at(n * 512, 512)
        r.normed_grad[:, cols] = nn(r.gate[...], r.w_gate[:, cols]) + nn(r.up[...], r.w_up[:, cols])

    loop(z.padded // 512, into)
    r.need_middle()
    normalize_back(z, r.middle, r.gains[1:2, :], r.normed_grad, r.grad, r.middle_grad, r.gain_out.at[1])

    def rounded2(i):
        rows = at(i * 64, 64)
        r.attn_back[rows, :] = r.middle_grad[rows, :].astype(BF)

    loop(z.tokens // 64, rounded2)
    r.need_attention()
    r.need_out()
    w = z.heads
    for start, size in ((0, 512), (512, w - 512)):
        cols = slice(start, start + size)
        back = nt(r.attn_back[...], r.w_out[cols, :])
        r.scaled[:, cols] = (back * r.inverse[:, cols]).astype(BF)
    r.scaled[:, w:] = jnp.zeros((z.tokens, z.padded - w), BF)

    attend_back(z, r)

    r.attention_done()

    def unrotate(i):
        rows = at(i * 64, 64)
        lo = half_mask(64)
        c, s = r.cos[rows, :], r.sin[rows, :]

        def turn(v):
            return v * c - swap_pairs(v) * s

        def joined(ref, g):
            a, b = ref[0, g, rows, :], ref[1, g, rows, :]
            return jnp.where(lo, a + pltpu.roll(b, HEAD, 1), 0.0), jnp.where(lo, 0.0, b + pltpu.roll(a, HEAD, 1))

        def put(m, v):
            r.qkv_back[rows, m * LANES : (m + 1) * LANES] = v.astype(BF)

        k = [joined(r.key_grad, g) for g in range(KEY_HEADS)]
        v = [joined(r.value_grad, g) for g in range(KEY_HEADS)]
        scale = HEAD**-0.5
        for m in range(7):
            put(m, turn(r.query_grad[rows, m * LANES : (m + 1) * LANES] * scale))
        last = jnp.where(lo, r.query_grad[rows, 7 * LANES : 8 * LANES] * scale, 0.0)
        put(7, turn(last + k[0][1]))
        put(8, turn(k[1][0] + k[2][1]))
        put(9, turn(k[3][0] + k[4][1]))
        put(10, v[0][0] + v[1][1])
        put(11, v[2][0] + v[3][1])
        put(12, v[4][0])

    loop(z.tokens // 64, unrotate)
    r.need_qkv()
    for n in range(2):
        cols = slice(n * 512, (n + 1) * 512)
        r.normed_grad[:, cols] = nn(r.qkv_back[:, : z.qkv], r.w_qkv[:, cols])
    normalize_back(z, r.state, r.gains[0:1, :], r.normed_grad, r.middle_grad, r.grad_in, r.gain_out.at[0])


def kept_shapes(z):
    t, d, f = z.tokens, z.padded, z.hidden
    return dict(
        query=((t, d), BF),
        keys=((2, KEY_HEADS, t, LANES), BF),
        values=((2, KEY_HEADS, t, LANES), BF),
        weights=((QUERY_HEADS, 3, t // 2, t // 2), BF),
        inverse=((t, d), F32),
        heads=((t, d), BF),
        middle=((t, d), F32),
        gate=((t, f), BF),
        up=((t, f), BF),
    )


def layer_shapes(z):
    t, d, f = z.tokens, z.padded, z.hidden
    return dict(kept_shapes(z), normed=((t, d), BF), normed2=((t, d), BF), hidden=((t, f), BF))


def weight_shapes(z):
    d, f = z.padded, z.hidden
    return dict(w_qkv=((z.qkv, d), BF), w_out=((z.heads, d), BF), w_gate=((f, d), BF), w_up=((f, d), BF), w_down=((f, d), BF))


def tables(z):
    t, d = z.tokens, z.padded
    return dict(gains=((2, d), F32), cos=((t, LANES), F32), sin=((t, LANES), F32))


def blocks_shape(z):
    return ((2, 2, z.n, 2, z.rows, BLOCK), BF)


def rows_first(z):
    t, d, f = z.tokens, z.padded, z.hidden
    left = dict(qkv_back=((t, z.qkv_padded), BF), heads=((t, d), BF), gate=((t, f), BF), up=((t, f), BF), hidden=((t, f), BF))
    right = dict(normed=((t, d), BF), attn_back=((t, d), BF), normed2=((t, d), BF), ffn_grad=((t, d), BF))
    return left, right


def make_call(body, ins, outs, scratch, in_vmem, sems, **params):
    n_in, n_out, n_s = list(ins), list(outs), list(scratch)

    def kernel(*refs):
        a, b, c = len(n_in), len(n_in) + len(n_out), len(n_in) + len(n_out) + len(n_s)
        group = lambda names, part: types.SimpleNamespace(**dict(zip(names, part)))
        body(group(n_in, refs[:a]), group(n_out, refs[a:b]), group(n_s, refs[b:c]), refs[c:])

    spec = lambda n: pl.BlockSpec(memory_space=pltpu.VMEM if n in in_vmem else pl.ANY)
    call = pl.pallas_call(
        kernel,
        out_shape=[jax.ShapeDtypeStruct(*outs[n]) for n in n_out],
        in_specs=[spec(n) for n in n_in],
        out_specs=[spec(n) for n in n_out],
        scratch_shapes=[pltpu.VMEM(*scratch[n]) for n in n_s] + [pltpu.SemaphoreType.DMA(s) for s in sems],
        compiler_params=pltpu.CompilerParams(vmem_limit_bytes=VMEM_BYTES, **params),
    )
    return lambda **vals: dict(zip(n_out, call(*[vals[n] for n in n_in])))


class Copies:
    def __init__(self, sems):
        self.sems, self.used, self.open = sems, 0, {}

    def start(self, src, dst):
        key = self.used
        self.used += 1
        self.open[key] = pltpu.make_async_copy(src, dst, self.sems.at[key])
        self.open[key].start()
        return key

    def wait(self, keys):
        for key in keys:
            if key in self.open:
                self.open.pop(key).wait()

    def later(self, keys):
        return lambda: self.wait(keys)

    def finish(self):
        self.wait(list(self.open))


SMALL = ("gains", "cos", "sin", "tokens")


def middle_kernel(z):
    t, d = z.tokens, z.padded
    kept = kept_shapes(z)
    ins = dict(tables(z), tokens=((t, d), BF), state=((t, d), F32), grad=((t, d), BF))
    ins.update(gathered=blocks_shape(z), dense_qkv=((z.qkv, d), BF), dense_out=((z.heads, d), BF))
    ins.update({"first_" + n: v for n, v in kept.items()})
    left, right = rows_first(z)
    both = dict(left, **right)
    outs = dict(result=((t, d), F32), grad_in=((t, d), F32), gain=((8, d), F32))
    outs.update({n + "2": v for n, v in both.items() if n != "ffn_grad"})
    outs.update({n + "1": both[n] for n in ("qkv_back", "attn_back", "gate", "up", "ffn_grad")})
    scratch = dict(layer_shapes(z), **weight_shapes(z), state=((t, d), F32), grad=((t, d), BF))
    scratch.update(qkv=((t, z.qkv_padded), F32), result=((t, d), F32), gain_out=((2, 8, d), F32))
    scratch.update(key_grad=((2, KEY_HEADS, t, LANES), F32), value_grad=((2, KEY_HEADS, t, LANES), F32))

    def body(i, o, s, sems):
        cps = Copies(sems[0])
        state = cps.start(i.state, s.state)
        w = start_weights(z, cps, i, s)
        grad = cps.start(i.grad, s.grad)
        none = lambda: None
        r = types.SimpleNamespace(**vars(s))
        vars(r).update(w, gains=i.gains, cos=i.cos, sin=i.sin, chunk=512, halves=False)
        r.gate_block = lambda n: s.w_gate[at(n * 512, 512), :]
        r.up_block = lambda n: s.w_up[at(n * 512, 512), :]

        def down():
            def last(n):
                cols = at(n * 512, 512)
                s.result[:, cols] = s.middle[:, cols] + nn(s.hidden[...], s.w_down[:, cols])

            loop(z.padded // 512, last)

        r.down = down
        cps.wait([state])
        forward(z, r)
        outs_now = [cps.start(s.result, o.result), cps.start(s.normed2, o.normed22), cps.start(s.hidden, o.hidden2)]
        heads_out = cps.start(s.heads, o.heads2)
        outs_now.append(cps.start(s.normed, o.normed2))
        s.gain_out[...] = jnp.zeros_like(s.gain_out)
        cps.wait([grad] + outs_now)

        back = types.SimpleNamespace(**vars(r))
        back.qkv_back = s.hidden.at[:, : z.qkv_padded]
        vars(back).update(scaled=s.normed2, attn_back=s.normed, normed_grad=s.result, middle_grad=s.middle, query_grad=s.qkv.at[:, :d], grad_in=s.state)
        vars(back).update(ffn_grad=s.grad, need_kept=none, need_middle=none, need_attention=none)
        ffn_out = []
        loads = {}

        def ffn_done():
            ffn_out.extend([cps.start(s.gate, o.gate2), cps.start(s.up, o.up2)])

        def load(n):
            loads[n] = cps.start(getattr(i, "first_" + n), getattr(s, n))

        def attention_done():
            cps.wait(ffn_out + [heads_out])
            for n in ("gate", "up", "inverse", "heads", "query", "keys", "values", "weights"):
                load(n)

        back.ffn_done, back.attention_done = ffn_done, attention_done
        backward(z, back)
        load("middle")
        factors = [cps.start(back.attn_back, o.attn_back2), cps.start(back.qkv_back, o.qkv_back2)]

        first = types.SimpleNamespace(**vars(back))
        vars(first).update(grad=s.state, state=i.tokens)
        first.need_kept = cps.later([loads["gate"], loads["up"]])
        first.need_middle = cps.later([loads["middle"]] + factors)
        first.need_attention = cps.later([loads[n] for n in ("inverse", "heads", "query", "keys", "values", "weights")])
        first.attention_done = none

        def ffn_done1():
            cps.start(s.gate, o.gate1)
            cps.start(s.up, o.up1)
            cps.start(s.grad, o.ffn_grad1)

        first.ffn_done = ffn_done1
        backward(z, first)
        cps.start(s.state, o.grad_in)
        cps.start(back.attn_back, o.attn_back1)
        cps.start(first.qkv_back, o.qkv_back1)
        o.gain[...] = jnp.zeros_like(o.gain)
        o.gain[0:1, :] = jnp.sum(s.gain_out[0], axis=0, keepdims=True)
        o.gain[1:2, :] = jnp.sum(s.gain_out[1], axis=0, keepdims=True)
        cps.finish()

    return make_call(body, ins, outs, scratch, SMALL + ("gain",), [(80,)])


def start_weights(z, cps, i, s):
    def blocks(w, k):
        w = w.reshape(z.n, 2, z.blocks[k], z.padded)
        rows = pl.ds(z.starts[k], z.blocks[k])
        return [cps.start(i.gathered.at[q // 2, q % 2, :, :, rows], w.at[:, :, :, q * BLOCK : (q + 1) * BLOCK]) for q in range(4)]

    qkv = [cps.start(i.dense_qkv, s.w_qkv)]
    out = [cps.start(i.dense_out, s.w_out)]
    gate = blocks(s.w_gate, 2) + blocks(s.w_up, 3)
    down = blocks(s.w_down, 4)
    return dict(need_qkv=cps.later(qkv), need_out=cps.later(out), need_gate=cps.later(gate), need_down=cps.later(down))


class Place:
    def __init__(self, n):
        mp, w = lax.axis_index("mp"), lax.axis_index("wide")
        self.n = n
        self.x, self.y, self.c, self.z = lax.rem(mp, 2), mp // 2, lax.rem(w, 2), w // 2

    def dev(self, x=None, y=None, z=None, c=None):
        x = self.x if x is None else x
        y = self.y if y is None else y
        z = self.z if z is None else z
        c = self.c if c is None else c
        return {"mp": y * 2 + x, "wide": z * 2 + c}

    def partner(self, axis):
        return self.dev(**{axis: 1 - getattr(self, axis)})

    def greet(self):
        bar = pltpu.get_barrier_semaphore()

        def signal(device):
            pl.semaphore_signal(bar, inc=1, device_id=device, device_id_type=MESH)

        for axis in "xyc":
            signal(self.partner(axis))

        @pl.when(self.z > 0)
        def _():
            signal(self.dev(z=self.z - 1))

        @pl.when(self.z < self.n - 1)
        def _():
            signal(self.dev(z=self.z + 1))

        pl.semaphore_wait(bar, 3 + jnp.where(self.z > 0, 1, 0) + jnp.where(self.z < self.n - 1, 1, 0))


def row_chunks(sizes, per):
    out, r = [], 0
    for s, p in zip(sizes, per):
        u = s // 16
        for k in range(p):
            size = (u // p + (1 if k < u % p else 0)) * 16
            out.append((r, size))
            r += size
    return out


SLACK = 1


def run_stages(entries):
    for entry in sorted(entries, key=lambda e: e[:2]):
        entry[2]()


def shares(units, weights):
    out, done, used = [], 0, 0
    for w in weights:
        done += w
        end = round(units * done / sum(weights))
        out.append(end - used)
        used = end
    return out


def row_chunks(start, rows, parts, orders):
    out, r = [], start
    for k, units in enumerate(shares(rows // 16, [1] * parts)):
        for order, u in zip(orders[k % len(orders)], shares(units, [1] * len(orders[0]))):
            if u:
                out.append((r, 16 * u, order, k))
                r += 16 * u
    return out


GATHER_ORDERS = (("xzy", "yzx", "zxy"), ("xzy", "yzx", "zyx"))
GATHER_PARTS = 8


def gather_plan(p, g, k, piece, ss, rs):
    r0, rc, order, _ = piece
    n, rows = p.n, pl.ds(r0, rc)
    a1, a2 = [a for a in order if a != "z"]
    z_first = order[0] == "z"

    def one(zo, other=False):
        x = 1 - p.x if other and a1 == "x" else p.x
        y = 1 - p.y if other and a1 == "y" else p.y
        return g.at[y, x, zo, p.c, rows]

    def pair(zo, other=False, c=None):
        c = p.c if c is None else c
        if a1 == "x":
            return g.at[1 - p.y if other else p.y, :, zo, c, rows]
        return g.at[:, 1 - p.x if other else p.x, zo, c, rows]

    def copy(ref, dev, s, r):
        return pltpu.make_async_remote_copy(src_ref=ref, dst_ref=ref, send_sem=ss.at[k, s], recv_sem=rs.at[k, r], device_id=dev, device_id_type=MESH)

    along = one if z_first else pair
    up = lambda zo: copy(along(zo), p.dev(z=p.z + 1), zo, zo)
    down = lambda zo: copy(along(zo), p.dev(z=p.z - 1), n + zo, zo)
    line_in = lambda zo: copy(along(zo), p.partner("c"), zo, zo)
    first = lambda zo, other=False: copy(one(zo, other), p.partner(a1), 2 * n + zo, n + zo)
    second = lambda zo, other=False: copy(pair(zo, other), p.partner(a2), 3 * n + zo, 2 * n + zo)

    def sibling(other, c=None):
        c = p.c if c is None else c
        if a1 == "x":
            part = g.at[1 - p.y if other else p.y, :, :, c, rows]
        else:
            part = g.at[:, 1 - p.x if other else p.x, :, c, rows]
        o = 1 if other else 0
        return copy(part, p.partner("c"), 4 * n + o, 3 * n + o)

    def line(zo):
        @pl.when((zo <= p.z) & (p.z < n - 1))
        def _():
            up(zo).start()

        @pl.when((zo >= p.z) & (p.z > 0))
        def _():
            down(zo).start()

    def at_distance(d, body):
        @pl.when(p.z - d >= 0)
        def _():
            body(p.z - d)

        @pl.when(p.z + d < n)
        def _():
            body(p.z + d)

    stages = []
    if z_first:

        def start():
            line(p.z)
            first(p.z).start()

        stages.append((0, start))
        for d in range(1, n):

            def hop(d=d):
                def body(zo):
                    line_in(zo).wait_recv()
                    line(zo)
                    first(zo).start()

                at_distance(d, body)

            stages.append((d, hop))

        def cross():
            for zo in range(n):
                first(zo, True).wait_recv()
                second(zo).start()

        stages.append((n, cross))
    else:

        def start():
            first(p.z).start()

        def meet():
            first(p.z, True).wait_recv()
            line(p.z)
            second(p.z).start()

        stages += [(0, start), (1, meet)]
        for d in range(1, n):

            def hop(d=d):
                def body(zo):
                    line_in(zo).wait_recv()
                    line(zo)
                    second(zo).start()

                at_distance(d, body)

            stages.append((d + 1, hop))

    def halfway():
        sibling(False).start()

    def arrived():
        for zo in range(n):
            second(zo, True).wait_recv()
        sibling(True).start()

    def done():
        sibling(False, 1 - p.c).wait_recv()
        sibling(True, 1 - p.c).wait_recv()

    def drain():
        for zo in range(n):

            @pl.when((zo <= p.z) & (p.z < n - 1))
            def _():
                up(zo).wait_send()

            @pl.when((zo >= p.z) & (p.z > 0))
            def _():
                down(zo).wait_send()

            second(zo).wait_send()
            if z_first:
                first(zo).wait_send()
        if not z_first:
            first(p.z).wait_send()
        sibling(False).wait_send()
        sibling(True).wait_send()

    return stages + [(n + 1, halfway), (n + 1 + SLACK, arrived), (n + 2 + SLACK, done)], drain


def first_kernel(z):
    t, d, n = z.tokens, z.padded, z.n
    pieces = row_chunks(0, z.rows, GATHER_PARTS, GATHER_ORDERS)
    layer = layer_shapes(z)
    ins = dict(tables(z), tokens=((t, d), BF), shard=((z.rows, BLOCK), BF))
    outs = dict(layer, result=((t, d), F32), gathered=blocks_shape(z), dense_qkv=((z.qkv, d), BF), dense_out=((z.heads, d), BF))
    scratch = dict(layer, result=((t, d), F32), qkv=((t, z.qkv_padded), F32), blocks=blocks_shape(z))
    scratch.update(w_qkv=((z.qkv, d), BF), w_out=((z.heads, d), BF))
    last_of = [max(p[3] for p in pieces if p[0] < s + b) for s, b in zip(z.starts, z.blocks)]
    when_done = lambda part: part + n + 2 + SLACK

    def body(i, o, s, sems):
        local, ss, rs = sems
        cps = Copies(local)
        p = Place(n)
        own = cps.start(i.shard, s.blocks.at[p.y, p.x, p.z, p.c])
        p.greet()
        cps.wait([own])

        def dense(k, target):
            per = z.rows_of[k]
            for j in range(z.wide):
                for q in range(4):
                    rows = s.blocks[q // 2, q % 2, j // 2, j % 2, z.starts[k] : z.starts[k] + per, :]
                    target[j * per : (j + 1) * per, q * BLOCK : (q + 1) * BLOCK] = rows

        def block(k):
            start, per, some = z.starts[k], z.rows_of[k], z.group // 2

            def read(j):
                rows = []
                for e in range(z.group):
                    quarters = [s.blocks[q // 2, q % 2, j * some + e // 2, e % 2, start : start + per, :] for q in range(4)]
                    rows.append(jnp.concatenate(quarters, axis=1))
                return jnp.concatenate(rows, axis=0)

            return read

        none = lambda: None
        r = types.SimpleNamespace(**vars(s))
        vars(r).update(gains=i.gains, cos=i.cos, sin=i.sin, state=i.tokens, chunk=640, halves=True)
        vars(r).update(gate_block=block(2), up_block=block(3), need_gate=none, need_down=none)

        def need_qkv():
            dense(0, s.w_qkv)
            cps.start(s.w_qkv, o.dense_qkv)

        def need_out():
            dense(1, s.w_out)
            cps.start(s.w_out, o.dense_out)

        def down():
            read = block(4)
            s.result[...] = s.middle[...]

            def add(j):
                s.result[...] += nn(s.hidden[:, at(j * 640, 640)], read(j))

            loop(z.hidden // 640, add)

        vars(r).update(need_qkv=need_qkv, need_out=need_out, down=down)
        steps = forward_steps(z, r)
        ready = [when_done(part) + 0.5 for part in last_of]
        first = ready[0]
        gate = max(ready[3], first + 2)
        times = [0.5, first, first, first + 1, first + 1, first + 2, max(ready[1], first + 2), gate, gate, ready[4]]

        plans = [gather_plan(p, s.blocks, k, piece, ss, rs) for k, piece in enumerate(pieces)]
        entries = [(pieces[k][3] + at_time, k, f) for k, (stages, _) in enumerate(plans) for at_time, f in stages]
        entries += [(at_time, k, f) for k, (at_time, f) in enumerate(zip(times, steps))]

        def out_of(part):
            rows = [p for p in pieces if p[3] == part]
            span = pl.ds(rows[0][0], sum(p[1] for p in rows))
            return lambda: cps.start(s.blocks.at[:, :, :, :, span], o.gathered.at[:, :, :, :, span])

        entries += [(when_done(part) + 0.25, part, out_of(part)) for part in range(GATHER_PARTS)]

        def keep(*names):
            return lambda: [cps.start(getattr(s, m), getattr(o, m)) for m in names]

        entries += [(times[5] + 0.1, 20, keep("normed", "query", "keys", "values", "weights", "inverse", "heads"))]
        entries += [(times[6] + 0.2, 20, keep("middle", "normed2")), (times[8] + 0.3, 20, keep("gate", "up", "hidden"))]
        run_stages(entries)
        cps.start(s.result, o.result)
        for _, drain in plans:
            drain()
        cps.finish()

    sems = [(40,), (len(pieces), 4 * n + 2), (len(pieces), 3 * n + 2)]
    return make_call(body, ins, outs, scratch, SMALL, sems, collective_id=1, has_side_effects=True)


REDUCE_ORDERS = (("yzx", "xzy", "yxz"), ("yzx", "xzy", "xyz"))


def add_into(target, extra):
    target[...] = (target[...].astype(F32) + extra[...].astype(F32)).astype(target.dtype)


def reduce_plan(p, t, bufs, out, k, piece, ss, rs):
    r0, rc, order = piece
    n, rows = p.n, pl.ds(r0, rc)
    from_sibling, from_first, from_line, from_last = bufs
    a1 = [a for a in order if a != "z"][0]
    z_last = order[2] == "z"

    def pair(zo, other=False):
        if a1 == "y":
            return t.at[1 - p.y if other else p.y, :, zo, rows]
        return t.at[:, 1 - p.x if other else p.x, zo, rows]

    def one(zo, other=False):
        x = 1 - p.x if other and a1 == "y" else p.x
        y = 1 - p.y if other and a1 == "x" else p.y
        return t.at[y, x, zo, rows]

    def sib_part(zo, other):
        if a1 == "y":
            return from_sibling.at[1 - p.y if other else p.y, :, zo, rows]
        return from_sibling.at[:, 1 - p.x if other else p.x, zo, rows]

    def copy(src, dst, dev, s, r):
        return pltpu.make_async_remote_copy(src_ref=src, dst_ref=dst, send_sem=ss.at[k, s], recv_sem=rs.at[k, r], device_id=dev, device_id_type=MESH)

    a2 = "x" if a1 == "y" else "y"
    line_ref = one if z_last else pair
    line_slot = (lambda v: from_line.at[0, v, rows]) if z_last else (lambda v: from_line.at[:, v, rows])
    across = lambda zo: copy(pair(zo, True), from_first.at[:, zo, rows], p.partner(a1), 1 + zo, 1 + zo)
    last = lambda zo: copy(one(zo, True), from_last.at[zo, rows], p.partner(a2), 1 + n + zo, 1 + n + zo)

    def send_up(zo):
        return copy(line_ref(zo), line_slot(zo), p.dev(z=p.z + 1), 1 + 2 * n + zo, 1 + 2 * n + zo)

    def send_down(zo):
        slot = jnp.where(zo == p.z - 1, n, zo)
        return copy(line_ref(zo), line_slot(slot), p.dev(z=p.z - 1), 1 + 2 * n + zo, 1 + 2 * n + slot)

    def line_in(slot):
        copy(line_slot(slot), line_slot(slot), p.partner("c"), 0, 1 + 2 * n + slot).wait_recv()

    def meet():
        def send(zo):
            add_into(pair(zo, True), sib_part(zo, True))
            across(zo).start()

        def keep(zo):
            add_into(pair(zo), sib_part(zo, False))

        loop(n, send)
        loop(n, keep)

    def crossed():
        def body(zo):
            across(zo).wait_recv()
            add_into(pair(zo), from_first.at[:, zo, rows])

        loop(n, body)
        if z_last:
            for zo in range(n):
                last(zo).start()

    def other_half():
        def body(zo):
            last(zo).wait_recv()
            add_into(one(zo), from_last.at[zo, rows])

        loop(n, body)

    def hop(s):
        @pl.when(p.z == s)
        def _():
            def body(i):
                zo = n - 1 - i

                @pl.when(p.z > 0)
                def _():
                    line_in(zo)
                    add_into(line_ref(zo), line_slot(zo))

                send_up(zo).start()

            lax.fori_loop(0, n - 1 - s, lambda i, c: (body(i), c)[1], 0)

        @pl.when(p.z == n - 1 - s)
        def _():
            def body(zo):
                @pl.when(p.z < n - 1)
                def _():
                    line_in(zo)
                    add_into(line_ref(zo), line_slot(zo))

                send_down(zo).start()

            lax.fori_loop(0, n - 1 - s, lambda i, c: (body(i), c)[1], 0)

    def line_end():
        @pl.when(p.z > 0)
        def _():
            line_in(p.z)
            add_into(line_ref(p.z), line_slot(p.z))

        @pl.when(p.z < n - 1)
        def _():
            line_in(n)
            add_into(line_ref(p.z), line_slot(n))

    def final_send():
        last(p.z).start()

    def finish():
        total = one(p.z)[...].astype(F32)
        if not z_last:
            last(p.z).wait_recv()
            total = total + from_last[p.z, rows].astype(F32)
        out[rows, :] = total

    def drain():
        for zo in range(n):
            across(zo).wait_send()
            if z_last:
                last(zo).wait_send()

            @pl.when(zo > p.z)
            def _():
                send_up(zo).wait_send()

            @pl.when(zo < p.z)
            def _():
                send_down(zo).wait_send()

        if not z_last:
            last(p.z).wait_send()

    stages = [(0, meet), (1, crossed)]
    o = 2
    if z_last:
        stages.append((2, other_half))
    stages += [(o + s, functools.partial(hop, s)) for s in range(n - 1)]
    stages.append((o + n - 1, line_end))
    if not z_last:
        stages.append((o + n - 1, final_send))
    stages.append((o + n, finish))
    return stages, drain


def last_kernel(z):
    t, d, n = z.tokens, z.padded, z.n
    left, right = rows_first(z)
    both = dict(left, **right)
    ins = {m + k: v for m, v in both.items() for k in "12"}
    ins.update(gain=((8, d), F32))
    outs = dict(sums=((z.rows, BLOCK), F32), gains=((8, d), F32))
    two = lambda v: ((2 * t, v[0][1]), BF)
    scratch = {m: two(v) for m, v in both.items() if m not in ("gate", "up")}
    stage = max(z.rows_of)
    scratch.update(
        t=((2, 2, n, z.rows, BLOCK), BF),
        staged=((STAGED, 2, 2, stage, BLOCK), BF),
        from_sibling=((2, 2, n, z.rows, BLOCK), BF),
        from_first=((2, n, z.rows, BLOCK), BF),
        from_line=((2, n + 1, z.rows, BLOCK), BF),
        from_last=((n, z.rows, BLOCK), BF),
        gain_sent=((3, 8, d), F32),
        gain_in=((3, 8, d), F32),
        gain_all=((n, 8, d), F32),
    )
    order = (1, 4, 2, 3, 0)
    parts = {0: 2, 1: 1, 2: 2, 3: 2, 4: 2}
    pieces, part_of, starts = [], {}, {}
    slot = 1
    for k in order:
        starts[k] = slot
        for r0, rc, way, part in row_chunks(z.starts[k], z.blocks[k], parts[k], REDUCE_ORDERS):
            pieces.append((r0, rc, way, slot + part, k))
        slot += parts[k]

    def body(i, o, s, sems):
        local, ss, rs, sib_s, sib_r, gain_s, gain_r = sems
        cps = Copies(local)
        need = {}

        def load(m, into):
            target = getattr(s, into)
            need[m] = cps.later([cps.start(getattr(i, m + k), target.at[pl.ds((2 - int(k)) * t, t)]) for k in "12"])

        for m in ("heads", "attn_back", "hidden", "ffn_grad", "normed2", "normed", "qkv_back"):
            load(m, m)
        p = Place(n)
        p.greet()
        count = [0]

        def sibling(k, zo, slot):
            rows = pl.ds(z.starts[k], z.blocks[k])
            return pltpu.make_async_remote_copy(
                src_ref=s.staged.at[slot, :, :, pl.ds(0, z.blocks[k])],
                dst_ref=s.from_sibling.at[:, :, zo, rows],
                send_sem=sib_s.at[slot],
                recv_sem=sib_r.at[k, zo],
                device_id=p.partner("c"),
                device_id_type=MESH,
            )

        sent = {}

        def put(k, zo, slot, a, b):
            per = z.rows_of[k]
            own, other = jnp.where(p.c == 0, a, b).astype(BF), jnp.where(p.c == 0, b, a).astype(BF)
            for q in range(4):
                lanes = slice(q * BLOCK, (q + 1) * BLOCK)
                s.t[q // 2, q % 2, zo, z.starts[k] : z.starts[k] + per, :] = own[:, lanes]
                s.staged[slot, q // 2, q % 2, :per, :] = other[:, lanes]

        def terms(k):
            m_left = (s.qkv_back, s.heads, s.hidden, s.hidden, s.hidden)[k]
            m_right = (s.normed, s.attn_back, s.normed2, s.normed2, s.ffn_grad)[k]
            per = z.rows_of[k]
            if k in (0, 1):
                some = 1
            else:
                some = z.group // 2
            for first in range(0, n, some):
                width = 2 * per * some
                value = tn(m_left[:, first * 2 * per : first * 2 * per + width], m_right[...])
                for e in range(some):
                    zo = first + e
                    slot = count[0] % STAGED
                    if slot in sent:
                        sent.pop(slot).wait_send()
                    count[0] += 1
                    put(k, zo, slot, value[2 * e * per : (2 * e + 1) * per], value[(2 * e + 1) * per : (2 * e + 2) * per])
                    sent[slot] = sibling(k, zo, slot)
                    sent[slot].start()

        def work(k):
            names = (("normed", "qkv_back"), ("heads", "attn_back"), ("gate", "normed2"), ("up", "normed2"), ("hidden", "ffn_grad"))[k]

            def run():
                if k in (2, 3):
                    load(names[0], "hidden")
                for m in names:
                    need[m]()
                terms(k)

            return run

        def sibling_in(k):
            def run():
                for zo in range(n):
                    sibling(k, zo, 0).wait_recv()

            return run

        entries = [(starts[k] - 0.5 if k != order[0] else 0, 0, work(k)) for k in order]
        entries += [(starts[k], -1, sibling_in(k)) for k in order]
        bufs = (s.from_sibling, s.from_first, s.from_line, s.from_last)
        plans = [reduce_plan(p, s.t, bufs, o.sums, k, piece[:3], ss, rs) for k, piece in enumerate(pieces)]
        entries += [(pieces[k][3] + at_time, k, f) for k, (stages, _) in enumerate(plans) for at_time, f in stages]
        stages, gains_drain = gain_plan(p, i.gain, s, o.gains, gain_s, gain_r)
        entries += [(1 + k, 100, f) for k, f in enumerate(stages)]
        run_stages(entries)
        for _, drain in plans:
            drain()
        for c in sent.values():
            c.wait_send()
        gains_drain()
        cps.finish()

    sems = [(40,), (len(pieces), 1 + 3 * n), (len(pieces), 2 + 3 * n), (STAGED,), (5, n), (3 + 2 * n,), (3 + n,)]
    return make_call(body, ins, outs, scratch, ("gain", "sums", "gains"), sems, collective_id=2, has_side_effects=True)


STAGED = 4


def gain_plan(p, mine, s, out, ss, rs):
    n = p.n

    def exchange(k, axis):
        return pltpu.make_async_remote_copy(
            src_ref=s.gain_sent.at[k], dst_ref=s.gain_in.at[k], send_sem=ss.at[k], recv_sem=rs.at[k], device_id=p.partner(axis), device_id_type=MESH
        )

    def pass_on(zo, up):
        ref = s.gain_all.at[zo]
        sem = 3 + zo + (0 if up else n)
        dev = p.dev(z=p.z + 1 if up else p.z - 1)
        return pltpu.make_async_remote_copy(src_ref=ref, dst_ref=ref, send_sem=ss.at[sem], recv_sem=rs.at[3 + zo], device_id=dev, device_id_type=MESH)

    def line(zo):
        @pl.when((zo <= p.z) & (p.z < n - 1))
        def _():
            pass_on(zo, True).start()

        @pl.when((zo >= p.z) & (p.z > 0))
        def _():
            pass_on(zo, False).start()

    def begin():
        s.gain_sent[0] = mine[...]
        exchange(0, "c").start()

    def step(k, axis, follow):
        def run():
            exchange(k, axis).wait_recv()
            total = s.gain_sent[k] + s.gain_in[k]
            if follow:
                s.gain_sent[k + 1] = total
                exchange(k + 1, follow).start()
            else:
                s.gain_all[p.z] = total
                line(p.z)

        return run

    def hop(d):
        def take(zo):
            ref = s.gain_all.at[zo]
            pltpu.make_async_remote_copy(
                src_ref=ref, dst_ref=ref, send_sem=ss.at[0], recv_sem=rs.at[3 + zo], device_id=p.partner("c"), device_id_type=MESH
            ).wait_recv()
            line(zo)

        def run():
            @pl.when(p.z - d >= 0)
            def _():
                take(p.z - d)

            @pl.when(p.z + d < n)
            def _():
                take(p.z + d)

        return run

    def finish():
        total = s.gain_all[0]
        for zo in range(1, n):
            total = total + s.gain_all[zo]
        out[...] = total

    def drain():
        for k, axis in enumerate("cxy"):
            exchange(k, axis).wait_send()
        for zo in range(n):

            @pl.when((zo <= p.z) & (p.z < n - 1))
            def _():
                pass_on(zo, True).wait_send()

            @pl.when((zo >= p.z) & (p.z > 0))
            def _():
                pass_on(zo, False).wait_send()

    return [begin, step(0, "c", "x"), step(1, "x", "y"), step(2, "y", "")] + [hop(d) for d in range(1, n)] + [finish], drain


def pad_model(z, v):
    rows = v.shape[0]
    v = v.reshape(rows, 4, z.quarter)
    return jnp.pad(v, ((0, 0), (0, 0), (0, BLOCK - z.quarter))).reshape(rows, z.padded)


def unpad_model(z, v):
    rows = v.shape[0]
    return v.reshape(rows, 4, BLOCK)[:, :, : z.quarter].reshape(rows, z.width)


def rotary_tables(count_of_rows):
    position = jnp.arange(count_of_rows).astype(F32)
    inverse = jnp.exp(jnp.arange(HEAD // 2).astype(F32) * (-2.0 * math.log(10000.0) / HEAD))
    angle = position[:, None] * inverse[None, :]
    cos, sin = jnp.cos(angle), jnp.sin(angle)
    return jnp.concatenate([cos] * 4, axis=1), jnp.concatenate([-sin, sin] * 2, axis=1)


def local(wide, tokens, cotangent, norm_gains, w_qkv, w_out, w_gate, w_up, w_down):
    z = Sizes(tokens.shape[0], tokens.shape[1], w_qkv.shape[1] * wide, w_out.shape[0] * wide, w_gate.shape[1] * wide, wide)
    shards = (w_qkv.T, w_out, w_gate.T, w_up.T, w_down)
    packed = [jnp.pad(s, ((0, b - s.shape[0]), (0, BLOCK - s.shape[1]))) for s, b in zip(shards, z.blocks)]
    shard = jnp.concatenate(packed, axis=0)
    cos, sin = rotary_tables(z.tokens)
    small = dict(gains=pad_model(z, norm_gains), cos=cos, sin=sin, tokens=pad_model(z, tokens))
    grad = pad_model(z, cotangent)
    one = first_kernel(z)(shard=shard, **small)
    kept = {"first_" + n: one[n] for n in kept_shapes(z)}
    weights = {n: one[n] for n in ("gathered", "dense_qkv", "dense_out")}
    two = middle_kernel(z)(state=one["result"], grad=grad, **small, **kept, **weights)
    factors = {n + "1": one[n] for n in ("normed", "normed2", "heads", "hidden")}
    factors.update(two, ffn_grad2=grad)
    out = last_kernel(z)(**factors)
    sums = out["sums"]
    parts = [sums[s : s + r, : z.quarter] for s, r in zip(z.starts, z.rows_of)]
    return (
        unpad_model(z, two["result"]),
        unpad_model(z, two["grad_in"]),
        unpad_model(z, out["gains"][:2]),
        parts[0].T,
        parts[1],
        parts[2].T,
        parts[3].T,
        parts[4],
    )


def solution(mesh):
    return jax.shard_map(
        functools.partial(local, mesh.shape["wide"]),
        mesh=mesh,
        in_specs=(
            P(("mp", "wide"), None),
            P(("mp", "wide"), None),
            P(),
            P("mp", "wide"),
            P("wide", "mp"),
            P("mp", "wide"),
            P("mp", "wide"),
            P("wide", "mp"),
        ),
        out_specs=(
            P(("mp", "wide"), None),
            P(("mp", "wide"), None),
            P(),
            P("mp", "wide"),
            P("wide", "mp"),
            P("mp", "wide"),
            P("mp", "wide"),
            P("wide", "mp"),
        ),
        check_vma=False,
    )
```

```python
import functools
import math
import types

import jax
import jax.numpy as jnp
import numpy as np
from jax import lax
from jax.experimental import pallas as pl
from jax.experimental.pallas import tpu as pltpu
from jax.sharding import PartitionSpec as P

EPSILON = 1e-05
NEGATIVE = -1e30
HEAD = 64
QUERY_HEADS = 15
KEY_HEADS = 5
GROUP = 3
LANES = 128
BLOCK = 256
BF = jnp.bfloat16
F32 = jnp.float32
MESH = pl.DeviceIdType.MESH
VMEM_BYTES = 62 * 2**20


def dot(a, b, contract):
    return lax.dot_general(a, b, ((contract[:1], contract[1:]), ((), ())), preferred_element_type=F32)


def nn(a, b):
    return dot(a, b, (1, 0))


def nt(a, b):
    return dot(a, b, (1, 1))


def tn(a, b):
    return dot(a, b, (0, 0))


def at(start, size):
    return pl.ds(pl.multiple_of(start, size), size)


def loop(count, body, **kw):
    def step(i, _):
        body(i)
        return 0

    lax.fori_loop(0, count, step, 0, **kw)


class Sizes:
    def __init__(self, tokens, width, qkv, heads, hidden, wide):
        self.tokens, self.width = tokens, width
        self.padded = 4 * BLOCK
        self.quarter = width // 4
        self.qkv, self.heads, self.hidden, self.wide = qkv, heads, hidden, wide
        up = lambda v: -(-v // 16) * 16
        self.rows_of = (qkv // wide, heads // wide, hidden // wide, hidden // wide, hidden // wide)
        self.blocks = tuple(up(v) for v in self.rows_of)
        self.starts = tuple(sum(self.blocks[:k]) for k in range(5))
        self.rows = sum(self.blocks)
        self.qkv_padded = -(-qkv // LANES) * LANES
        self.n = wide // 2
        self.group = 640 // self.rows_of[2]


def normalize(z, state, gain_row, out):
    def body(i):
        rows = at(i * 64, 64)
        s = state[rows, :].astype(F32)
        r = lax.rsqrt(jnp.sum(s * s, axis=1, keepdims=True) * (1.0 / z.width) + EPSILON)
        out[rows, :] = (s * r * gain_row).astype(BF)

    loop(z.tokens // 64, body)


def normalize_back(z, state, gain_row, incoming, passed, out, gain_out):
    def body(i):
        rows = at(i * 64, 64)
        s = state[rows, :].astype(F32)
        g = incoming[rows, :]
        r = lax.rsqrt(jnp.sum(s * s, axis=1, keepdims=True) * (1.0 / z.width) + EPSILON)
        n = s * r
        gn = g * n
        c = g * gain_row
        m = jnp.sum(gn * gain_row, axis=1, keepdims=True) * (1.0 / z.width)
        out[rows, :] = passed[rows, :].astype(F32) + r * (c - n * m)
        gain_out[...] += jnp.sum(gn.reshape(8, 8, z.padded), axis=0)

    loop(z.tokens // 64, body)


def half_mask(rows):
    return lax.broadcasted_iota(jnp.int32, (rows, LANES), 1) < HEAD


def swap_pairs(v):
    lane = lax.rem(lax.broadcasted_iota(jnp.int32, v.shape, 1), HEAD)
    return jnp.where(lane < HEAD // 2, pltpu.roll(v, LANES - HEAD // 2, 1), pltpu.roll(v, HEAD // 2, 1))


def project_qkv(z, normed, w_qkv, table, qkv, query, keys, values):
    cos, sin = table
    w = z.qkv
    half = 5 * LANES
    for start in (0, half, 2 * half):
        size = min(half, w - start)
        qkv[:, start : start + size] = nt(normed[...], w_qkv[start : start + size, :])

    def body(i):
        rows = at(i * 64, 64)
        lo = half_mask(64)
        c, s = cos[rows, :], sin[rows, :]
        zero = jnp.zeros((64, LANES), F32)

        def place(target, g, v, low):
            other = pltpu.roll(v, HEAD, 1)
            a, b = (v, other) if low else (other, v)
            target[0, g, rows, :] = jnp.where(lo, a, zero).astype(BF)
            target[1, g, rows, :] = jnp.where(lo, zero, b).astype(BF)

        for m in range(10):
            v = qkv[rows, m * LANES : (m + 1) * LANES]
            v = v * c + swap_pairs(v) * s
            if m < 7:
                query[rows, m * LANES : (m + 1) * LANES] = (v * (HEAD**-0.5)).astype(BF)
            elif m == 7:
                query[rows, m * LANES : (m + 1) * LANES] = jnp.where(lo, v * (HEAD**-0.5), zero).astype(BF)
                place(keys, 0, v, False)
            else:
                place(keys, 2 * (m - 8) + 1, v, True)
                place(keys, 2 * (m - 8) + 2, v, False)
        for m in range(2):
            v = qkv[rows, (10 + m) * LANES : (11 + m) * LANES]
            place(values, 2 * m, v, True)
            place(values, 2 * m + 1, v, False)
        v = qkv[rows, 12 * LANES : 13 * LANES]
        place(values, 4, v, True)

    loop(z.tokens // 64, body)


def causal(rows):
    return lax.broadcasted_iota(jnp.int32, (rows, rows), 0) >= lax.broadcasted_iota(jnp.int32, (rows, rows), 1)


def attend(z, r, first, count):
    t = z.tokens // 2
    query, keys, values, weights = r.query, r.keys, r.values, r.weights

    def one(m, parity):
        cols = at(m * LANES, LANES)
        h = 2 * m + parity
        g = h // GROUP
        mask = half_mask(z.tokens)
        own = mask if parity == 0 else jnp.logical_not(mask)
        value = jnp.where(own, values[parity, g], jnp.ones((), BF))
        s = nt(query[:t, cols], keys[parity, g, :t, :])
        s = jnp.where(causal(t), s, NEGATIVE)
        p = jnp.exp(s - jnp.max(s, axis=1, keepdims=True)).astype(BF)
        weights[h, 0] = p
        top = nn(p, value[:t])
        a = nt(query[t:, cols], keys[parity, g, :t, :])
        b = nt(query[t:, cols], keys[parity, g, t:, :])
        b = jnp.where(causal(t), b, NEGATIVE)
        high = jnp.max(jnp.maximum(a, b), axis=1, keepdims=True)
        pa = jnp.exp(a - high).astype(BF)
        pb = jnp.exp(b - high).astype(BF)
        weights[h, 1] = pa
        weights[h, 2] = pb
        return top, nn(pa, value[:t]) + nn(pb, value[t:])

    def finish(m, low, high):
        cols = at(m * LANES, LANES)
        lo = half_mask(t)
        for k in range(2):
            rows = slice(k * t, (k + 1) * t)
            inv = 1.0 / pltpu.roll(jnp.where(lo, high[k], low[k]), HEAD, 1)
            r.inverse[rows, cols] = inv
            r.heads[rows, cols] = (jnp.where(lo, low[k], high[k]) * inv).astype(BF)

    def pair(i):
        finish(first + i, one(first + i, 0), one(first + i, 1))

    last = QUERY_HEADS // 2
    loop(min(first + count, last) - first, pair)
    if first + count > last:
        empty = jnp.where(half_mask(t), 1.0, 0.0)
        finish(last, one(last, 0), (empty, empty))


def forward_steps(z, r):
    chunk = r.chunk

    def start():
        normalize(z, r.state, r.gains[0:1, :], r.normed)

    def qkv():
        r.need_qkv()
        project_qkv(z, r.normed, r.w_qkv, (r.cos, r.sin), r.qkv, r.query, r.keys, r.values)

    def heads(first):
        return lambda: attend(z, r, first, 2)

    def out():
        r.need_out()
        for n in range(2):
            cols = slice(n * 512, (n + 1) * 512)
            r.middle[:, cols] = r.state[:, cols].astype(F32) + nn(r.heads[:, : z.heads], r.w_out[:, cols])
        normalize(z, r.middle, r.gains[1:2, :], r.normed2)

    def gate_up(i):
        cols = at(i * chunk, chunk)
        gate = nt(r.normed2[...], r.gate_block(i))
        up = nt(r.normed2[...], r.up_block(i))
        r.gate[:, cols] = gate.astype(BF)
        r.up[:, cols] = up.astype(BF)
        r.hidden[:, cols] = (gate * jax.nn.sigmoid(gate) * up).astype(BF)

    def ffn():
        r.need_gate()
        loop(z.hidden // chunk, gate_up)

    def some(first, count):
        return lambda: loop(count, lambda i: gate_up(first + i))

    def down():
        r.need_down()
        r.down()

    if r.halves:
        half = z.hidden // chunk // 2
        return [start, qkv, heads(0), heads(2), heads(4), heads(6), out, some(0, half), some(half, half), down]
    return [start, qkv, lambda: attend(z, r, 0, 8), out, ffn, down]


def forward(z, r):
    for step in forward_steps(z, r):
        step()


def attend_back(z, r):
    t = z.tokens // 2
    query, keys, values, weights, scaled, heads = r.query, r.keys, r.values, r.weights, r.scaled, r.heads
    query_grad, key_grad, value_grad = r.query_grad, r.key_grad, r.value_grad
    key_grad[...] = jnp.zeros_like(key_grad)
    value_grad[...] = jnp.zeros_like(value_grad)

    first, second = slice(0, t), slice(t, 2 * t)

    def one(m, parity):
        h = 2 * m + parity
        g = h // GROUP
        cols = at(m * LANES, LANES)
        key = keys.at[parity, g]
        value = values.at[parity, g]
        mask = half_mask(2 * t)
        own = mask if parity == 0 else jnp.logical_not(mask)
        both = scaled[:, cols].astype(F32) * heads[:, cols].astype(F32)
        delta = jnp.sum(jnp.where(own, both, 0.0), axis=1, keepdims=True)

        def grad(tile, rows, other):
            w = weights[h, tile]
            dp = nt(scaled[rows, cols], value[other, :])
            return (w.astype(F32) * (dp - delta[rows])).astype(BF), w

        s00, w00 = grad(0, first, first)
        s10, w10 = grad(1, second, first)
        s11, w11 = grad(2, second, second)
        q1, q2 = query[first, cols], query[second, cols]
        d1, d2 = scaled[first, cols], scaled[second, cols]
        key_grad[parity, g, first, :] += tn(s00, q1) + tn(s10, q2)
        key_grad[parity, g, second, :] += tn(s11, q2)
        value_grad[parity, g, first, :] += tn(w00, d1) + tn(w10, d2)
        value_grad[parity, g, second, :] += tn(w11, d2)
        return nn(s00, key[first, :]), nn(s10, key[first, :]) + nn(s11, key[second, :])

    def pair(m):
        cols = at(m * LANES, LANES)
        a, b = one(m, 0), one(m, 1)
        query_grad[first, cols] = a[0] + b[0]
        query_grad[second, cols] = a[1] + b[1]

    m = QUERY_HEADS // 2
    loop(m, pair)
    cols = slice(m * LANES, (m + 1) * LANES)
    query_grad[first, cols], query_grad[second, cols] = one(m, 0)


def unrotate_qkv(z, r):
    def unrotate(i):
        rows = at(i * 64, 64)
        lo = half_mask(64)
        c, s = r.cos[rows, :], r.sin[rows, :]

        def turn(v):
            return v * c - swap_pairs(v) * s

        def joined(ref, g):
            a, b = ref[0, g, rows, :], ref[1, g, rows, :]
            return jnp.where(lo, a + pltpu.roll(b, HEAD, 1), 0.0), jnp.where(lo, 0.0, b + pltpu.roll(a, HEAD, 1))

        def put(m, v):
            r.qkv_back[rows, m * LANES : (m + 1) * LANES] = v.astype(BF)

        k = [joined(r.key_grad, g) for g in range(KEY_HEADS)]
        v = [joined(r.value_grad, g) for g in range(KEY_HEADS)]
        scale = HEAD**-0.5
        for m in range(7):
            put(m, turn(r.query_grad[rows, m * LANES : (m + 1) * LANES] * scale))
        last = jnp.where(lo, r.query_grad[rows, 7 * LANES : 8 * LANES] * scale, 0.0)
        put(7, turn(last + k[0][1]))
        put(8, turn(k[1][0] + k[2][1]))
        put(9, turn(k[3][0] + k[4][1]))
        put(10, v[0][0] + v[1][1])
        put(11, v[2][0] + v[3][1])
        put(12, v[4][0])

    loop(z.tokens // 64, unrotate)


def backward_steps(z, r):
    ffn_grad = r.ffn_grad

    def rounded():
        def body(i):
            rows = at(i * 64, 64)
            ffn_grad[rows, :] = r.grad[rows, :].astype(BF)

        if r.grad is not ffn_grad:
            loop(z.tokens // 64, body)

    def ffn():
        r.need_down()
        r.need_kept()

        def body(n):
            cols = at(n * 512, 512)
            back = nt(ffn_grad[...], r.w_down[cols, :])
            gate = r.gate[:, cols].astype(F32)
            up = r.up[:, cols].astype(F32)
            s = jax.nn.sigmoid(gate)
            r.gate[:, cols] = (back * up * s * (1.0 + gate * (1.0 - s))).astype(BF)
            r.up[:, cols] = (back * gate * s).astype(BF)

        loop(z.hidden // 512, body)
        r.ffn_done()

    def into():
        r.need_gate()

        def body(n):
            cols = at(n * 512, 512)
            r.normed_grad[:, cols] = nn(r.gate[...], r.w_gate[:, cols]) + nn(r.up[...], r.w_up[:, cols])

        loop(z.padded // 512, body)

    def norm2():
        r.need_middle()
        normalize_back(z, r.middle, r.gains[1:2, :], r.normed_grad, r.grad, r.middle_grad, r.gain_out.at[1])

        def body(i):
            rows = at(i * 64, 64)
            r.attn_back[rows, :] = r.middle_grad[rows, :].astype(BF)

        loop(z.tokens // 64, body)

    def out():
        r.need_attention()
        r.need_out()
        w = z.heads
        for start, size in ((0, 512), (512, w - 512)):
            cols = slice(start, start + size)
            back = nt(r.attn_back[...], r.w_out[cols, :])
            r.scaled[:, cols] = (back * r.inverse[:, cols]).astype(BF)
        r.scaled[:, w:] = jnp.zeros((z.tokens, z.padded - w), BF)

    def attention():
        attend_back(z, r)
        r.attention_done()

    def unrotate():
        unrotate_qkv(z, r)

    def qkv():
        r.need_qkv()
        for n in range(2):
            cols = slice(n * 512, (n + 1) * 512)
            r.normed_grad[:, cols] = nn(r.qkv_back[:, : z.qkv], r.w_qkv[:, cols])

    def norm1():
        normalize_back(z, r.state, r.gains[0:1, :], r.normed_grad, r.middle_grad, r.grad_in, r.gain_out.at[0])

    return [rounded, ffn, into, norm2, out, attention, unrotate, qkv, norm1]


def backward(z, r):
    for step in backward_steps(z, r):
        step()


def kept_shapes(z):
    t, d, f = z.tokens, z.padded, z.hidden
    return dict(
        query=((t, d), BF),
        keys=((2, KEY_HEADS, t, LANES), BF),
        values=((2, KEY_HEADS, t, LANES), BF),
        weights=((QUERY_HEADS, 3, t // 2, t // 2), BF),
        inverse=((t, d), F32),
        heads=((t, d), BF),
        middle=((t, d), F32),
        gate=((t, f), BF),
        up=((t, f), BF),
    )


def layer_shapes(z):
    t, d, f = z.tokens, z.padded, z.hidden
    return dict(kept_shapes(z), normed=((t, d), BF), normed2=((t, d), BF), hidden=((t, f), BF))


def weight_shapes(z):
    d, f = z.padded, z.hidden
    return dict(w_qkv=((z.qkv, d), BF), w_out=((z.heads, d), BF), w_gate=((f, d), BF), w_up=((f, d), BF), w_down=((f, d), BF))


def tables(z):
    t, d = z.tokens, z.padded
    return dict(gains=((2, z.width), F32), cos=((t, LANES), F32), sin=((t, LANES), F32))


def blocks_shape(z):
    return ((2, 2, z.n, 2, z.rows, BLOCK), BF)


def rows_first(z):
    t, d, f = z.tokens, z.padded, z.hidden
    left = dict(qkv_back=((t, z.qkv_padded), BF), heads=((t, d), BF), gate=((t, f), BF), up=((t, f), BF), hidden=((t, f), BF))
    right = dict(normed=((t, d), BF), attn_back=((t, d), BF), normed2=((t, d), BF), ffn_grad=((t, d), BF))
    return left, right


def make_call(name, body, ins, outs, scratch, in_vmem, sems, **params):
    n_in, n_out, n_s = list(ins), list(outs), list(scratch)

    def kernel(*refs):
        a, b, c = len(n_in), len(n_in) + len(n_out), len(n_in) + len(n_out) + len(n_s)
        group = lambda names, part: types.SimpleNamespace(**dict(zip(names, part)))
        body(group(n_in, refs[:a]), group(n_out, refs[a:b]), group(n_s, refs[b:c]), refs[c:])

    spec = lambda n: pl.BlockSpec(memory_space=pltpu.VMEM if n in in_vmem else pl.ANY)
    call = pl.pallas_call(
        kernel,
        out_shape=[jax.ShapeDtypeStruct(*outs[n]) for n in n_out],
        in_specs=[spec(n) for n in n_in],
        out_specs=[spec(n) for n in n_out],
        scratch_shapes=[pltpu.VMEM(*scratch[n]) for n in n_s] + [pltpu.SemaphoreType.DMA(s) for s in sems],
        compiler_params=pltpu.CompilerParams(vmem_limit_bytes=VMEM_BYTES, **params),
        name=name,
    )
    return lambda **vals: dict(zip(n_out, call(*[vals[n] for n in n_in])))


class Copies:
    def __init__(self, sems):
        self.sems, self.used, self.open = sems, 0, {}

    def start(self, src, dst):
        key = self.used
        self.used += 1
        self.open[key] = pltpu.make_async_copy(src, dst, self.sems.at[key])
        self.open[key].start()
        return key

    def wait(self, keys):
        for key in keys:
            if key in self.open:
                self.open.pop(key).wait()

    def later(self, keys):
        return lambda: self.wait(keys)

    def finish(self):
        self.wait(list(self.open))


SMALL = ("gains", "cos", "sin", "tokens")


def pad_into(z, target, source, turned=True):
    target[...] = jnp.zeros(target.shape, target.dtype)
    for q in range(4):
        part = slice(q * z.quarter, (q + 1) * z.quarter)
        value = source[part, :].astype(F32).T.astype(target.dtype) if turned else source[:, part]
        target[:, q * BLOCK : q * BLOCK + z.quarter] = value


def unpad_into(z, target, value, first=0):
    for q in range(value.shape[1] // BLOCK):
        start = (first + q) * z.quarter
        target[start : start + z.quarter, :] = value[:, q * BLOCK : (q + 1) * BLOCK].T[: z.quarter, :]


def middle_kernel(z):
    t, d = z.tokens, z.padded
    kept = kept_shapes(z)
    ins = dict(tables(z), tokens=((t, d), BF), state=((t, d), F32), cotangent=((z.width, t), BF))
    ins.update(gathered=blocks_shape(z), dense_qkv=((z.qkv, d), BF), dense_out=((z.heads, d), BF))
    ins.update({"first_" + n: v for n, v in kept.items()})
    left, right = rows_first(z)
    both = dict(left, **right)
    outs = dict(result=((z.width, t), F32), grad_in=((z.width, t), F32), gain=((8, d), F32))
    outs.update({n + "2": v for n, v in both.items()})
    outs.update({n + "1": both[n] for n in ("qkv_back", "attn_back", "gate", "up", "ffn_grad")})
    scratch = dict(layer_shapes(z), **weight_shapes(z), state=((t, d), F32), grad=((t, d), BF))
    scratch.update(qkv=((t, z.qkv_padded), F32), plain=((z.width, t), F32), gain_out=((2, 8, d), F32), gains=((2, d), F32))
    scratch.update(key_grad=((2, KEY_HEADS, t, LANES), F32), value_grad=((2, KEY_HEADS, t, LANES), F32))

    def body(i, o, s, sems):
        cps = Copies(sems[0])
        state = cps.start(i.state, s.state)
        w = start_weights(z, cps, i, s)
        pad_into(z, s.gains, i.gains, False)
        pad_into(z, s.grad, i.cotangent)
        grad = cps.start(s.grad, o.ffn_grad2)
        none = lambda: None
        r = types.SimpleNamespace(**vars(s))
        vars(r).update(w, cos=i.cos, sin=i.sin, chunk=512, halves=False)
        r.gate_block = lambda n: s.w_gate[at(n * 512, 512), :]
        r.up_block = lambda n: s.w_up[at(n * 512, 512), :]

        def down():
            for n in range(2):
                cols = slice(n * 512, (n + 1) * 512)
                unpad_into(z, s.plain, s.middle[:, cols] + nn(s.hidden[...], s.w_down[:, cols]), 2 * n)

        r.down = down
        cps.wait([state])
        forward(z, r)
        outs_now = [cps.start(s.plain, o.result), cps.start(s.normed2, o.normed22), cps.start(s.hidden, o.hidden2)]
        heads_out = cps.start(s.heads, o.heads2)
        outs_now.append(cps.start(s.normed, o.normed2))
        s.gain_out[...] = jnp.zeros_like(s.gain_out)
        cps.wait([grad] + outs_now)

        back = types.SimpleNamespace(**vars(r))
        back.qkv_back = s.hidden.at[:, : z.qkv_padded]
        vars(back).update(scaled=s.normed2, attn_back=s.normed, normed_grad=s.qkv.at[:, :d], middle_grad=s.middle, query_grad=s.qkv.at[:, :d], grad_in=s.state)
        vars(back).update(ffn_grad=s.grad, need_kept=none, need_middle=none, need_attention=none)
        ffn_out = []
        loads = {}

        def ffn_done():
            ffn_out.extend([cps.start(s.gate, o.gate2), cps.start(s.up, o.up2)])

        def load(n):
            loads[n] = cps.start(getattr(i, "first_" + n), getattr(s, n))

        def attention_done():
            cps.wait(ffn_out + [heads_out])
            for n in ("gate", "up", "inverse", "heads", "query", "keys", "values", "weights"):
                load(n)

        back.ffn_done, back.attention_done = ffn_done, attention_done
        backward(z, back)
        load("middle")
        factors = [cps.start(back.attn_back, o.attn_back2), cps.start(back.qkv_back, o.qkv_back2)]

        first = types.SimpleNamespace(**vars(back))
        vars(first).update(grad=s.state, state=s.grad)
        first.need_kept = cps.later([loads["gate"], loads["up"]])
        first.need_middle = cps.later([loads["middle"]] + factors)
        first.need_attention = cps.later([loads[n] for n in ("inverse", "heads", "query", "keys", "values", "weights")])
        sent = []

        def ffn_done1():
            cps.start(s.gate, o.gate1)
            cps.start(s.up, o.up1)
            sent.append(cps.start(s.grad, o.ffn_grad1))

        def attention_done1():
            cps.wait(sent)
            sent.append(cps.start(i.tokens, s.grad))

        first.attention_done = attention_done1
        first.need_qkv = lambda: cps.wait(sent)

        first.ffn_done = ffn_done1
        backward(z, first)
        unpad_into(z, s.plain, s.state[...])
        cps.start(s.plain, o.grad_in)
        cps.start(back.attn_back, o.attn_back1)
        cps.start(first.qkv_back, o.qkv_back1)
        o.gain[...] = jnp.zeros_like(o.gain)
        o.gain[0:1, :] = jnp.sum(s.gain_out[0], axis=0, keepdims=True)
        o.gain[1:2, :] = jnp.sum(s.gain_out[1], axis=0, keepdims=True)
        cps.finish()

    return make_call("second_layer", body, ins, outs, scratch, ("gains", "cos", "sin", "cotangent", "gain"), [(80,)])


def start_weights(z, cps, i, s):
    def blocks(w, k):
        w = w.reshape(z.n, 2, z.blocks[k], z.padded)
        rows = pl.ds(z.starts[k], z.blocks[k])
        return [cps.start(i.gathered.at[q // 2, q % 2, :, :, rows], w.at[:, :, :, q * BLOCK : (q + 1) * BLOCK]) for q in range(4)]

    qkv = [cps.start(i.dense_qkv, s.w_qkv)]
    out = [cps.start(i.dense_out, s.w_out)]
    gate = blocks(s.w_gate, 2) + blocks(s.w_up, 3)
    down = blocks(s.w_down, 4)
    return dict(need_qkv=cps.later(qkv), need_out=cps.later(out), need_gate=cps.later(gate), need_down=cps.later(down))


class Place:
    def __init__(self, n):
        mp, w = lax.axis_index("mp"), lax.axis_index("wide")
        self.n = n
        self.x, self.y, self.c, self.z = lax.rem(mp, 2), mp // 2, lax.rem(w, 2), w // 2

    def dev(self, x=None, y=None, z=None, c=None):
        x = self.x if x is None else x
        y = self.y if y is None else y
        z = self.z if z is None else z
        c = self.c if c is None else c
        return {"mp": y * 2 + x, "wide": z * 2 + c}

    def partner(self, axis):
        return self.dev(**{axis: 1 - getattr(self, axis)})

    def greet(self):
        bar = pltpu.get_barrier_semaphore()

        def signal(device):
            pl.semaphore_signal(bar, inc=1, device_id=device, device_id_type=MESH)

        for axis in "xyc":
            signal(self.partner(axis))

        @pl.when(self.z > 0)
        def _():
            signal(self.dev(z=self.z - 1))

        @pl.when(self.z < self.n - 1)
        def _():
            signal(self.dev(z=self.z + 1))

    def met(self):
        bar = pltpu.get_barrier_semaphore()
        pl.semaphore_wait(bar, 3 + jnp.where(self.z > 0, 1, 0) + jnp.where(self.z < self.n - 1, 1, 0))


def row_chunks(sizes, per):
    out, r = [], 0
    for s, p in zip(sizes, per):
        u = s // 16
        for k in range(p):
            size = (u // p + (1 if k < u % p else 0)) * 16
            out.append((r, size))
            r += size
    return out


def run_stages(entries):
    for entry in sorted(entries, key=lambda e: e[:2]):
        entry[2]()


def shares(units, weights):
    out, done, used = [], 0, 0
    for w in weights:
        done += w
        end = round(units * done / sum(weights))
        out.append(end - used)
        used = end
    return out


def row_chunks(start, rows, parts, orders):
    out, r = [], start
    for k, units in enumerate(shares(rows // 16, [1] * parts)):
        for order, u in zip(orders[k % len(orders)], shares(units, [1] * len(orders[0]))):
            if u:
                out.append((r, 16 * u, order, k))
                r += 16 * u
    return out


GATHER_ORDERS = (("xzy", "yzx"), ("zxy", "zyx"), ("yzx", "xzy"))
GATHER_PARTS = 10
GATHER_TIMES = ((-1.44, 0.95, 2.47, 0.87, 0.01, 0.95, 1.6), (-4.28, -0.02, 0.47, 0.69, 1.14, 2.95, 4.2))
STEP_GAP = 0.7


def gather_plan(p, g, k, piece, ss, rs):
    r0, rc, order, _ = piece
    n, rows = p.n, pl.ds(r0, rc)
    a1, a2 = [a for a in order if a != "z"]
    z_first = order[0] == "z"

    def one(zo, other=False):
        x = 1 - p.x if other and a1 == "x" else p.x
        y = 1 - p.y if other and a1 == "y" else p.y
        return g.at[y, x, zo, p.c, rows]

    def pair(zo, other=False, c=None):
        c = p.c if c is None else c
        if a1 == "x":
            return g.at[1 - p.y if other else p.y, :, zo, c, rows]
        return g.at[:, 1 - p.x if other else p.x, zo, c, rows]

    def copy(ref, dev, s, r):
        return pltpu.make_async_remote_copy(src_ref=ref, dst_ref=ref, send_sem=ss.at[k, s], recv_sem=rs.at[k, r], device_id=dev, device_id_type=MESH)

    along = one if z_first else pair
    up = lambda zo: copy(along(zo), p.dev(z=p.z + 1), zo, zo)
    down = lambda zo: copy(along(zo), p.dev(z=p.z - 1), n + zo, zo)
    line_in = lambda zo: copy(along(zo), p.partner("c"), zo, zo)
    first = lambda zo, other=False: copy(one(zo, other), p.partner(a1), 2 * n + zo, n + zo)
    second = lambda zo, other=False: copy(pair(zo, other), p.partner(a2), 3 * n + zo, 2 * n + zo)

    def sibling(other, c=None):
        c = p.c if c is None else c
        if a1 == "x":
            part = g.at[1 - p.y if other else p.y, :, :, c, rows]
        else:
            part = g.at[:, 1 - p.x if other else p.x, :, c, rows]
        o = 1 if other else 0
        return copy(part, p.partner("c"), 4 * n + o, 3 * n + o)

    def line(zo):
        @pl.when((zo <= p.z) & (p.z < n - 1))
        def _():
            up(zo).start()

        @pl.when((zo >= p.z) & (p.z > 0))
        def _():
            down(zo).start()

    def at_distance(d, body):
        @pl.when(p.z - d >= 0)
        def _():
            body(p.z - d)

        @pl.when(p.z + d < n)
        def _():
            body(p.z + d)

    stages = []
    times = GATHER_TIMES[1 if z_first else 0]
    hop_time, step = times[1:3] if z_first else times[2:4]
    last_hop = hop_time + (n - 2) * step
    if z_first:

        def start():
            line(p.z)
            first(p.z).start()

        stages.append((times[0], start))
        for d in range(1, n):

            def hop(d=d):
                def body(zo):
                    line_in(zo).wait_recv()
                    line(zo)
                    first(zo).start()

                at_distance(d, body)

            stages.append((hop_time + (d - 1) * step, hop))

        def cross():
            for zo in range(n):
                first(zo, True).wait_recv()
                second(zo).start()

        stages.append((last_hop + times[3], cross))
    else:

        def start():
            first(p.z).start()

        def meet():
            first(p.z, True).wait_recv()
            line(p.z)
            second(p.z).start()

        stages += [(times[0], start), (times[1], meet)]
        for d in range(1, n):

            def hop(d=d):
                def body(zo):
                    line_in(zo).wait_recv()
                    line(zo)
                    second(zo).start()

                at_distance(d, body)

            stages.append((hop_time + (d - 1) * step, hop))

    def halfway():
        sibling(False).start()

    def arrived():
        for zo in range(n):
            second(zo, True).wait_recv()
        sibling(True).start()

    def done():
        sibling(False, 1 - p.c).wait_recv()
        sibling(True, 1 - p.c).wait_recv()

    def drain():
        for zo in range(n):

            @pl.when((zo <= p.z) & (p.z < n - 1))
            def _():
                up(zo).wait_send()

            @pl.when((zo >= p.z) & (p.z > 0))
            def _():
                down(zo).wait_send()

            second(zo).wait_send()
            if z_first:
                first(zo).wait_send()
        if not z_first:
            first(p.z).wait_send()
        sibling(False).wait_send()
        sibling(True).wait_send()

    return stages + [(last_hop + at_time, f) for at_time, f in zip(times[-3:], (halfway, arrived, done))], drain


def first_kernel(z):
    t, d, n = z.tokens, z.padded, z.n
    pieces = row_chunks(0, z.rows, GATHER_PARTS, GATHER_ORDERS)
    layer = layer_shapes(z)
    shards = weight_shards(z, BF)
    ins = dict(tables(z), tokens=((z.width, t), BF), **shards)
    outs = dict(layer, start=((t, d), BF), result=((t, d), F32), gathered=blocks_shape(z), dense_qkv=((z.qkv, d), BF), dense_out=((z.heads, d), BF))
    scratch = dict(layer, result=((t, d), F32), qkv=((t, z.qkv_padded), F32), blocks=blocks_shape(z))
    scratch.update(w_qkv=((z.qkv, d), BF), w_out=((z.heads, d), BF), start=((t, d), BF), gains=((2, d), F32))

    def body(i, o, s, sems):
        local, ss, rs = sems
        cps = Copies(local)
        p = Place(n)
        p.greet()
        for k, name in enumerate(shards):
            w = getattr(i, name)[...]
            rows = z.starts[k]
            s.blocks[p.y, p.x, p.z, p.c, rows : rows + z.blocks[k], :] = jnp.zeros((z.blocks[k], BLOCK), BF)
            s.blocks[p.y, p.x, p.z, p.c, rows : rows + z.rows_of[k], : z.quarter] = w
        p.met()

        def dense(k, target):
            per = z.rows_of[k]
            for j in range(z.wide):
                for q in range(4):
                    rows = s.blocks[q // 2, q % 2, j // 2, j % 2, z.starts[k] : z.starts[k] + per, :]
                    target[j * per : (j + 1) * per, q * BLOCK : (q + 1) * BLOCK] = rows

        def block(k):
            start, per, some = z.starts[k], z.rows_of[k], z.group // 2

            def read(j):
                rows = []
                for e in range(z.group):
                    quarters = [s.blocks[q // 2, q % 2, j * some + e // 2, e % 2, start : start + per, :] for q in range(4)]
                    rows.append(jnp.concatenate(quarters, axis=1))
                return jnp.concatenate(rows, axis=0)

            return read

        none = lambda: None
        r = types.SimpleNamespace(**vars(s))
        vars(r).update(cos=i.cos, sin=i.sin, state=s.start, chunk=640, halves=True)
        vars(r).update(gate_block=block(2), up_block=block(3), need_gate=none, need_down=none)

        def need_qkv():
            dense(0, s.w_qkv)
            cps.start(s.w_qkv, o.dense_qkv)

        def need_out():
            dense(1, s.w_out)
            cps.start(s.w_out, o.dense_out)

        def down():
            read = block(4)
            s.result[...] = s.middle[...]

            def add(j):
                s.result[...] += nn(s.hidden[:, at(j * 640, 640)], read(j))

            loop(z.hidden // 640, add)

        vars(r).update(need_qkv=need_qkv, need_out=need_out, down=down)
        steps = forward_steps(z, r)

        def begin():
            pad_into(z, s.gains, i.gains, False)
            pad_into(z, s.start, i.tokens)
            cps.start(s.start, o.start)
            forward_start()

        forward_start, steps[0] = steps[0], begin
        plans = [gather_plan(p, s.blocks, k, piece, ss, rs) for k, piece in enumerate(pieces)]
        entries = [(pieces[k][3] + at_time, k, f) for k, (stages, _) in enumerate(plans) for at_time, f in stages]
        done = [pieces[k][3] + stages[-1][0] for k, (stages, _) in enumerate(plans)]
        ready = [max(at_time for at_time, piece in zip(done, pieces) if piece[0] < e) for e in (z.starts + (z.rows,))[1:]]
        times = [0.5]
        for k in (0, 0, 0, 0, 0, 1, 3, 3, 4):
            times.append(max(ready[k] + 0.5, times[-1] + STEP_GAP))
        entries += [(at_time, -1, f) for at_time, f in zip(times, steps)]

        def out_of(part):
            rows = [p for p in pieces if p[3] == part]
            span = pl.ds(rows[0][0], sum(p[1] for p in rows))
            return lambda: cps.start(s.blocks.at[:, :, :, :, span], o.gathered.at[:, :, :, :, span])

        for part in range(GATHER_PARTS):
            entries.append((max(at_time for at_time, piece in zip(done, pieces) if piece[3] == part), 100 + part, out_of(part)))

        def keep(*names):
            return lambda: [cps.start(getattr(s, m), getattr(o, m)) for m in names]

        entries += [(times[5], 0, keep("normed", "query", "keys", "values", "weights", "inverse", "heads"))]
        entries += [(times[6], 0, keep("middle", "normed2")), (times[8], 0, keep("gate", "up", "hidden"))]
        run_stages(entries)
        cps.start(s.result, o.result)
        for _, drain in plans:
            drain()
        cps.finish()

    sems = [(40,), (len(pieces), 4 * n + 2), (len(pieces), 3 * n + 2)]
    return make_call("first_layer", body, ins, outs, scratch, SMALL + tuple(shards), sems, collective_id=1, has_side_effects=True)


REDUCE_ORDERS = (("yzx", "xzy", "yxz", "xyz"),)
REDUCE_WEIGHTS = (4, 2, 3, 0, 1)
REDUCE_PARTS = (1, 1, 2, 2, 2)
REDUCE_TIMES = ((0.1, 2.05, 2.1, 1.2, 0.8, 1.45, 2.65), (0.7, 2.65, 3.4, 3.55, 1.5, 0.8, 2.3))
WORK_LEAD, WORK_STEP = 1.0, 0.07


def weight_shards(z, kind):
    names = ("w_qkv_shard", "w_out_shard", "w_gate_shard", "w_up_shard", "w_down_shard")
    return {name: ((rows, z.quarter), kind) for name, rows in zip(names, z.rows_of)}


def add_into(target, extra):
    target[...] = target[...] + extra[...].astype(target.dtype)


def reduce_plan(p, t, bufs, out, k, piece, ss, rs):
    r0, rc, order = piece
    n, rows = p.n, pl.ds(r0, rc)
    from_sibling, from_first, from_line, from_last = bufs
    a1 = [a for a in order if a != "z"][0]
    z_last = order[2] == "z"

    def pair(zo, other=False):
        if a1 == "y":
            return t.at[1 - p.y if other else p.y, :, zo, rows]
        return t.at[:, 1 - p.x if other else p.x, zo, rows]

    def one(zo, other=False):
        x = 1 - p.x if other and a1 == "y" else p.x
        y = 1 - p.y if other and a1 == "x" else p.y
        return t.at[y, x, zo, rows]

    def sib_part(zo, other):
        if a1 == "y":
            return from_sibling.at[1 - p.y if other else p.y, :, zo, rows]
        return from_sibling.at[:, 1 - p.x if other else p.x, zo, rows]

    def copy(src, dst, dev, s, r):
        return pltpu.make_async_remote_copy(src_ref=src, dst_ref=dst, send_sem=ss.at[k, s], recv_sem=rs.at[k, r], device_id=dev, device_id_type=MESH)

    a2 = "x" if a1 == "y" else "y"
    line_ref = one if z_last else pair
    line_slot = (lambda v: from_line.at[0, v, rows]) if z_last else (lambda v: from_line.at[:, v, rows])
    across = lambda zo: copy(pair(zo, True), from_first.at[:, zo, rows], p.partner(a1), 1 + zo, 1 + zo)
    last = lambda zo: copy(one(zo, True), from_last.at[zo, rows], p.partner(a2), 1 + n + zo, 1 + n + zo)

    def send_up(zo):
        return copy(line_ref(zo), line_slot(zo), p.dev(z=p.z + 1), 1 + 2 * n + zo, 1 + 2 * n + zo)

    def send_down(zo):
        slot = jnp.where(zo == p.z - 1, n, zo)
        return copy(line_ref(zo), line_slot(slot), p.dev(z=p.z - 1), 1 + 2 * n + zo, 1 + 2 * n + slot)

    def line_in(slot):
        copy(line_slot(slot), line_slot(slot), p.partner("c"), 0, 1 + 2 * n + slot).wait_recv()

    def meet():
        def send(zo):
            add_into(pair(zo, True), sib_part(zo, True))
            across(zo).start()

        def keep(zo):
            add_into(pair(zo), sib_part(zo, False))

        loop(n, send)
        loop(n, keep)

    def crossed():
        def body(zo):
            across(zo).wait_recv()
            add_into(pair(zo), from_first.at[:, zo, rows])

        loop(n, body)
        if z_last:
            for zo in range(n):
                last(zo).start()

    def other_half():
        def body(zo):
            last(zo).wait_recv()
            add_into(one(zo), from_last.at[zo, rows])

        loop(n, body)

    def hop(s):
        @pl.when(p.z == s)
        def _():
            def body(i):
                zo = n - 1 - i

                @pl.when(p.z > 0)
                def _():
                    line_in(zo)
                    add_into(line_ref(zo), line_slot(zo))

                send_up(zo).start()

            lax.fori_loop(0, n - 1 - s, lambda i, c: (body(i), c)[1], 0)

        @pl.when(p.z == n - 1 - s)
        def _():
            def body(zo):
                @pl.when(p.z < n - 1)
                def _():
                    line_in(zo)
                    add_into(line_ref(zo), line_slot(zo))

                send_down(zo).start()

            lax.fori_loop(0, n - 1 - s, lambda i, c: (body(i), c)[1], 0)

    def line_end():
        @pl.when(p.z > 0)
        def _():
            line_in(p.z)
            add_into(line_ref(p.z), line_slot(p.z))

        @pl.when(p.z < n - 1)
        def _():
            line_in(n)
            add_into(line_ref(p.z), line_slot(n))

    def final_send():
        last(p.z).start()

    def finish():
        total = one(p.z)[...].astype(F32)
        if not z_last:
            last(p.z).wait_recv()
            total = total + from_last[p.z, rows].astype(F32)
        out[rows, :] = total

    def drain():
        for zo in range(n):
            across(zo).wait_send()
            if z_last:
                last(zo).wait_send()

            @pl.when(zo > p.z)
            def _():
                send_up(zo).wait_send()

            @pl.when(zo < p.z)
            def _():
                send_down(zo).wait_send()

        if not z_last:
            last(p.z).wait_send()

    if z_last:
        first, second, third, hop_time, step, end, finish_time = REDUCE_TIMES[1]
        stages = [(first, meet), (second, crossed), (third, other_half)]
    else:
        first, second, hop_time, step, end, send, finish_time = REDUCE_TIMES[0]
        stages = [(first, meet), (second, crossed)]
    for s in range(n - 1):
        stages.append((hop_time, functools.partial(hop, s)))
        hop_time += step
    stages.append((hop_time - step + end, line_end))
    if not z_last:
        stages.append((hop_time - step + send, final_send))
    stages.append((hop_time - step + finish_time, finish))
    return stages, drain


def last_kernel(z):
    t, d, n = z.tokens, z.padded, z.n
    left, right = rows_first(z)
    both = dict(left, **right)
    ins = {m + k: v for m, v in both.items() for k in "12"}
    ins.update(gain=((8, d), F32))
    outs = dict(sums=((z.rows, BLOCK), F32), gain_sums=((8, d), F32))
    two = lambda v: ((2 * t, v[0][1]), BF)
    scratch = {m: two(v) for m, v in both.items() if m not in ("gate", "up")}
    stage = max(z.rows_of)
    scratch.update(
        t=((2, 2, n, z.rows, BLOCK), BF),
        staged=((STAGED, 2, 2, stage, BLOCK), BF),
        from_sibling=((2, 2, n, z.rows, BLOCK), BF),
        from_first=((2, n, z.rows, BLOCK), BF),
        from_line=((2, n + 1, z.rows, BLOCK), BF),
        from_last=((n, z.rows, BLOCK), BF),
        gain_sent=((3, 8, d), F32),
        gain_in=((3, 8, d), F32),
        gain_all=((n, 8, d), F32),
    )
    order, parts = REDUCE_WEIGHTS, REDUCE_PARTS
    pieces, starts = [], {}
    slot = 1
    for k in order:
        starts[k] = slot
        for r0, rc, way, part in row_chunks(z.starts[k], z.blocks[k], parts[k], REDUCE_ORDERS):
            pieces.append((r0, rc, way, slot + part, k))
        slot += parts[k]

    def body(i, o, s, sems):
        local, ss, rs, sib_s, sib_r, gain_s, gain_r = sems
        cps = Copies(local)
        need = {}

        def load(m, into):
            target = getattr(s, into)
            need[m] = cps.later([cps.start(getattr(i, m + k), target.at[pl.ds((2 - int(k)) * t, t)]) for k in "12"])

        for m in ("heads", "attn_back", "hidden", "ffn_grad", "normed2", "normed", "qkv_back"):
            load(m, m)
        p = Place(n)
        p.greet()
        p.met()
        count = [0]

        def sibling(k, zo, slot):
            rows = pl.ds(z.starts[k], z.blocks[k])
            return pltpu.make_async_remote_copy(
                src_ref=s.staged.at[slot, :, :, pl.ds(0, z.blocks[k])],
                dst_ref=s.from_sibling.at[:, :, zo, rows],
                send_sem=sib_s.at[slot],
                recv_sem=sib_r.at[k, zo],
                device_id=p.partner("c"),
                device_id_type=MESH,
            )

        sent = {}

        def put(k, zo, slot, a, b):
            per = z.rows_of[k]
            own, other = jnp.where(p.c == 0, a, b).astype(BF), jnp.where(p.c == 0, b, a).astype(BF)
            for q in range(4):
                lanes = slice(q * BLOCK, (q + 1) * BLOCK)
                s.t[q // 2, q % 2, zo, z.starts[k] : z.starts[k] + per, :] = own[:, lanes]
                s.staged[slot, q // 2, q % 2, :per, :] = other[:, lanes]

        names = (("normed", "qkv_back"), ("heads", "attn_back"), ("gate", "normed2"), ("up", "normed2"), ("hidden", "ffn_grad"))
        some = [1, 1] + [z.group // 2] * 3

        def work(k, first):
            per = z.rows_of[k]

            def run():
                if first == 0:
                    if k in (2, 3):
                        load(names[k][0], "hidden")
                    for m in names[k]:
                        need[m]()
                m_left = (s.qkv_back, s.heads, s.hidden, s.hidden, s.hidden)[k]
                m_right = (s.normed, s.attn_back, s.normed2, s.normed2, s.ffn_grad)[k]
                width = 2 * per * some[k]
                value = tn(m_left[:, first * 2 * per : first * 2 * per + width], m_right[...])
                for e in range(some[k]):
                    zo = first + e
                    slot = count[0] % STAGED
                    if slot in sent:
                        sent.pop(slot).wait_send()
                    count[0] += 1
                    put(k, zo, slot, value[2 * e * per : (2 * e + 1) * per], value[(2 * e + 1) * per : (2 * e + 2) * per])
                    sent[slot] = sibling(k, zo, slot)
                    sent[slot].start()

            return run

        entries = [(starts[k] - WORK_LEAD + first * 4 / n * WORK_STEP * parts[k], -1, work(k, first)) for k in order for first in range(0, n, some[k])]
        met = set()

        def after_sibling(k, f):
            def run():
                if k not in met:
                    met.add(k)
                    for zo in range(n):
                        sibling(k, zo, 0).wait_recv()
                f()

            return run

        bufs = (s.from_sibling, s.from_first, s.from_line, s.from_last)
        plans = [reduce_plan(p, s.t, bufs, o.sums, k, piece[:3], ss, rs) for k, piece in enumerate(pieces)]
        for k, (stages, _) in enumerate(plans):
            stages[0] = (stages[0][0], after_sibling(pieces[k][4], stages[0][1]))
        entries += [(pieces[k][3] + at_time, k, f) for k, (stages, _) in enumerate(plans) for at_time, f in stages]
        stages, gains_drain = gain_plan(z, p, i.gain, s, o.gain_sums, gain_s, gain_r)
        entries += [(1 + k, 100, f) for k, f in enumerate(stages)]
        run_stages(entries)
        for _, drain in plans:
            drain()
        for c in sent.values():
            c.wait_send()
        gains_drain()
        cps.finish()

    sems = [(40,), (len(pieces), 1 + 3 * n), (len(pieces), 2 + 3 * n), (STAGED,), (5, n), (3 + 2 * n,), (3 + n,)]
    return make_call("gradients", body, ins, outs, scratch, ("gain", "sums", "gain_sums"), sems, collective_id=2, has_side_effects=True)


STAGED = 4


def gain_plan(z, p, mine, s, out, ss, rs):
    n = p.n

    def exchange(k, axis):
        return pltpu.make_async_remote_copy(
            src_ref=s.gain_sent.at[k], dst_ref=s.gain_in.at[k], send_sem=ss.at[k], recv_sem=rs.at[k], device_id=p.partner(axis), device_id_type=MESH
        )

    def pass_on(zo, up):
        ref = s.gain_all.at[zo]
        sem = 3 + zo + (0 if up else n)
        dev = p.dev(z=p.z + 1 if up else p.z - 1)
        return pltpu.make_async_remote_copy(src_ref=ref, dst_ref=ref, send_sem=ss.at[sem], recv_sem=rs.at[3 + zo], device_id=dev, device_id_type=MESH)

    def line(zo):
        @pl.when((zo <= p.z) & (p.z < n - 1))
        def _():
            pass_on(zo, True).start()

        @pl.when((zo >= p.z) & (p.z > 0))
        def _():
            pass_on(zo, False).start()

    def begin():
        s.gain_sent[0] = mine[...]
        exchange(0, "c").start()

    def step(k, axis, follow):
        def run():
            exchange(k, axis).wait_recv()
            total = s.gain_sent[k] + s.gain_in[k]
            if follow:
                s.gain_sent[k + 1] = total
                exchange(k + 1, follow).start()
            else:
                s.gain_all[p.z] = total
                line(p.z)

        return run

    def hop(d):
        def take(zo):
            ref = s.gain_all.at[zo]
            pltpu.make_async_remote_copy(
                src_ref=ref, dst_ref=ref, send_sem=ss.at[0], recv_sem=rs.at[3 + zo], device_id=p.partner("c"), device_id_type=MESH
            ).wait_recv()
            line(zo)

        def run():
            @pl.when(p.z - d >= 0)
            def _():
                take(p.z - d)

            @pl.when(p.z + d < n)
            def _():
                take(p.z + d)

        return run

    def finish():
        total = s.gain_all[0]
        for zo in range(1, n):
            total = total + s.gain_all[zo]
        out[...] = total

    def drain():
        for k, axis in enumerate("cxy"):
            exchange(k, axis).wait_send()
        for zo in range(n):

            @pl.when((zo <= p.z) & (p.z < n - 1))
            def _():
                pass_on(zo, True).wait_send()

            @pl.when((zo >= p.z) & (p.z > 0))
            def _():
                pass_on(zo, False).wait_send()

    return [begin, step(0, "c", "x"), step(1, "x", "y"), step(2, "y", "")] + [hop(d) for d in range(1, n)] + [finish], drain


def unpack_kernel(z):
    shards = weight_shards(z, F32)
    ins = dict(sums=((z.rows, BLOCK), F32), gain_sums=((8, z.padded), F32))
    outs = dict(shards, gain_grads=((2, z.width), F32))

    def body(i, o, s, sems):
        for k, name in enumerate(shards):
            getattr(o, name)[...] = i.sums[z.starts[k] : z.starts[k] + z.rows_of[k], : z.quarter]
        for q in range(4):
            o.gain_grads[:, q * z.quarter : (q + 1) * z.quarter] = i.gain_sums[:2, q * BLOCK : q * BLOCK + z.quarter]

    return make_call("unpack", body, ins, outs, {}, tuple(ins) + tuple(outs), [])


def rotary_tables(count_of_rows):
    position = np.arange(count_of_rows, dtype=np.float32)
    inverse = np.exp(np.arange(HEAD // 2, dtype=np.float32) * np.float32(-2.0 * math.log(10000.0) / HEAD))
    angle = position[:, None] * inverse[None, :]
    cos, sin = np.cos(angle), np.sin(angle)
    return np.concatenate([cos] * 4, axis=1), np.concatenate([-sin, sin] * 2, axis=1)


def local(wide, tokens, cotangent, norm_gains, w_qkv, w_out, w_gate, w_up, w_down):
    z = Sizes(tokens.shape[0], tokens.shape[1], w_qkv.shape[1] * wide, w_out.shape[0] * wide, w_gate.shape[1] * wide, wide)
    cos, sin = rotary_tables(z.tokens)
    small = dict(gains=norm_gains, cos=jnp.asarray(cos), sin=jnp.asarray(sin))
    shards = dict(zip(weight_shards(z, BF), (w_qkv.T, w_out, w_gate.T, w_up.T, w_down)))
    one = first_kernel(z)(tokens=tokens.T, **small, **shards)
    kept = {"first_" + n: one[n] for n in kept_shapes(z)}
    weights = {n: one[n] for n in ("gathered", "dense_qkv", "dense_out")}
    two = middle_kernel(z)(tokens=one["start"], state=one["result"], cotangent=cotangent.T, **small, **kept, **weights)
    factors = {n + "1": one[n] for n in ("normed", "normed2", "heads", "hidden")}
    out = unpack_kernel(z)(**last_kernel(z)(**factors, **two))
    grads = [out[n] for n in weight_shards(z, F32)]
    return (two["result"].T, two["grad_in"].T, out["gain_grads"], grads[0].T, grads[1], grads[2].T, grads[3].T, grads[4])


def solution(mesh):
    return jax.shard_map(
        functools.partial(local, mesh.shape["wide"]),
        mesh=mesh,
        in_specs=(
            P(("mp", "wide"), None),
            P(("mp", "wide"), None),
            P(),
            P("mp", "wide"),
            P("wide", "mp"),
            P("mp", "wide"),
            P("mp", "wide"),
            P("wide", "mp"),
        ),
        out_specs=(
            P(("mp", "wide"), None),
            P(("mp", "wide"), None),
            P(),
            P("mp", "wide"),
            P("wide", "mp"),
            P("mp", "wide"),
            P("mp", "wide"),
            P("wide", "mp"),
        ),
        check_vma=False,
    )
```

```python
import functools
import math
import types

import jax
import jax.numpy as jnp
import numpy as np
from jax import lax
from jax.experimental import pallas as pl
from jax.experimental.pallas import tpu as pltpu
from jax.sharding import PartitionSpec as P

EPSILON = 1e-05
NEGATIVE = -1e30
HEAD = 64
QUERY_HEADS = 15
KEY_HEADS = 5
GROUP = 3
LANES = 128
BLOCK = 256
BF = jnp.bfloat16
F32 = jnp.float32
MESH = pl.DeviceIdType.MESH
VMEM_BYTES = 62 * 2**20


def dot(a, b, contract):
    return lax.dot_general(a, b, ((contract[:1], contract[1:]), ((), ())), preferred_element_type=F32)


def nn(a, b):
    return dot(a, b, (1, 0))


def nt(a, b):
    return dot(a, b, (1, 1))


def tn(a, b):
    return dot(a, b, (0, 0))


def at(start, size):
    return pl.ds(pl.multiple_of(start, size), size)


def loop(count, body, **kw):
    def step(i, _):
        body(i)
        return 0

    lax.fori_loop(0, count, step, 0, **kw)


class Sizes:
    def __init__(self, tokens, width, qkv, heads, hidden, wide):
        self.tokens, self.width = tokens, width
        self.padded = 4 * BLOCK
        self.quarter = width // 4
        self.qkv, self.heads, self.hidden, self.wide = qkv, heads, hidden, wide
        up = lambda v: -(-v // 16) * 16
        self.rows_of = (qkv // wide, heads // wide, hidden // wide, hidden // wide, hidden // wide)
        self.blocks = tuple(up(v) for v in self.rows_of)
        self.starts = tuple(sum(self.blocks[:k]) for k in range(5))
        self.rows = sum(self.blocks)
        self.qkv_padded = -(-qkv // LANES) * LANES
        self.n = wide // 2
        self.group = 640 // self.rows_of[2]


def normalize(z, state, gain_row, out):
    def body(i):
        rows = at(i * 64, 64)
        s = state[rows, :].astype(F32)
        r = lax.rsqrt(jnp.sum(s * s, axis=1, keepdims=True) * (1.0 / z.width) + EPSILON)
        out[rows, :] = (s * r * gain_row).astype(BF)

    loop(z.tokens // 64, body, unroll=True)


def normalize_back(z, state, gain_row, incoming, passed, out, gain_out):
    def body(i):
        rows = at(i * 64, 64)
        s = state[rows, :].astype(F32)
        g = incoming[rows, :]
        r = lax.rsqrt(jnp.sum(s * s, axis=1, keepdims=True) * (1.0 / z.width) + EPSILON)
        n = s * r
        gn = g * n
        c = g * gain_row
        m = jnp.sum(gn * gain_row, axis=1, keepdims=True) * (1.0 / z.width)
        out[rows, :] = passed[rows, :].astype(F32) + r * (c - n * m)
        gain_out[...] += jnp.sum(gn.reshape(8, 8, z.padded), axis=0)

    loop(z.tokens // 64, body, unroll=True)


def half_mask(rows):
    return lax.broadcasted_iota(jnp.int32, (rows, LANES), 1) < HEAD


def swap_pairs(v):
    lane = lax.rem(lax.broadcasted_iota(jnp.int32, v.shape, 1), HEAD)
    return jnp.where(lane < HEAD // 2, pltpu.roll(v, LANES - HEAD // 2, 1), pltpu.roll(v, HEAD // 2, 1))


def project_qkv(z, r):
    half = 5 * LANES
    for start in (0, half, 2 * half):
        size = min(half, z.qkv - start)
        r.qkv[:, start : start + size] = nt(r.normed[...], r.w_qkv[start : start + size, :])

    def body(i):
        rows = at(i * LANES, LANES)
        lo = half_mask(LANES)
        c, s = r.cos[rows, :], r.sin[rows, :]
        zero = jnp.zeros((LANES, LANES), F32)

        def place(target, turned, v, first, second):
            other, across = pltpu.roll(v, HEAD, 1), v.T.astype(BF)
            if first is not None:
                target[0, first, rows, :] = jnp.where(lo, v, zero).astype(BF)
                target[1, first, rows, :] = jnp.where(lo, zero, other).astype(BF)
                turned[first, :, rows] = across[:HEAD]
            if second is not None:
                target[0, second, rows, :] = jnp.where(lo, other, zero).astype(BF)
                target[1, second, rows, :] = jnp.where(lo, zero, v).astype(BF)
                turned[second, :, rows] = across[HEAD:]

        for m in range(10):
            lanes = slice(m * LANES, (m + 1) * LANES)
            v = r.qkv[rows, lanes]
            v = v * c + swap_pairs(v) * s
            if m < 8:
                q = v * HEAD**-0.5
                r.query[rows, lanes] = (q if m < 7 else jnp.where(lo, q, zero)).astype(BF)
            if m >= 7:
                place(r.keys, r.keys_turned, v, None if m == 7 else 2 * m - 15, 2 * m - 14)
        for m in range(3):
            v = r.qkv[rows, (10 + m) * LANES : (11 + m) * LANES]
            place(r.values, r.values_turned, v, 2 * m, 2 * m + 1 if m < 2 else None)

    loop(z.tokens // LANES, body, unroll=True)


def masked(s):
    rows = lax.broadcasted_iota(jnp.int32, s.shape, 0)
    return jnp.where(rows <= lax.broadcasted_iota(jnp.int32, s.shape, 1), s, NEGATIVE)


def attend(z, r, first, count):
    t = z.tokens // 2

    def one(m, parity):
        h = 2 * m + parity
        g = h // GROUP
        cols = at(m * LANES, LANES)
        early, late = r.query[:t, cols], r.query[t:, cols]
        key, value = r.keys.at[parity, g], r.values_turned.at[g]
        a = masked(nt(key[:t, :], early))
        b, c = nt(key[:t, :], late), masked(nt(key[t:, :], late))
        a = jnp.exp(a - jnp.max(a, axis=0, keepdims=True))
        high = jnp.maximum(jnp.max(b, axis=0, keepdims=True), jnp.max(c, axis=0, keepdims=True))
        b, c = jnp.exp(b - high), jnp.exp(c - high)
        a = (a * (1.0 / jnp.sum(a, axis=0, keepdims=True))).astype(BF)
        inverse = 1.0 / (jnp.sum(b, axis=0, keepdims=True) + jnp.sum(c, axis=0, keepdims=True))
        b, c = (b * inverse).astype(BF), (c * inverse).astype(BF)
        r.weights[h, 0], r.weights[h, 1], r.weights[h, 2] = a, b, c
        return nn(value[:, :t], a), nn(value[:, :t], b) + nn(value[:, t:], c)

    def put(m, low, high):
        cols = at(m * LANES, LANES)
        r.heads[:t, cols] = jnp.concatenate([low[0], high[0]], axis=0).T.astype(BF)
        r.heads[t:, cols] = jnp.concatenate([low[1], high[1]], axis=0).T.astype(BF)

    def pair(i):
        put(first + i, one(first + i, 0), one(first + i, 1))

    last = QUERY_HEADS // 2
    loop(min(first + count, last) - first, pair, unroll=True)
    if first + count > last:
        empty = jnp.zeros((HEAD, t), F32)
        put(last, one(last, 0), (empty, empty))


def forward_steps(z, r):
    chunk = r.chunk

    def start():
        normalize(z, r.state, r.gains[0:1, :], r.normed)

    def qkv():
        r.need_qkv()
        project_qkv(z, r)

    def heads(first):
        return lambda: attend(z, r, first, 2)

    def out():
        r.need_out()
        for n in range(2):
            cols = slice(n * 512, (n + 1) * 512)
            r.middle[:, cols] = r.state[:, cols].astype(F32) + nn(r.heads[:, : z.heads], r.w_out[:, cols])
        normalize(z, r.middle, r.gains[1:2, :], r.normed2)

    def gate_up(i):
        cols = at(i * chunk, chunk)
        gate = nt(r.normed2[...], r.gate_block(i))
        up = nt(r.normed2[...], r.up_block(i))
        r.gate[:, cols] = gate.astype(BF)
        r.up[:, cols] = up.astype(BF)
        r.hidden[:, cols] = (gate * jax.nn.sigmoid(gate) * up).astype(BF)

    def ffn():
        r.need_gate()
        loop(z.hidden // chunk, gate_up, unroll=True)

    def some(first, count):
        return lambda: loop(count, lambda i: gate_up(first + i), unroll=True)

    def down():
        r.need_down()
        r.down()

    if r.halves:
        half = z.hidden // chunk // 2
        return [start, qkv, heads(0), heads(2), heads(4), heads(6), out, some(0, half), some(half, half), down]
    return [start, qkv, lambda: attend(z, r, 0, 8), out, ffn, down]


def forward(z, r):
    for step in forward_steps(z, r):
        step()


def attend_back(z, r):
    t = z.tokens // 2
    r.key_grad[...] = jnp.zeros_like(r.key_grad)
    r.value_grad[...] = jnp.zeros_like(r.value_grad)
    first, second = slice(0, t), slice(t, 2 * t)

    def one(m, parity):
        h = 2 * m + parity
        g = h // GROUP
        cols = at(m * LANES, LANES)
        key, value = r.keys_turned.at[g], r.values.at[parity, g]
        d1, d2 = r.heads_grad[first, cols], r.heads_grad[second, cols]
        q1, q2 = r.query[first, cols], r.query[second, cols]
        a, b, c = r.weights[h, 0], r.weights[h, 1], r.weights[h, 2]
        fa, fb, fc = a.astype(F32), b.astype(F32), c.astype(F32)
        ga, gb, gc = nt(value[first, :], d1), nt(value[first, :], d2), nt(value[second, :], d2)
        ta, tb, tc = fa * ga, fb * gb, fc * gc
        da = jnp.sum(ta, axis=0, keepdims=True)
        db = jnp.sum(tb, axis=0, keepdims=True) + jnp.sum(tc, axis=0, keepdims=True)
        sa, sb, sc = (ta - fa * da).astype(BF), (tb - fb * db).astype(BF), (tc - fc * db).astype(BF)
        r.value_grad[parity, g, first, :] += nn(a, d1) + nn(b, d2)
        r.value_grad[parity, g, second, :] += nn(c, d2)
        r.key_grad[parity, g, first, :] += nn(sa, q1) + nn(sb, q2)
        r.key_grad[parity, g, second, :] += nn(sc, q2)
        return nn(key[:, :t], sa), nn(key[:, :t], sb) + nn(key[:, t:], sc)

    def put(m, low, high):
        cols = at(m * LANES, LANES)
        r.query_grad[first, cols] = jnp.concatenate([low[0], high[0]], axis=0).T
        r.query_grad[second, cols] = jnp.concatenate([low[1], high[1]], axis=0).T

    last = QUERY_HEADS // 2
    loop(last, lambda m: put(m, one(m, 0), one(m, 1)), unroll=True)
    empty = jnp.zeros((HEAD, t), F32)
    put(last, one(last, 0), (empty, empty))


def unrotate_qkv(z, r):
    def unrotate(i):
        rows = at(i * 64, 64)
        lo = half_mask(64)
        c, s = r.cos[rows, :], r.sin[rows, :]

        def turn(v):
            return v * c - swap_pairs(v) * s

        def joined(ref, g):
            a, b = ref[0, g, rows, :], ref[1, g, rows, :]
            return jnp.where(lo, a + pltpu.roll(b, HEAD, 1), 0.0), jnp.where(lo, 0.0, b + pltpu.roll(a, HEAD, 1))

        def put(m, v):
            r.qkv_back[rows, m * LANES : (m + 1) * LANES] = v.astype(BF)

        k = [joined(r.key_grad, g) for g in range(KEY_HEADS)]
        v = [joined(r.value_grad, g) for g in range(KEY_HEADS)]
        scale = HEAD**-0.5
        for m in range(7):
            put(m, turn(r.query_grad[rows, m * LANES : (m + 1) * LANES] * scale))
        last = jnp.where(lo, r.query_grad[rows, 7 * LANES : 8 * LANES] * scale, 0.0)
        put(7, turn(last + k[0][1]))
        put(8, turn(k[1][0] + k[2][1]))
        put(9, turn(k[3][0] + k[4][1]))
        put(10, v[0][0] + v[1][1])
        put(11, v[2][0] + v[3][1])
        put(12, v[4][0])

    loop(z.tokens // 64, unrotate, unroll=True)


def backward_steps(z, r):
    ffn_grad = r.ffn_grad

    def rounded():
        def body(i):
            rows = at(i * 64, 64)
            ffn_grad[rows, :] = r.grad[rows, :].astype(BF)

        if r.grad is not ffn_grad:
            loop(z.tokens // 64, body, unroll=True)

    def ffn():
        r.need_down()
        r.need_kept()

        def body(n):
            cols = at(n * 512, 512)
            back = nt(ffn_grad[...], r.w_down[cols, :])
            gate = r.gate[:, cols].astype(F32)
            up = r.up[:, cols].astype(F32)
            s = jax.nn.sigmoid(gate)
            r.gate[:, cols] = (back * up * s * (1.0 + gate * (1.0 - s))).astype(BF)
            r.up[:, cols] = (back * gate * s).astype(BF)

        loop(z.hidden // 512, body, unroll=True)
        r.ffn_done()

    def into():
        r.need_gate()

        def body(n):
            cols = at(n * 512, 512)
            r.normed_grad[:, cols] = nn(r.gate[...], r.w_gate[:, cols]) + nn(r.up[...], r.w_up[:, cols])

        loop(z.padded // 512, body, unroll=True)

    def norm2():
        r.need_middle()
        normalize_back(z, r.middle, r.gains[1:2, :], r.normed_grad, r.grad, r.middle_grad, r.gain_out.at[1])

        def body(i):
            rows = at(i * 64, 64)
            r.attn_back[rows, :] = r.middle_grad[rows, :].astype(BF)

        loop(z.tokens // 64, body, unroll=True)
        r.norm2_done()

    def out():
        r.need_attention()
        r.need_out()
        w = z.heads
        for start, size in ((0, 512), (512, w - 512)):
            cols = slice(start, start + size)
            back = nt(r.attn_back[...], r.w_out[cols, :])
            r.heads_grad[:, cols] = back.astype(BF)
        r.heads_grad[:, w:] = jnp.zeros((z.tokens, z.padded - w), BF)

    def attention():
        attend_back(z, r)
        r.attention_done()

    def unrotate():
        unrotate_qkv(z, r)
        r.unrotate_done()

    def qkv():
        r.need_qkv()
        for n in range(2):
            cols = slice(n * 512, (n + 1) * 512)
            r.normed_grad[:, cols] = nn(r.qkv_back[:, : z.qkv], r.w_qkv[:, cols])

    def norm1():
        normalize_back(z, r.state, r.gains[0:1, :], r.normed_grad, r.middle_grad, r.grad_in, r.gain_out.at[0])

    return [rounded, ffn, into, norm2, out, attention, unrotate, qkv, norm1]


def backward(z, r):
    for step in backward_steps(z, r):
        step()


def kept_shapes(z):
    t, d, f = z.tokens, z.padded, z.hidden
    return dict(
        query=((t, d), BF),
        keys=((2, KEY_HEADS, t, LANES), BF),
        values=((2, KEY_HEADS, t, LANES), BF),
        keys_turned=((KEY_HEADS, HEAD, t), BF),
        weights=((QUERY_HEADS, 3, t // 2, t // 2), BF),
        heads=((t, d), BF),
        middle=((t, d), F32),
        gate=((t, f), BF),
        up=((t, f), BF),
    )


def layer_shapes(z):
    t, d, f = z.tokens, z.padded, z.hidden
    return dict(kept_shapes(z), normed=((t, d), BF), normed2=((t, d), BF), hidden=((t, f), BF), values_turned=((KEY_HEADS, HEAD, t), BF))


def weight_shapes(z):
    d, f = z.padded, z.hidden
    return dict(w_qkv=((z.qkv, d), BF), w_out=((z.heads, d), BF), w_gate=((f, d), BF), w_up=((f, d), BF), w_down=((f, d), BF))


def tables(z):
    t, d = z.tokens, z.padded
    return dict(gains=((2, z.width), F32), cos=((t, LANES), F32), sin=((t, LANES), F32))


def blocks_shape(z):
    return ((2, 2, z.n, 2, z.rows, BLOCK), BF)


def rows_first(z):
    t, d, f = z.tokens, z.padded, z.hidden
    left = dict(qkv_back=((t, z.qkv_padded), BF), heads=((t, d), BF), gate=((t, f), BF), up=((t, f), BF), hidden=((t, f), BF))
    right = dict(normed=((t, d), BF), attn_back=((t, d), BF), normed2=((t, d), BF), ffn_grad=((t, d), BF))
    return left, right


def make_call(name, body, ins, outs, scratch, in_vmem, sems, **params):
    n_in, n_out, n_s = list(ins), list(outs), list(scratch)

    def kernel(*refs):
        a, b, c = len(n_in), len(n_in) + len(n_out), len(n_in) + len(n_out) + len(n_s)
        group = lambda names, part: types.SimpleNamespace(**dict(zip(names, part)))
        body(group(n_in, refs[:a]), group(n_out, refs[a:b]), group(n_s, refs[b:c]), refs[c:])

    spec = lambda n: pl.BlockSpec(memory_space=pltpu.VMEM if n in in_vmem else pl.ANY)
    call = pl.pallas_call(
        kernel,
        out_shape=[jax.ShapeDtypeStruct(*outs[n]) for n in n_out],
        in_specs=[spec(n) for n in n_in],
        out_specs=[spec(n) for n in n_out],
        scratch_shapes=[pltpu.VMEM(*scratch[n]) for n in n_s] + [pltpu.SemaphoreType.DMA(s) for s in sems],
        compiler_params=pltpu.CompilerParams(vmem_limit_bytes=VMEM_BYTES, **params),
        name=name,
    )
    return lambda **vals: dict(zip(n_out, call(*[vals[n] for n in n_in])))


class Copies:
    def __init__(self, sems):
        self.sems, self.used, self.open = sems, 0, {}

    def start(self, src, dst):
        key = self.used
        self.used += 1
        self.open[key] = pltpu.make_async_copy(src, dst, self.sems.at[key])
        self.open[key].start()
        return key

    def wait(self, keys):
        for key in keys:
            if key in self.open:
                self.open.pop(key).wait()

    def later(self, keys):
        return lambda: self.wait(keys)

    def finish(self):
        self.wait(list(self.open))


SMALL = ("gains", "cos", "sin", "tokens")


def pad_into(z, target, source, turned=True):
    target[...] = jnp.zeros(target.shape, target.dtype)
    for q in range(4):
        part = slice(q * z.quarter, (q + 1) * z.quarter)
        value = source[part, :].astype(F32).T.astype(target.dtype) if turned else source[:, part]
        target[:, q * BLOCK : q * BLOCK + z.quarter] = value


def unpad_into(z, target, value, first=0):
    for q in range(value.shape[1] // BLOCK):
        start = (first + q) * z.quarter
        target[start : start + z.quarter, :] = value[:, q * BLOCK : (q + 1) * BLOCK].T[: z.quarter, :]


def middle_kernel(z):
    t, d = z.tokens, z.padded
    kept = kept_shapes(z)
    ins = dict(tables(z), tokens=((t, d), BF), state=((t, d), F32), cotangent=((z.width, t), BF))
    ins.update(gathered=blocks_shape(z), dense_qkv=((z.qkv, d), BF), dense_out=((z.heads, d), BF))
    ins.update({"first_" + n: v for n, v in kept.items()})
    left, right = rows_first(z)
    both = dict(left, **right)
    outs = dict(result=((z.width, t), F32), grad_in=((z.width, t), F32), gain=((8, d), F32))
    outs.update({n + "2": v for n, v in both.items()})
    outs.update({n + "1": both[n] for n in ("qkv_back", "attn_back", "gate", "up", "ffn_grad")})
    scratch = dict(layer_shapes(z), **weight_shapes(z), state=((t, d), F32), grad=((t, d), BF))
    scratch.update(qkv=((t, z.qkv_padded), F32), plain=((z.width, t), F32), gain_out=((2, 8, d), F32), gains=((2, d), F32))
    scratch.update(key_grad=((2, KEY_HEADS, t, LANES), F32), value_grad=((2, KEY_HEADS, t, LANES), F32))

    def body(i, o, s, sems):
        cps = Copies(sems[0])
        state = cps.start(i.state, s.state)
        qkv = cps.start(i.dense_qkv, s.w_qkv)
        pad_into(z, s.gains, i.gains, False)
        s.gain_out[...] = jnp.zeros_like(s.gain_out)
        none = lambda: None
        r = types.SimpleNamespace(**vars(s))
        vars(r).update(cos=i.cos, sin=i.sin, chunk=512, halves=False)
        r.gate_block = lambda n: s.w_gate[at(n * 512, 512), :]
        r.up_block = lambda n: s.w_up[at(n * 512, 512), :]

        def down():
            for n in range(2):
                cols = slice(n * 512, (n + 1) * 512)
                unpad_into(z, s.plain, s.middle[:, cols] + nn(s.hidden[...], s.w_down[:, cols]), 2 * n)

        r.down = down
        cps.wait([state])

        def need_qkv():
            cps.wait([qkv])
            vars(r).update(start_weights(z, cps, i, s))

        r.need_qkv = need_qkv
        forward(z, r)
        sent = dict(plain=cps.start(s.plain, o.result))
        for n, target in (("normed", o.normed2), ("normed2", o.normed22), ("hidden", o.hidden2), ("heads", o.heads2)):
            sent[n] = cps.start(getattr(s, n), target)
        pad_into(z, s.grad, i.cotangent)
        sent["grad"] = cps.start(s.grad, o.ffn_grad2)
        wait = lambda *names: (lambda: cps.wait([sent[n] for n in names]))

        back = types.SimpleNamespace(**vars(r))
        back.qkv_back = s.hidden.at[:, : z.qkv_padded]
        vars(back).update(heads_grad=s.normed2, attn_back=s.normed, normed_grad=s.qkv.at[:, :d], middle_grad=s.middle, query_grad=s.qkv.at[:, :d], grad_in=s.state)
        vars(back).update(ffn_grad=s.grad, need_kept=none, need_middle=wait("normed"), need_attention=wait("normed2"), need_qkv=none)
        loads = {}

        def send(n, source, target):
            sent[n] = cps.start(source, target)

        def load(n):
            loads[n] = cps.start(getattr(i, "first_" + n), getattr(s, n))

        def ffn_done():
            send("gate", s.gate, o.gate2)
            send("up", s.up, o.up2)

        def attention_done():
            wait("gate", "up", "heads", "hidden")()
            for n in ("gate", "up", "heads", "query", "keys", "values", "keys_turned", "weights"):
                load(n)

        back.ffn_done, back.attention_done = ffn_done, attention_done
        back.norm2_done = lambda: send("attn_back", s.normed, o.attn_back2)
        back.unrotate_done = lambda: send("qkv_back", back.qkv_back, o.qkv_back2)
        backward(z, back)
        load("middle")
        wait("grad")()

        first = types.SimpleNamespace(**vars(back))
        vars(first).update(grad=s.state, state=s.grad)
        first.need_kept = cps.later([loads["gate"], loads["up"]])
        first.need_middle = lambda: (cps.wait([loads["middle"]]), wait("attn_back")())
        first.need_attention = cps.later([loads[n] for n in ("heads", "query", "keys", "values", "keys_turned", "weights")])

        def ffn_done1():
            cps.start(s.gate, o.gate1)
            cps.start(s.up, o.up1)
            send("grad", s.grad, o.ffn_grad1)

        def attention_done1():
            wait("grad", "qkv_back")()
            send("tokens", i.tokens, s.grad)

        first.ffn_done, first.attention_done = ffn_done1, attention_done1
        first.norm2_done = lambda: send("attn_back", s.normed, o.attn_back1)
        first.unrotate_done = lambda: send("qkv_back", back.qkv_back, o.qkv_back1)
        first.need_qkv = lambda: wait("tokens")()
        backward(z, first)
        wait("plain")()
        unpad_into(z, s.plain, s.state[...])
        cps.start(s.plain, o.grad_in)
        o.gain[...] = jnp.zeros_like(o.gain)
        o.gain[0:1, :] = jnp.sum(s.gain_out[0], axis=0, keepdims=True)
        o.gain[1:2, :] = jnp.sum(s.gain_out[1], axis=0, keepdims=True)
        cps.finish()

    return make_call("second_layer", body, ins, outs, scratch, ("gains", "cos", "sin", "cotangent", "gain"), [(80,)])


def start_weights(z, cps, i, s):
    def blocks(w, k):
        w = w.reshape(z.n, 2, z.blocks[k], z.padded)
        rows = pl.ds(z.starts[k], z.blocks[k])
        return [cps.start(i.gathered.at[q // 2, q % 2, :, :, rows], w.at[:, :, :, q * BLOCK : (q + 1) * BLOCK]) for q in range(4)]

    out = [cps.start(i.dense_out, s.w_out)]
    gate = blocks(s.w_gate, 2) + blocks(s.w_up, 3)
    down = blocks(s.w_down, 4)
    return dict(need_out=cps.later(out), need_gate=cps.later(gate), need_down=cps.later(down))


class Place:
    def __init__(self, n):
        mp, w = lax.axis_index("mp"), lax.axis_index("wide")
        self.n = n
        self.x, self.y, self.c, self.z = lax.rem(mp, 2), mp // 2, lax.rem(w, 2), w // 2
        self.axes = ["y", "x"] + z_orders(n)

    def coordinate(self, axis):
        if axis[0] == "z":
            return lax.rem(self.z // 2 ** int(axis[1:]), 2)
        return getattr(self, axis)

    def partner(self, axis):
        away = 1 - 2 * self.coordinate(axis)
        x, y, c, z = self.x, self.y, self.c, self.z
        if axis == "x":
            x = x + away
        elif axis == "y":
            y = y + away
        elif axis == "c":
            c = c + away
        else:
            z = z + away * 2 ** int(axis[1:])
        return {"mp": y * 2 + x, "wide": z * 2 + c}

    def dev(self, z):
        return {"mp": self.y * 2 + self.x, "wide": z * 2 + self.c}

    def signal(self, device):
        pl.semaphore_signal(pltpu.get_barrier_semaphore(), inc=1, device_id=device, device_id_type=MESH)

    def greet_line(self):
        for axis in "xyc":
            self.signal(self.partner(axis))

        @pl.when(self.z > 0)
        def _():
            self.signal(self.dev(self.z - 1))

        @pl.when(self.z < self.n - 1)
        def _():
            self.signal(self.dev(self.z + 1))

    def met_line(self):
        count = 3 + jnp.where(self.z > 0, 1, 0) + jnp.where(self.z < self.n - 1, 1, 0)
        pl.semaphore_wait(pltpu.get_barrier_semaphore(), count)

    def greet(self):
        for axis in self.axes + ["c"]:
            self.signal(self.partner(axis))

    def met(self):
        pl.semaphore_wait(pltpu.get_barrier_semaphore(), len(self.axes) + 1)


def run_stages(entries):
    for entry in sorted(entries, key=lambda e: e[:2]):
        entry[2]()


def shares(units, weights):
    out, done, used = [], 0, 0
    for w in weights:
        done += w
        end = round(units * done / sum(weights))
        out.append(end - used)
        used = end
    return out


def row_chunks(start, rows, parts, orders, first=0):
    out, r = [], start
    for k, units in enumerate(shares(rows // 16, parts)):
        turn = orders[(first + k) % len(orders)]
        for order, u in zip(turn, shares(units, [1] * len(turn))):
            if u:
                out.append((r, 16 * u, order, k))
                r += 16 * u
    return out


GATHER_ORDERS = (("xzy", "yzx"), ("zxy", "zyx"), ("yzx", "xzy"))
GATHER_PARTS = (1,) * 10
GATHER_TIMES = ((-1.44, 0.95, 2.47, 0.87, 0.01, 0.95, 1.6), (-4.28, -0.02, 0.47, 0.69, 1.14, 2.95, 4.2))
STEP_GAP = 0.7


def along(p, axes, free, turned, rows):
    mine = [p.coordinate(a) for a in axes]
    return tuple(slice(None) if a in free else 1 - v if a == turned else v for a, v in zip(axes, mine)) + rows


def gather_plan(p, g, k, piece, ss, rs):
    r0, rc, order, _ = piece
    n, rows = p.n, pl.ds(r0, rc)
    a1, a2 = [a for a in order if a != "z"]
    z_first = order[0] == "z"

    def one(zo, other=False):
        x = 1 - p.x if other and a1 == "x" else p.x
        y = 1 - p.y if other and a1 == "y" else p.y
        return g.at[y, x, zo, p.c, rows]

    def pair(zo, other=False, c=None):
        c = p.c if c is None else c
        if a1 == "x":
            return g.at[1 - p.y if other else p.y, :, zo, c, rows]
        return g.at[:, 1 - p.x if other else p.x, zo, c, rows]

    def copy(ref, dev, s, r):
        return pltpu.make_async_remote_copy(src_ref=ref, dst_ref=ref, send_sem=ss.at[k, s], recv_sem=rs.at[k, r], device_id=dev, device_id_type=MESH)

    along = one if z_first else pair
    up = lambda zo: copy(along(zo), p.dev(p.z + 1), zo, zo)
    down = lambda zo: copy(along(zo), p.dev(p.z - 1), n + zo, zo)
    line_in = lambda zo: copy(along(zo), p.partner("c"), zo, zo)
    first = lambda zo, other=False: copy(one(zo, other), p.partner(a1), 2 * n + zo, n + zo)
    second = lambda zo, other=False: copy(pair(zo, other), p.partner(a2), 3 * n + zo, 2 * n + zo)

    def sibling(other, c=None):
        c = p.c if c is None else c
        if a1 == "x":
            part = g.at[1 - p.y if other else p.y, :, :, c, rows]
        else:
            part = g.at[:, 1 - p.x if other else p.x, :, c, rows]
        o = 1 if other else 0
        return copy(part, p.partner("c"), 4 * n + o, 3 * n + o)

    def line(zo):
        @pl.when((zo <= p.z) & (p.z < n - 1))
        def _():
            up(zo).start()

        @pl.when((zo >= p.z) & (p.z > 0))
        def _():
            down(zo).start()

    def at_distance(d, body):
        @pl.when(p.z - d >= 0)
        def _():
            body(p.z - d)

        @pl.when(p.z + d < n)
        def _():
            body(p.z + d)

    stages = []
    times = GATHER_TIMES[1 if z_first else 0]
    hop_time, step = times[1:3] if z_first else times[2:4]
    last_hop = hop_time + (n - 2) * step
    if z_first:

        def start():
            line(p.z)
            first(p.z).start()

        stages.append((times[0], start))
        for d in range(1, n):

            def hop(d=d):
                def body(zo):
                    line_in(zo).wait_recv()
                    line(zo)
                    first(zo).start()

                at_distance(d, body)

            stages.append((hop_time + (d - 1) * step, hop))

        def cross():
            for zo in range(n):
                first(zo, True).wait_recv()
                second(zo).start()

        stages.append((last_hop + times[3], cross))
    else:

        def start():
            first(p.z).start()

        def meet():
            first(p.z, True).wait_recv()
            line(p.z)
            second(p.z).start()

        stages += [(times[0], start), (times[1], meet)]
        for d in range(1, n):

            def hop(d=d):
                def body(zo):
                    line_in(zo).wait_recv()
                    line(zo)
                    second(zo).start()

                at_distance(d, body)

            stages.append((hop_time + (d - 1) * step, hop))

    def halfway():
        sibling(False).start()

    def arrived():
        for zo in range(n):
            second(zo, True).wait_recv()
        sibling(True).start()

    def done():
        sibling(False, 1 - p.c).wait_recv()
        sibling(True, 1 - p.c).wait_recv()

    def drain():
        for zo in range(n):

            @pl.when((zo <= p.z) & (p.z < n - 1))
            def _():
                up(zo).wait_send()

            @pl.when((zo >= p.z) & (p.z > 0))
            def _():
                down(zo).wait_send()

            second(zo).wait_send()
            if z_first:
                first(zo).wait_send()
        if not z_first:
            first(p.z).wait_send()
        sibling(False).wait_send()
        sibling(True).wait_send()

    return stages + [(last_hop + at_time, f) for at_time, f in zip(times[-3:], (halfway, arrived, done))], drain


def stage_times(table, count):
    more = count - len(table)
    return list(table[:-2]) + [table[-3] + 1 + k for k in range(more)] + [v + more for v in table[-2:]]


def first_kernel(z):
    t, d, n = z.tokens, z.padded, z.n
    pieces = row_chunks(0, z.rows, GATHER_PARTS, GATHER_ORDERS)
    layer = layer_shapes(z)
    shards = weight_shards(z, BF)
    ins = dict(tables(z), tokens=((z.width, t), BF), **shards)
    outs = dict({m: v for m, v in layer.items() if m != "values_turned"}, start=((t, d), BF), result=((t, d), F32), gathered=blocks_shape(z), dense_qkv=((z.qkv, d), BF), dense_out=((z.heads, d), BF))
    scratch = dict(layer, result=((t, d), F32), qkv=((t, z.qkv_padded), F32), blocks=blocks_shape(z))
    scratch.update(w_qkv=((z.qkv, d), BF), w_out=((z.heads, d), BF), start=((t, d), BF), gains=((2, d), F32))

    def body(i, o, s, sems):
        local, ss, rs = sems
        cps = Copies(local)
        p = Place(n)
        p.greet_line()
        for k, name in enumerate(shards):
            w = getattr(i, name)[...]
            rows = z.starts[k]
            s.blocks[p.y, p.x, p.z, p.c, rows : rows + z.blocks[k], :] = jnp.zeros((z.blocks[k], BLOCK), BF)
            s.blocks[p.y, p.x, p.z, p.c, rows : rows + z.rows_of[k], : z.quarter] = w
        p.met_line()

        def dense(k, target):
            per = z.rows_of[k]
            for j in range(z.wide):
                for q in range(4):
                    rows = s.blocks[q // 2, q % 2, j // 2, j % 2, z.starts[k] : z.starts[k] + per, :]
                    target[j * per : (j + 1) * per, q * BLOCK : (q + 1) * BLOCK] = rows

        def block(k):
            start, per, some = z.starts[k], z.rows_of[k], z.group // 2

            def read(j):
                rows = []
                for e in range(z.group):
                    quarters = [s.blocks[q // 2, q % 2, j * some + e // 2, e % 2, start : start + per, :] for q in range(4)]
                    rows.append(jnp.concatenate(quarters, axis=1))
                return jnp.concatenate(rows, axis=0)

            return read

        none = lambda: None
        r = types.SimpleNamespace(**vars(s))
        vars(r).update(cos=i.cos, sin=i.sin, state=s.start, chunk=640, halves=True)
        vars(r).update(gate_block=block(2), up_block=block(3), need_gate=none, need_down=none)

        def need_qkv():
            dense(0, s.w_qkv)
            cps.start(s.w_qkv, o.dense_qkv)

        def need_out():
            dense(1, s.w_out)
            cps.start(s.w_out, o.dense_out)

        def down():
            read = block(4)
            s.result[...] = s.middle[...]

            def add(j):
                s.result[...] += nn(s.hidden[:, at(j * 640, 640)], read(j))

            loop(z.hidden // 640, add)

        vars(r).update(need_qkv=need_qkv, need_out=need_out, down=down)
        steps = forward_steps(z, r)

        def begin():
            pad_into(z, s.gains, i.gains, False)
            pad_into(z, s.start, i.tokens)
            cps.start(s.start, o.start)
            forward_start()

        forward_start, steps[0] = steps[0], begin
        plans = [gather_plan(p, s.blocks, k, piece, ss, rs) for k, piece in enumerate(pieces)]
        entries = [(pieces[k][3] + at_time, k, f) for k, (stages, _) in enumerate(plans) for at_time, f in stages]
        done = [pieces[k][3] + stages[-1][0] for k, (stages, _) in enumerate(plans)]
        ready = [max(at_time for at_time, piece in zip(done, pieces) if piece[0] < e) for e in (z.starts + (z.rows,))[1:]]
        times = [0.5]
        for k in (0, 0, 0, 0, 0, 1, 3, 3, 4):
            times.append(max(ready[k] + 0.5, times[-1] + STEP_GAP))
        entries += [(at_time, -1, f) for at_time, f in zip(times, steps)]

        def out_of(part):
            rows = [p for p in pieces if p[3] == part]
            span = pl.ds(rows[0][0], sum(p[1] for p in rows))
            return lambda: cps.start(s.blocks.at[:, :, :, :, span], o.gathered.at[:, :, :, :, span])

        for part in range(len(GATHER_PARTS)):
            entries.append((max(at_time for at_time, piece in zip(done, pieces) if piece[3] == part), 100 + part, out_of(part)))

        def keep(*names):
            return lambda: [cps.start(getattr(s, m), getattr(o, m)) for m in names]

        entries += [(times[5], 0, keep("normed", "query", "keys", "values", "keys_turned", "weights", "heads"))]
        entries += [(times[6], 0, keep("middle", "normed2")), (times[8], 0, keep("gate", "up", "hidden"))]
        run_stages(entries)
        cps.start(s.result, o.result)
        for _, drain in plans:
            drain()
        cps.finish()

    sems = [(40,), (len(pieces), 4 * n + 2), (len(pieces), 3 * n + 2)]
    return make_call("first_layer", body, ins, outs, scratch, SMALL + tuple(shards), sems, collective_id=1, has_side_effects=True)


def z_orders(n):
    return ["z%d" % k for k in reversed(range(n.bit_length() - 1))]


def reduce_orders(n):
    z = z_orders(n)[::-1]
    half = len(z) // 2
    first, second = [(b,) + tuple(z[:half]) + (a,) + tuple(z[half:]) for a, b in ("xy", "yx")]
    return ((first, second), (second, first))


REDUCE_WEIGHTS = (1, 4, 0, 2, 3)
REDUCE_PARTS = (2, 1, 3, 3, 3)
REDUCE_TIMES = (0.8, 2.71, 4.93, 7.05, 9.17)
WORK_LEAD, WORK_STEP = 0.77, 0.146


def weight_shards(z, kind):
    names = ("w_qkv_shard", "w_out_shard", "w_gate_shard", "w_up_shard", "w_down_shard")
    return {name: ((rows, z.quarter), kind) for name, rows in zip(names, z.rows_of)}


def add_into(target, extra):
    target[...] = target[...] + extra[...].astype(target.dtype)


def reduce_plan(p, t, from_sibling, bufs, out, k, piece, ss, rs):
    r0, rc, order, _ = piece
    axes, last = p.axes, len(order) - 1
    rows = pl.ds(r0, rc)

    def part(ref, s, other):
        return ref.at[along(p, axes, order[s + 1 :], order[s] if other else None, (rows,))]

    def step(s):
        return pltpu.make_async_remote_copy(
            src_ref=part(t, s, True),
            dst_ref=bufs[s].at[(slice(None),) * (last - s) + (rows,)],
            send_sem=ss.at[k, s],
            recv_sem=rs.at[k, s],
            device_id=p.partner(order[s]),
            device_id_type=MESH,
        )

    def meet():
        add_into(part(t, 0, True), part(from_sibling, 0, True))
        step(0).start()
        add_into(part(t, 0, False), part(from_sibling, 0, False))

    def follow(s):
        step(s - 1).wait_recv()
        left = [a for a in axes if a in order[s:]]
        for other in (True, False):
            side = 1 - p.coordinate(order[s]) if other else p.coordinate(order[s])
            index = tuple(side if a == order[s] else slice(None) for a in left) + (rows,)
            add_into(part(t, s, other), bufs[s - 1].at[index])
            if other:
                step(s).start()

    def finish():
        step(last).wait_recv()
        out[rows, :] = part(t, last, False)[...].astype(F32) + bufs[last][rows, :].astype(F32)

    def drain():
        for s in range(last + 1):
            step(s).wait_send()

    return [meet] + [functools.partial(follow, s) for s in range(1, last + 1)] + [finish], drain


def last_kernel(z):
    t, d, n = z.tokens, z.padded, z.n
    left, right = rows_first(z)
    both = dict(left, **right)
    ins = {m + k: v for m, v in both.items() for k in "12"}
    ins.update(gain=((8, d), F32))
    outs = dict(sums=((z.rows, BLOCK), F32), gain_sums=((8, d), F32))
    two = lambda v: ((2 * t, v[0][1]), BF)
    scratch = {m: two(v) for m, v in both.items() if m not in ("gate", "up")}
    stage = max(z.rows_of)
    scratch.update(
        t=((2, 2, n, z.rows, BLOCK), BF),
        staged=((STAGED, 2, 2, stage, BLOCK), BF),
        from_sibling=((2, 2, n, z.rows, BLOCK), BF),
        gain_sent=((n.bit_length() + 2, 8, d), F32),
        gain_in=((n.bit_length() + 2, 8, d), F32),
    )
    pairs = 2 + n.bit_length() - 1
    for k in range(pairs):
        scratch["step%d" % k] = ((2,) * (pairs - 1 - k) + (z.rows, BLOCK), BF)
    order, parts = REDUCE_WEIGHTS, REDUCE_PARTS
    pieces, starts = [], {}
    slot = 1
    for k in order:
        starts[k] = slot
        for r0, rc, way, part in row_chunks(z.starts[k], z.blocks[k], (1,) * parts[k], reduce_orders(n), slot):
            pieces.append((r0, rc, way, slot + part, k))
        slot += parts[k]

    def body(i, o, s, sems):
        local, ss, rs, sib_s, sib_r, gain_s, gain_r = sems
        cps = Copies(local)
        need = {}

        names = (("qkv_back", "normed"), ("heads", "attn_back"), ("gate", "normed2"), ("up", "normed2"), ("hidden", "ffn_grad"))
        in_hidden = ("hidden", "gate", "up")

        def load(k):
            for m in names[k]:
                if m not in need:
                    target = s.hidden if m in in_hidden else getattr(s, m)
                    need[m] = cps.later([cps.start(getattr(i, m + a), target.at[pl.ds((2 - int(a)) * t, t)]) for a in "12"])

        load(order[0])
        p = Place(n)
        p.greet()
        p.met()
        count = [0]

        def sibling(k, zo, slot):
            rows = pl.ds(z.starts[k], z.blocks[k])
            return pltpu.make_async_remote_copy(
                src_ref=s.staged.at[slot, :, :, pl.ds(0, z.blocks[k])],
                dst_ref=s.from_sibling.at[:, :, zo, rows],
                send_sem=sib_s.at[slot],
                recv_sem=sib_r.at[k, zo],
                device_id=p.partner("c"),
                device_id_type=MESH,
            )

        sent = {}

        def put(k, zo, slot, a, b):
            per = z.rows_of[k]
            own, other = jnp.where(p.c == 0, a, b).astype(BF), jnp.where(p.c == 0, b, a).astype(BF)
            for q in range(4):
                lanes = slice(q * BLOCK, (q + 1) * BLOCK)
                s.t[q // 2, q % 2, zo, z.starts[k] : z.starts[k] + per, :] = own[:, lanes]
                s.staged[slot, q // 2, q % 2, :per, :] = other[:, lanes]

        some = [1, 1] + [z.group // 2] * 3

        def work(k, first):
            per = z.rows_of[k]

            def run():
                if first == 0:
                    load(k)
                    for m in names[k]:
                        need[m]()
                    after = order[order.index(k) + 1 :][:1]
                    if after and not (names[k][0] in in_hidden and names[after[0]][0] in in_hidden):
                        load(after[0])
                m_left = (s.qkv_back, s.heads, s.hidden, s.hidden, s.hidden)[k]
                m_right = (s.normed, s.attn_back, s.normed2, s.normed2, s.ffn_grad)[k]
                width = 2 * per * some[k]
                value = tn(m_left[:, first * 2 * per : first * 2 * per + width], m_right[...])
                for e in range(some[k]):
                    zo = first + e
                    slot = count[0] % STAGED
                    if slot in sent:
                        sent.pop(slot).wait_send()
                    count[0] += 1
                    put(k, zo, slot, value[2 * e * per : (2 * e + 1) * per], value[(2 * e + 1) * per : (2 * e + 2) * per])
                    sent[slot] = sibling(k, zo, slot)
                    sent[slot].start()

            return run

        latest = REDUCE_TIMES[0] - 0.01
        entries = []
        for k in order:
            for first in range(0, n, some[k]):
                at_time = starts[k] + min(first * 4 / n * WORK_STEP * parts[k] - WORK_LEAD, latest)
                entries.append((at_time, -1, work(k, first)))
        met = set()

        def after_sibling(k, f):
            def run():
                if k not in met:
                    met.add(k)
                    for zo in range(n):
                        sibling(k, zo, 0).wait_recv()
                f()

            return run

        cube = lambda ref: ref.reshape((2,) * pairs + (z.rows, BLOCK))
        bufs = [getattr(s, "step%d" % k) for k in range(pairs)]
        plans = [reduce_plan(p, cube(s.t), cube(s.from_sibling), bufs, o.sums, k, piece[:4], ss, rs) for k, piece in enumerate(pieces)]
        when = stage_times(REDUCE_TIMES, pairs + 1)
        for k, (stages, _) in enumerate(plans):
            stages[0] = after_sibling(pieces[k][4], stages[0])
        entries += [(pieces[k][3] + at_time, k, f) for k, (stages, _) in enumerate(plans) for at_time, f in zip(when, stages)]
        stages, gains_drain = gain_plan(p, i.gain, s, o.gain_sums, gain_s, gain_r)
        entries += [(1 + k, 100, f) for k, f in enumerate(stages)]
        run_stages(entries)
        for _, drain in plans:
            drain()
        for c in sent.values():
            c.wait_send()
        gains_drain()
        cps.finish()

    sems = [(40,), (len(pieces), pairs), (len(pieces), pairs), (STAGED,), (5, n), (pairs + 1,), (pairs + 1,)]
    return make_call("gradients", body, ins, outs, scratch, ("gain", "sums", "gain_sums"), sems, collective_id=2, has_side_effects=True)


STAGED = 4


def gain_plan(p, mine, s, out, ss, rs):
    axes = ["c"] + p.axes

    def exchange(k):
        return pltpu.make_async_remote_copy(
            src_ref=s.gain_sent.at[k], dst_ref=s.gain_in.at[k], send_sem=ss.at[k], recv_sem=rs.at[k], device_id=p.partner(axes[k]), device_id_type=MESH
        )

    def begin():
        s.gain_sent[0] = mine[...]
        exchange(0).start()

    def step(k):
        exchange(k).wait_recv()
        total = s.gain_sent[k] + s.gain_in[k]
        if k + 1 < len(axes):
            s.gain_sent[k + 1] = total
            exchange(k + 1).start()
        else:
            out[...] = total

    def drain():
        for k in range(len(axes)):
            exchange(k).wait_send()

    return [begin] + [functools.partial(step, k) for k in range(len(axes))], drain


def unpack_kernel(z):
    shards = weight_shards(z, F32)
    ins = dict(sums=((z.rows, BLOCK), F32), gain_sums=((8, z.padded), F32))
    outs = dict(shards, gain_grads=((2, z.width), F32))

    def body(i, o, s, sems):
        for k, name in enumerate(shards):
            getattr(o, name)[...] = i.sums[z.starts[k] : z.starts[k] + z.rows_of[k], : z.quarter]
        for q in range(4):
            o.gain_grads[:, q * z.quarter : (q + 1) * z.quarter] = i.gain_sums[:2, q * BLOCK : q * BLOCK + z.quarter]

    return make_call("unpack", body, ins, outs, {}, tuple(ins) + tuple(outs), [])


def rotary_tables(count_of_rows):
    position = np.arange(count_of_rows, dtype=np.float32)
    inverse = np.exp(np.arange(HEAD // 2, dtype=np.float32) * np.float32(-2.0 * math.log(10000.0) / HEAD))
    angle = position[:, None] * inverse[None, :]
    cos, sin = np.cos(angle), np.sin(angle)
    return np.concatenate([cos] * 4, axis=1), np.concatenate([-sin, sin] * 2, axis=1)


def local(wide, tokens, cotangent, norm_gains, w_qkv, w_out, w_gate, w_up, w_down):
    z = Sizes(tokens.shape[0], tokens.shape[1], w_qkv.shape[1] * wide, w_out.shape[0] * wide, w_gate.shape[1] * wide, wide)
    cos, sin = rotary_tables(z.tokens)
    small = dict(gains=norm_gains, cos=jnp.asarray(cos), sin=jnp.asarray(sin))
    shards = dict(zip(weight_shards(z, BF), (w_qkv.T, w_out, w_gate.T, w_up.T, w_down)))
    one = first_kernel(z)(tokens=tokens.T, **small, **shards)
    kept = {"first_" + n: one[n] for n in kept_shapes(z)}
    weights = {n: one[n] for n in ("gathered", "dense_qkv", "dense_out")}
    two = middle_kernel(z)(tokens=one["start"], state=one["result"], cotangent=cotangent.T, **small, **kept, **weights)
    factors = {n + "1": one[n] for n in ("normed", "normed2", "heads", "hidden")}
    out = unpack_kernel(z)(**last_kernel(z)(**factors, **two))
    grads = [out[n] for n in weight_shards(z, F32)]
    return (two["result"].T, two["grad_in"].T, out["gain_grads"], grads[0].T, grads[1], grads[2].T, grads[3].T, grads[4])


def solution(mesh):
    return jax.shard_map(
        functools.partial(local, mesh.shape["wide"]),
        mesh=mesh,
        in_specs=(
            P(("mp", "wide"), None),
            P(("mp", "wide"), None),
            P(),
            P("mp", "wide"),
            P("wide", "mp"),
            P("mp", "wide"),
            P("mp", "wide"),
            P("wide", "mp"),
        ),
        out_specs=(
            P(("mp", "wide"), None),
            P(("mp", "wide"), None),
            P(),
            P("mp", "wide"),
            P("wide", "mp"),
            P("mp", "wide"),
            P("mp", "wide"),
            P("wide", "mp"),
        ),
        check_vma=False,
    )
```

```python
import functools
import math
import types

import jax
import jax.numpy as jnp
import numpy as np
from jax import lax
from jax.experimental import pallas as pl
from jax.experimental.pallas import tpu as pltpu
from jax.sharding import PartitionSpec as P

EPSILON = 1e-05
NEGATIVE = -1e30
HEAD = 64
QUERY_HEADS = 15
KEY_HEADS = 5
GROUP = 3
LANES = 128
BLOCK = 256
BF = jnp.bfloat16
F32 = jnp.float32
MESH = pl.DeviceIdType.MESH
VMEM_BYTES = 62 * 2**20


def dot(a, b, contract):
    return lax.dot_general(a, b, ((contract[:1], contract[1:]), ((), ())), preferred_element_type=F32)


def nn(a, b):
    return dot(a, b, (1, 0))


def nt(a, b):
    return dot(a, b, (1, 1))


def tn(a, b):
    return dot(a, b, (0, 0))


def at(start, size):
    return pl.ds(pl.multiple_of(start, size), size)


def loop(count, body, **kw):
    def step(i, _):
        body(i)
        return 0

    lax.fori_loop(0, count, step, 0, **kw)


class Sizes:
    def __init__(self, tokens, width, qkv, heads, hidden, wide):
        self.tokens, self.width = tokens, width
        self.padded = 4 * BLOCK
        self.quarter = width // 4
        self.qkv, self.heads, self.hidden, self.wide = qkv, heads, hidden, wide
        up = lambda v: -(-v // 16) * 16
        self.rows_of = (qkv // wide, heads // wide, hidden // wide, hidden // wide, hidden // wide)
        self.blocks = tuple(up(v) for v in self.rows_of)
        self.starts = tuple(sum(self.blocks[:k]) for k in range(5))
        self.rows = sum(self.blocks)
        self.qkv_padded = -(-qkv // LANES) * LANES
        self.n = wide // 2
        self.group = 640 // self.rows_of[2]


def normalize(z, state, gain_row, out):
    def body(i):
        rows = at(i * 64, 64)
        s = state[rows, :].astype(F32)
        r = lax.rsqrt(jnp.sum(s * s, axis=1, keepdims=True) * (1.0 / z.width) + EPSILON)
        out[rows, :] = (s * r * gain_row).astype(BF)

    loop(z.tokens // 64, body, unroll=True)


def normalize_back(z, state, gain_row, incoming, passed, out, gain_out):
    def body(i):
        rows = at(i * 64, 64)
        s = state[rows, :].astype(F32)
        g = incoming[rows, :]
        r = lax.rsqrt(jnp.sum(s * s, axis=1, keepdims=True) * (1.0 / z.width) + EPSILON)
        n = s * r
        gn = g * n
        c = g * gain_row
        m = jnp.sum(gn * gain_row, axis=1, keepdims=True) * (1.0 / z.width)
        out[rows, :] = passed[rows, :].astype(F32) + r * (c - n * m)
        gain_out[...] += jnp.sum(gn.reshape(8, 8, z.padded), axis=0)

    loop(z.tokens // 64, body, unroll=True)


def half_mask(rows):
    return lax.broadcasted_iota(jnp.int32, (rows, LANES), 1) < HEAD


def swap_pairs(v):
    lane = lax.rem(lax.broadcasted_iota(jnp.int32, v.shape, 1), HEAD)
    return jnp.where(lane < HEAD // 2, pltpu.roll(v, LANES - HEAD // 2, 1), pltpu.roll(v, HEAD // 2, 1))


def project_qkv(z, r):
    half = 5 * LANES
    for start in (0, half, 2 * half):
        size = min(half, z.qkv - start)
        r.qkv[:, start : start + size] = nt(r.normed[...], r.w_qkv[start : start + size, :])

    def body(i):
        rows = at(i * LANES, LANES)
        lo = half_mask(LANES)
        c, s = r.cos[rows, :], r.sin[rows, :]
        zero = jnp.zeros((LANES, LANES), F32)

        def place(target, turned, v, first, second):
            other, across = pltpu.roll(v, HEAD, 1), v.T.astype(BF)
            if first is not None:
                target[0, first, rows, :] = jnp.where(lo, v, zero).astype(BF)
                target[1, first, rows, :] = jnp.where(lo, zero, other).astype(BF)
                turned[first, :, rows] = across[:HEAD]
            if second is not None:
                target[0, second, rows, :] = jnp.where(lo, other, zero).astype(BF)
                target[1, second, rows, :] = jnp.where(lo, zero, v).astype(BF)
                turned[second, :, rows] = across[HEAD:]

        for m in range(10):
            lanes = slice(m * LANES, (m + 1) * LANES)
            v = r.qkv[rows, lanes]
            v = v * c + swap_pairs(v) * s
            if m < 8:
                q = v * HEAD**-0.5
                r.query[rows, lanes] = (q if m < 7 else jnp.where(lo, q, zero)).astype(BF)
            if m >= 7:
                place(r.keys, r.keys_turned, v, None if m == 7 else 2 * m - 15, 2 * m - 14)
        for m in range(3):
            v = r.qkv[rows, (10 + m) * LANES : (11 + m) * LANES]
            place(r.values, r.values_turned, v, 2 * m, 2 * m + 1 if m < 2 else None)

    loop(z.tokens // LANES, body, unroll=True)


def masked(s):
    rows = lax.broadcasted_iota(jnp.int32, s.shape, 0)
    return jnp.where(rows <= lax.broadcasted_iota(jnp.int32, s.shape, 1), s, NEGATIVE)


def attend(z, r, first, count):
    t = z.tokens // 2

    def one(m, parity):
        h = 2 * m + parity
        g = h // GROUP
        cols = at(m * LANES, LANES)
        early, late = r.query[:t, cols], r.query[t:, cols]
        key, value = r.keys.at[parity, g], r.values_turned.at[g]
        a = masked(nt(key[:t, :], early))
        b, c = nt(key[:t, :], late), masked(nt(key[t:, :], late))
        a = jnp.exp(a - jnp.max(a, axis=0, keepdims=True))
        high = jnp.maximum(jnp.max(b, axis=0, keepdims=True), jnp.max(c, axis=0, keepdims=True))
        b, c = jnp.exp(b - high), jnp.exp(c - high)
        a = (a * (1.0 / jnp.sum(a, axis=0, keepdims=True))).astype(BF)
        inverse = 1.0 / (jnp.sum(b, axis=0, keepdims=True) + jnp.sum(c, axis=0, keepdims=True))
        b, c = (b * inverse).astype(BF), (c * inverse).astype(BF)
        r.weights[h, 0], r.weights[h, 1], r.weights[h, 2] = a, b, c
        return nn(value[:, :t], a), nn(value[:, :t], b) + nn(value[:, t:], c)

    def put(m, low, high):
        cols = at(m * LANES, LANES)
        r.heads[:t, cols] = jnp.concatenate([low[0], high[0]], axis=0).T.astype(BF)
        r.heads[t:, cols] = jnp.concatenate([low[1], high[1]], axis=0).T.astype(BF)

    def pair(i):
        put(first + i, one(first + i, 0), one(first + i, 1))

    last = QUERY_HEADS // 2
    loop(min(first + count, last) - first, pair, unroll=True)
    if first + count > last:
        empty = jnp.zeros((HEAD, t), F32)
        put(last, one(last, 0), (empty, empty))


def forward_steps(z, r):
    chunk = r.chunk

    def start():
        normalize(z, r.state, r.gains[0:1, :], r.normed)

    def qkv():
        r.need_qkv()
        project_qkv(z, r)

    def heads(first):
        return lambda: attend(z, r, first, 2)

    def out():
        r.need_out()
        for n in range(2):
            cols = slice(n * 512, (n + 1) * 512)
            r.middle[:, cols] = r.state[:, cols].astype(F32) + nn(r.heads[:, : z.heads], r.w_out[:, cols])
        normalize(z, r.middle, r.gains[1:2, :], r.normed2)

    def gate_up(i):
        cols = at(i * chunk, chunk)
        gate = nt(r.normed2[...], r.gate_block(i))
        up = nt(r.normed2[...], r.up_block(i))
        r.gate[:, cols] = gate.astype(BF)
        r.up[:, cols] = up.astype(BF)
        r.hidden[:, cols] = (gate * jax.nn.sigmoid(gate) * up).astype(BF)

    def ffn():
        r.need_gate()
        loop(z.hidden // chunk, gate_up, unroll=True)

    def some(first, count):
        return lambda: loop(count, lambda i: gate_up(first + i), unroll=True)

    def down():
        r.need_down()
        r.down()

    if r.halves:
        half = z.hidden // chunk // 2
        return [start, qkv, heads(0), heads(2), heads(4), heads(6), out, some(0, half), some(half, half), down]
    return [start, qkv, lambda: attend(z, r, 0, 8), out, ffn, down]


def forward(z, r):
    for step in forward_steps(z, r):
        step()


def attend_back(z, r):
    t = z.tokens // 2
    r.key_grad[...] = jnp.zeros_like(r.key_grad)
    r.value_grad[...] = jnp.zeros_like(r.value_grad)
    first, second = slice(0, t), slice(t, 2 * t)

    def one(m, parity):
        h = 2 * m + parity
        g = h // GROUP
        cols = at(m * LANES, LANES)
        key, value = r.keys_turned.at[g], r.values.at[parity, g]
        d1, d2 = r.heads_grad[first, cols], r.heads_grad[second, cols]
        q1, q2 = r.query[first, cols], r.query[second, cols]
        a, b, c = r.weights[h, 0], r.weights[h, 1], r.weights[h, 2]
        fa, fb, fc = a.astype(F32), b.astype(F32), c.astype(F32)
        ga, gb, gc = nt(value[first, :], d1), nt(value[first, :], d2), nt(value[second, :], d2)
        ta, tb, tc = fa * ga, fb * gb, fc * gc
        da = jnp.sum(ta, axis=0, keepdims=True)
        db = jnp.sum(tb, axis=0, keepdims=True) + jnp.sum(tc, axis=0, keepdims=True)
        sa, sb, sc = (ta - fa * da).astype(BF), (tb - fb * db).astype(BF), (tc - fc * db).astype(BF)
        r.value_grad[parity, g, first, :] += nn(a, d1) + nn(b, d2)
        r.value_grad[parity, g, second, :] += nn(c, d2)
        r.key_grad[parity, g, first, :] += nn(sa, q1) + nn(sb, q2)
        r.key_grad[parity, g, second, :] += nn(sc, q2)
        return nn(key[:, :t], sa), nn(key[:, :t], sb) + nn(key[:, t:], sc)

    def put(m, low, high):
        cols = at(m * LANES, LANES)
        r.query_grad[first, cols] = jnp.concatenate([low[0], high[0]], axis=0).T
        r.query_grad[second, cols] = jnp.concatenate([low[1], high[1]], axis=0).T

    last = QUERY_HEADS // 2
    loop(last, lambda m: put(m, one(m, 0), one(m, 1)), unroll=True)
    empty = jnp.zeros((HEAD, t), F32)
    put(last, one(last, 0), (empty, empty))


def unrotate_qkv(z, r):
    def unrotate(i):
        rows = at(i * 64, 64)
        lo = half_mask(64)
        c, s = r.cos[rows, :], r.sin[rows, :]

        def turn(v):
            return v * c - swap_pairs(v) * s

        def joined(ref, g):
            a, b = ref[0, g, rows, :], ref[1, g, rows, :]
            return jnp.where(lo, a + pltpu.roll(b, HEAD, 1), 0.0), jnp.where(lo, 0.0, b + pltpu.roll(a, HEAD, 1))

        def put(m, v):
            r.qkv_back[rows, m * LANES : (m + 1) * LANES] = v.astype(BF)

        k = [joined(r.key_grad, g) for g in range(KEY_HEADS)]
        v = [joined(r.value_grad, g) for g in range(KEY_HEADS)]
        scale = HEAD**-0.5
        for m in range(7):
            put(m, turn(r.query_grad[rows, m * LANES : (m + 1) * LANES] * scale))
        last = jnp.where(lo, r.query_grad[rows, 7 * LANES : 8 * LANES] * scale, 0.0)
        put(7, turn(last + k[0][1]))
        put(8, turn(k[1][0] + k[2][1]))
        put(9, turn(k[3][0] + k[4][1]))
        put(10, v[0][0] + v[1][1])
        put(11, v[2][0] + v[3][1])
        put(12, v[4][0])

    loop(z.tokens // 64, unrotate, unroll=True)


def backward_steps(z, r):
    ffn_grad = r.ffn_grad

    def rounded():
        def body(i):
            rows = at(i * 64, 64)
            ffn_grad[rows, :] = r.grad[rows, :].astype(BF)

        if r.grad is not ffn_grad:
            loop(z.tokens // 64, body, unroll=True)

    def ffn():
        r.need_down()
        r.need_kept()

        def body(n):
            cols = at(n * 512, 512)
            back = nt(ffn_grad[...], r.w_down[cols, :])
            gate = r.gate[:, cols].astype(F32)
            up = r.up[:, cols].astype(F32)
            s = jax.nn.sigmoid(gate)
            r.gate[:, cols] = (back * up * s * (1.0 + gate * (1.0 - s))).astype(BF)
            r.up[:, cols] = (back * gate * s).astype(BF)

        loop(z.hidden // 512, body, unroll=True)
        r.ffn_done()

    def into():
        r.need_gate()

        def body(n):
            cols = at(n * 512, 512)
            r.normed_grad[:, cols] = nn(r.gate[...], r.w_gate[:, cols]) + nn(r.up[...], r.w_up[:, cols])

        loop(z.padded // 512, body, unroll=True)

    def norm2():
        r.need_middle()
        normalize_back(z, r.middle, r.gains[1:2, :], r.normed_grad, r.grad, r.middle_grad, r.gain_out.at[1])

        def body(i):
            rows = at(i * 64, 64)
            r.attn_back[rows, :] = r.middle_grad[rows, :].astype(BF)

        loop(z.tokens // 64, body, unroll=True)
        r.norm2_done()

    def out():
        r.need_attention()
        r.need_out()
        w = z.heads
        for start, size in ((0, 512), (512, w - 512)):
            cols = slice(start, start + size)
            back = nt(r.attn_back[...], r.w_out[cols, :])
            r.heads_grad[:, cols] = back.astype(BF)
        r.heads_grad[:, w:] = jnp.zeros((z.tokens, z.padded - w), BF)

    def attention():
        attend_back(z, r)
        r.attention_done()

    def unrotate():
        unrotate_qkv(z, r)
        r.unrotate_done()

    def qkv():
        r.need_qkv()
        for n in range(2):
            cols = slice(n * 512, (n + 1) * 512)
            r.normed_grad[:, cols] = nn(r.qkv_back[:, : z.qkv], r.w_qkv[:, cols])

    def norm1():
        normalize_back(z, r.state, r.gains[0:1, :], r.normed_grad, r.middle_grad, r.grad_in, r.gain_out.at[0])

    return [rounded, ffn, into, norm2, out, attention, unrotate, qkv, norm1]


def backward(z, r):
    for step in backward_steps(z, r):
        step()


def kept_shapes(z):
    t, d, f = z.tokens, z.padded, z.hidden
    return dict(
        query=((t, d), BF),
        keys=((2, KEY_HEADS, t, LANES), BF),
        values=((2, KEY_HEADS, t, LANES), BF),
        keys_turned=((KEY_HEADS, HEAD, t), BF),
        weights=((QUERY_HEADS, 3, t // 2, t // 2), BF),
        heads=((t, d), BF),
        middle=((t, d), F32),
        gate=((t, f), BF),
        up=((t, f), BF),
    )


def layer_shapes(z):
    t, d, f = z.tokens, z.padded, z.hidden
    return dict(kept_shapes(z), normed=((t, d), BF), normed2=((t, d), BF), hidden=((t, f), BF), values_turned=((KEY_HEADS, HEAD, t), BF))


def weight_shapes(z):
    d, f = z.padded, z.hidden
    return dict(w_qkv=((z.qkv, d), BF), w_out=((z.heads, d), BF), w_gate=((f, d), BF), w_up=((f, d), BF), w_down=((f, d), BF))


def tables(z):
    t, d = z.tokens, z.padded
    return dict(gains=((2, z.width), F32), cos=((t, LANES), F32), sin=((t, LANES), F32))


def blocks_shape(z):
    return ((2, 2, z.n, 2, z.rows, BLOCK), BF)


def rows_first(z):
    t, d, f = z.tokens, z.padded, z.hidden
    left = dict(qkv_back=((t, z.qkv_padded), BF), heads=((t, d), BF), gate=((t, f), BF), up=((t, f), BF), hidden=((t, f), BF))
    right = dict(normed=((t, d), BF), attn_back=((t, d), BF), normed2=((t, d), BF), ffn_grad=((t, d), BF))
    return left, right


def make_call(name, body, ins, outs, scratch, in_vmem, sems, **params):
    n_in, n_out, n_s = list(ins), list(outs), list(scratch)

    def kernel(*refs):
        a, b, c = len(n_in), len(n_in) + len(n_out), len(n_in) + len(n_out) + len(n_s)
        group = lambda names, part: types.SimpleNamespace(**dict(zip(names, part)))
        body(group(n_in, refs[:a]), group(n_out, refs[a:b]), group(n_s, refs[b:c]), refs[c:])

    spec = lambda n: pl.BlockSpec(memory_space=pltpu.VMEM if n in in_vmem else pl.ANY)
    call = pl.pallas_call(
        kernel,
        out_shape=[jax.ShapeDtypeStruct(*outs[n]) for n in n_out],
        in_specs=[spec(n) for n in n_in],
        out_specs=[spec(n) for n in n_out],
        scratch_shapes=[pltpu.VMEM(*scratch[n]) for n in n_s] + [pltpu.SemaphoreType.DMA(s) for s in sems],
        compiler_params=pltpu.CompilerParams(vmem_limit_bytes=VMEM_BYTES, **params),
        name=name,
    )
    return lambda **vals: dict(zip(n_out, call(*[vals[n] for n in n_in])))


class Copies:
    def __init__(self, sems):
        self.sems, self.used, self.open = sems, 0, {}

    def start(self, src, dst):
        key = self.used
        self.used += 1
        self.open[key] = pltpu.make_async_copy(src, dst, self.sems.at[key])
        self.open[key].start()
        return key

    def wait(self, keys):
        for key in keys:
            if key in self.open:
                self.open.pop(key).wait()

    def later(self, keys):
        return lambda: self.wait(keys)

    def finish(self):
        self.wait(list(self.open))


SMALL = ("gains", "cos", "sin", "tokens")


def pad_into(z, target, source, turned=True):
    target[...] = jnp.zeros(target.shape, target.dtype)
    for q in range(4):
        part = slice(q * z.quarter, (q + 1) * z.quarter)
        value = source[part, :].astype(F32).T.astype(target.dtype) if turned else source[:, part]
        target[:, q * BLOCK : q * BLOCK + z.quarter] = value


def unpad_into(z, target, value, first=0):
    for q in range(value.shape[1] // BLOCK):
        start = (first + q) * z.quarter
        target[start : start + z.quarter, :] = value[:, q * BLOCK : (q + 1) * BLOCK].T[: z.quarter, :]


def middle_kernel(z):
    t, d = z.tokens, z.padded
    kept = kept_shapes(z)
    ins = dict(tables(z), tokens=((t, d), BF), state=((t, d), F32), cotangent=((z.width, t), BF))
    ins.update(gathered=blocks_shape(z), dense_qkv=((z.qkv, d), BF), dense_out=((z.heads, d), BF))
    ins.update({"first_" + n: v for n, v in kept.items()})
    left, right = rows_first(z)
    both = dict(left, **right)
    outs = dict(result=((z.width, t), F32), grad_in=((z.width, t), F32), gain=((8, d), F32))
    outs.update({n + "2": v for n, v in both.items()})
    outs.update({n + "1": both[n] for n in ("qkv_back", "attn_back", "gate", "up", "ffn_grad")})
    scratch = dict(layer_shapes(z), **weight_shapes(z), state=((t, d), F32), grad=((t, d), BF))
    scratch.update(qkv=((t, z.qkv_padded), F32), plain=((z.width, t), F32), gain_out=((2, 8, d), F32), gains=((2, d), F32))
    scratch.update(key_grad=((2, KEY_HEADS, t, LANES), F32), value_grad=((2, KEY_HEADS, t, LANES), F32))

    def body(i, o, s, sems):
        cps = Copies(sems[0])
        state = cps.start(i.state, s.state)
        qkv = cps.start(i.dense_qkv, s.w_qkv)
        pad_into(z, s.gains, i.gains, False)
        s.gain_out[...] = jnp.zeros_like(s.gain_out)
        none = lambda: None
        r = types.SimpleNamespace(**vars(s))
        vars(r).update(cos=i.cos, sin=i.sin, chunk=512, halves=False)
        r.gate_block = lambda n: s.w_gate[at(n * 512, 512), :]
        r.up_block = lambda n: s.w_up[at(n * 512, 512), :]

        def down():
            for n in range(2):
                cols = slice(n * 512, (n + 1) * 512)
                unpad_into(z, s.plain, s.middle[:, cols] + nn(s.hidden[...], s.w_down[:, cols]), 2 * n)

        r.down = down
        cps.wait([state])

        def need_qkv():
            cps.wait([qkv])
            vars(r).update(start_weights(z, cps, i, s))

        r.need_qkv = need_qkv
        forward(z, r)
        sent = dict(plain=cps.start(s.plain, o.result))
        for n, target in (("normed", o.normed2), ("normed2", o.normed22), ("hidden", o.hidden2), ("heads", o.heads2)):
            sent[n] = cps.start(getattr(s, n), target)
        pad_into(z, s.grad, i.cotangent)
        sent["grad"] = cps.start(s.grad, o.ffn_grad2)
        wait = lambda *names: (lambda: cps.wait([sent[n] for n in names]))

        back = types.SimpleNamespace(**vars(r))
        back.qkv_back = s.hidden.at[:, : z.qkv_padded]
        vars(back).update(heads_grad=s.normed2, attn_back=s.normed, normed_grad=s.qkv.at[:, :d], middle_grad=s.middle, query_grad=s.qkv.at[:, :d], grad_in=s.state)
        vars(back).update(ffn_grad=s.grad, need_kept=none, need_middle=wait("normed"), need_attention=wait("normed2"), need_qkv=none)
        loads = {}

        def send(n, source, target):
            sent[n] = cps.start(source, target)

        def load(n):
            loads[n] = cps.start(getattr(i, "first_" + n), getattr(s, n))

        def ffn_done():
            send("gate", s.gate, o.gate2)
            send("up", s.up, o.up2)

        def attention_done():
            wait("gate", "up", "heads", "hidden")()
            for n in ("gate", "up", "heads", "query", "keys", "values", "keys_turned", "weights"):
                load(n)

        back.ffn_done, back.attention_done = ffn_done, attention_done
        back.norm2_done = lambda: send("attn_back", s.normed, o.attn_back2)
        back.unrotate_done = lambda: send("qkv_back", back.qkv_back, o.qkv_back2)
        backward(z, back)
        load("middle")
        wait("grad")()

        first = types.SimpleNamespace(**vars(back))
        vars(first).update(grad=s.state, state=s.grad)
        first.need_kept = cps.later([loads["gate"], loads["up"]])
        first.need_middle = lambda: (cps.wait([loads["middle"]]), wait("attn_back")())
        first.need_attention = cps.later([loads[n] for n in ("heads", "query", "keys", "values", "keys_turned", "weights")])

        def ffn_done1():
            cps.start(s.gate, o.gate1)
            cps.start(s.up, o.up1)
            send("grad", s.grad, o.ffn_grad1)

        def attention_done1():
            wait("grad", "qkv_back")()
            send("tokens", i.tokens, s.grad)

        first.ffn_done, first.attention_done = ffn_done1, attention_done1
        first.norm2_done = lambda: send("attn_back", s.normed, o.attn_back1)
        first.unrotate_done = lambda: send("qkv_back", back.qkv_back, o.qkv_back1)
        first.need_qkv = lambda: wait("tokens")()
        backward(z, first)
        wait("plain")()
        unpad_into(z, s.plain, s.state[...])
        cps.start(s.plain, o.grad_in)
        o.gain[...] = jnp.zeros_like(o.gain)
        o.gain[0:1, :] = jnp.sum(s.gain_out[0], axis=0, keepdims=True)
        o.gain[1:2, :] = jnp.sum(s.gain_out[1], axis=0, keepdims=True)
        cps.finish()

    return make_call("second_layer", body, ins, outs, scratch, ("gains", "cos", "sin", "cotangent", "gain"), [(80,)])


def start_weights(z, cps, i, s):
    def blocks(w, k):
        w = w.reshape(z.n, 2, z.blocks[k], z.padded)
        rows = pl.ds(z.starts[k], z.blocks[k])
        return [cps.start(i.gathered.at[q // 2, q % 2, :, :, rows], w.at[:, :, :, q * BLOCK : (q + 1) * BLOCK]) for q in range(4)]

    out = [cps.start(i.dense_out, s.w_out)]
    gate = blocks(s.w_gate, 2) + blocks(s.w_up, 3)
    down = blocks(s.w_down, 4)
    return dict(need_out=cps.later(out), need_gate=cps.later(gate), need_down=cps.later(down))


class Place:
    def __init__(self, n):
        mp, w = lax.axis_index("mp"), lax.axis_index("wide")
        self.n = n
        self.x, self.y, self.c, self.z = lax.rem(mp, 2), mp // 2, lax.rem(w, 2), w // 2
        self.axes = ["y", "x"] + z_orders(n)

    def coordinate(self, axis):
        if axis[0] == "z":
            return lax.rem(self.z // 2 ** int(axis[1:]), 2)
        return getattr(self, axis)

    def partner(self, axis):
        away = 1 - 2 * self.coordinate(axis)
        x, y, c, z = self.x, self.y, self.c, self.z
        if axis == "x":
            x = x + away
        elif axis == "y":
            y = y + away
        elif axis == "c":
            c = c + away
        else:
            z = z + away * 2 ** int(axis[1:])
        return {"mp": y * 2 + x, "wide": z * 2 + c}

    def dev(self, z):
        return {"mp": self.y * 2 + self.x, "wide": z * 2 + self.c}

    def signal(self, device):
        pl.semaphore_signal(pltpu.get_barrier_semaphore(), inc=1, device_id=device, device_id_type=MESH)

    def greet_line(self):
        for axis in "xyc":
            self.signal(self.partner(axis))

        @pl.when(self.z > 0)
        def _():
            self.signal(self.dev(self.z - 1))

        @pl.when(self.z < self.n - 1)
        def _():
            self.signal(self.dev(self.z + 1))

    def met_line(self):
        count = 3 + jnp.where(self.z > 0, 1, 0) + jnp.where(self.z < self.n - 1, 1, 0)
        pl.semaphore_wait(pltpu.get_barrier_semaphore(), count)

    def greet(self):
        for axis in self.axes + ["c"]:
            self.signal(self.partner(axis))

    def met(self):
        pl.semaphore_wait(pltpu.get_barrier_semaphore(), len(self.axes) + 1)


def run_stages(entries):
    for entry in sorted(entries, key=lambda e: e[:2]):
        entry[2]()


def shares(units, weights):
    out, done, used = [], 0, 0
    for w in weights:
        done += w
        end = round(units * done / sum(weights))
        out.append(end - used)
        used = end
    return out


def row_chunks(start, rows, parts, orders, first=0):
    out, r = [], start
    for k, units in enumerate(shares(rows // 16, parts)):
        turn = orders[(first + k) % len(orders)]
        for order, u in zip(turn, shares(units, [1] * len(turn))):
            if u:
                out.append((r, 16 * u, order, k))
                r += 16 * u
    return out


GATHER_ORDERS = (("xzy", "yzx"), ("zxy", "zyx"), ("yzx", "xzy"))
GATHER_PARTS = (1,) * 10
GATHER_TIMES = ((-1.44, 0.95, 2.47, 0.87, 0.01, 0.95, 1.6), (-4.28, -0.02, 0.47, 0.69, 1.14, 2.95, 4.2))
STEP_GAP = 0.7


def along(p, axes, free, turned, rows):
    mine = [p.coordinate(a) for a in axes]
    return tuple(slice(None) if a in free else 1 - v if a == turned else v for a, v in zip(axes, mine)) + rows


def gather_plan(p, g, k, piece, ss, rs):
    r0, rc, order, _ = piece
    n, rows = p.n, pl.ds(r0, rc)
    a1, a2 = [a for a in order if a != "z"]
    z_first = order[0] == "z"

    def one(zo, other=False):
        x = 1 - p.x if other and a1 == "x" else p.x
        y = 1 - p.y if other and a1 == "y" else p.y
        return g.at[y, x, zo, p.c, rows]

    def pair(zo, other=False, c=None):
        c = p.c if c is None else c
        if a1 == "x":
            return g.at[1 - p.y if other else p.y, :, zo, c, rows]
        return g.at[:, 1 - p.x if other else p.x, zo, c, rows]

    def copy(ref, dev, s, r):
        return pltpu.make_async_remote_copy(src_ref=ref, dst_ref=ref, send_sem=ss.at[k, s], recv_sem=rs.at[k, r], device_id=dev, device_id_type=MESH)

    along = one if z_first else pair
    up = lambda zo: copy(along(zo), p.dev(p.z + 1), zo, zo)
    down = lambda zo: copy(along(zo), p.dev(p.z - 1), n + zo, zo)
    line_in = lambda zo: copy(along(zo), p.partner("c"), zo, zo)
    first = lambda zo, other=False: copy(one(zo, other), p.partner(a1), 2 * n + zo, n + zo)
    second = lambda zo, other=False: copy(pair(zo, other), p.partner(a2), 3 * n + zo, 2 * n + zo)

    def sibling(other, c=None):
        c = p.c if c is None else c
        if a1 == "x":
            part = g.at[1 - p.y if other else p.y, :, :, c, rows]
        else:
            part = g.at[:, 1 - p.x if other else p.x, :, c, rows]
        o = 1 if other else 0
        return copy(part, p.partner("c"), 4 * n + o, 3 * n + o)

    def line(zo):
        @pl.when((zo <= p.z) & (p.z < n - 1))
        def _():
            up(zo).start()

        @pl.when((zo >= p.z) & (p.z > 0))
        def _():
            down(zo).start()

    def at_distance(d, body):
        @pl.when(p.z - d >= 0)
        def _():
            body(p.z - d)

        @pl.when(p.z + d < n)
        def _():
            body(p.z + d)

    stages = []
    times = GATHER_TIMES[1 if z_first else 0]
    hop_time, step = times[1:3] if z_first else times[2:4]
    last_hop = hop_time + (n - 2) * step
    if z_first:

        def start():
            line(p.z)
            first(p.z).start()

        stages.append((times[0], start))
        for d in range(1, n):

            def hop(d=d):
                def body(zo):
                    line_in(zo).wait_recv()
                    line(zo)
                    first(zo).start()

                at_distance(d, body)

            stages.append((hop_time + (d - 1) * step, hop))

        def cross():
            for zo in range(n):
                first(zo, True).wait_recv()
                second(zo).start()

        stages.append((last_hop + times[3], cross))
    else:

        def start():
            first(p.z).start()

        def meet():
            first(p.z, True).wait_recv()
            line(p.z)
            second(p.z).start()

        stages += [(times[0], start), (times[1], meet)]
        for d in range(1, n):

            def hop(d=d):
                def body(zo):
                    line_in(zo).wait_recv()
                    line(zo)
                    second(zo).start()

                at_distance(d, body)

            stages.append((hop_time + (d - 1) * step, hop))

    def halfway():
        sibling(False).start()

    def arrived():
        for zo in range(n):
            second(zo, True).wait_recv()
        sibling(True).start()

    def done():
        sibling(False, 1 - p.c).wait_recv()
        sibling(True, 1 - p.c).wait_recv()

    def drain():
        for zo in range(n):

            @pl.when((zo <= p.z) & (p.z < n - 1))
            def _():
                up(zo).wait_send()

            @pl.when((zo >= p.z) & (p.z > 0))
            def _():
                down(zo).wait_send()

            second(zo).wait_send()
            if z_first:
                first(zo).wait_send()
        if not z_first:
            first(p.z).wait_send()
        sibling(False).wait_send()
        sibling(True).wait_send()

    return stages + [(last_hop + at_time, f) for at_time, f in zip(times[-3:], (halfway, arrived, done))], drain


def stage_times(table, count):
    more = count - len(table)
    return list(table[:-2]) + [table[-3] + 1 + k for k in range(more)] + [v + more for v in table[-2:]]


def first_kernel(z):
    t, d, n = z.tokens, z.padded, z.n
    pieces = row_chunks(0, z.rows, GATHER_PARTS, GATHER_ORDERS)
    layer = layer_shapes(z)
    shards = weight_shards(z, BF)
    ins = dict(tables(z), tokens=((z.width, t), BF), **shards)
    outs = dict({m: v for m, v in layer.items() if m != "values_turned"}, start=((t, d), BF), result=((t, d), F32), gathered=blocks_shape(z), dense_qkv=((z.qkv, d), BF), dense_out=((z.heads, d), BF))
    scratch = dict(layer, result=((t, d), F32), qkv=((t, z.qkv_padded), F32), blocks=blocks_shape(z))
    scratch.update(w_qkv=((z.qkv, d), BF), w_out=((z.heads, d), BF), start=((t, d), BF), gains=((2, d), F32))

    def body(i, o, s, sems):
        local, ss, rs = sems
        cps = Copies(local)
        p = Place(n)
        p.greet_line()
        for k, name in enumerate(shards):
            w = getattr(i, name)[...]
            rows = z.starts[k]
            s.blocks[p.y, p.x, p.z, p.c, rows : rows + z.blocks[k], :] = jnp.zeros((z.blocks[k], BLOCK), BF)
            s.blocks[p.y, p.x, p.z, p.c, rows : rows + z.rows_of[k], : z.quarter] = w
        p.met_line()

        def dense(k, target):
            per = z.rows_of[k]
            for j in range(z.wide):
                for q in range(4):
                    rows = s.blocks[q // 2, q % 2, j // 2, j % 2, z.starts[k] : z.starts[k] + per, :]
                    target[j * per : (j + 1) * per, q * BLOCK : (q + 1) * BLOCK] = rows

        def block(k):
            start, per, some = z.starts[k], z.rows_of[k], z.group // 2

            def read(j):
                rows = []
                for e in range(z.group):
                    quarters = [s.blocks[q // 2, q % 2, j * some + e // 2, e % 2, start : start + per, :] for q in range(4)]
                    rows.append(jnp.concatenate(quarters, axis=1))
                return jnp.concatenate(rows, axis=0)

            return read

        none = lambda: None
        r = types.SimpleNamespace(**vars(s))
        vars(r).update(cos=i.cos, sin=i.sin, state=s.start, chunk=640, halves=True)
        vars(r).update(gate_block=block(2), up_block=block(3), need_gate=none, need_down=none)

        def need_qkv():
            dense(0, s.w_qkv)
            cps.start(s.w_qkv, o.dense_qkv)

        def need_out():
            dense(1, s.w_out)
            cps.start(s.w_out, o.dense_out)

        def down():
            read = block(4)
            s.result[...] = s.middle[...]

            def add(j):
                s.result[...] += nn(s.hidden[:, at(j * 640, 640)], read(j))

            loop(z.hidden // 640, add)

        vars(r).update(need_qkv=need_qkv, need_out=need_out, down=down)
        steps = forward_steps(z, r)

        def begin():
            pad_into(z, s.gains, i.gains, False)
            pad_into(z, s.start, i.tokens)
            cps.start(s.start, o.start)
            forward_start()

        forward_start, steps[0] = steps[0], begin
        plans = [gather_plan(p, s.blocks, k, piece, ss, rs) for k, piece in enumerate(pieces)]
        entries = [(pieces[k][3] + at_time, k, f) for k, (stages, _) in enumerate(plans) for at_time, f in stages]
        done = [pieces[k][3] + stages[-1][0] for k, (stages, _) in enumerate(plans)]
        ready = [max(at_time for at_time, piece in zip(done, pieces) if piece[0] < e) for e in (z.starts + (z.rows,))[1:]]
        times = [0.5]
        for k in (0, 0, 0, 0, 0, 1, 3, 3, 4):
            times.append(max(ready[k] + 0.5, times[-1] + STEP_GAP))
        entries += [(at_time, -1, f) for at_time, f in zip(times, steps)]

        def out_of(part):
            rows = [p for p in pieces if p[3] == part]
            span = pl.ds(rows[0][0], sum(p[1] for p in rows))
            return lambda: cps.start(s.blocks.at[:, :, :, :, span], o.gathered.at[:, :, :, :, span])

        for part in range(len(GATHER_PARTS)):
            entries.append((max(at_time for at_time, piece in zip(done, pieces) if piece[3] == part), 100 + part, out_of(part)))

        def keep(*names):
            return lambda: [cps.start(getattr(s, m), getattr(o, m)) for m in names]

        def keep_half(k):
            cols = slice(k * z.hidden // 2, (k + 1) * z.hidden // 2)
            return lambda: [cps.start(getattr(s, m).at[:, cols], getattr(o, m).at[:, cols]) for m in ("gate", "up", "hidden")]

        entries += [(times[5], 0, keep("normed", "query", "keys", "values", "keys_turned", "weights", "heads"))]
        entries += [(times[6], 0, keep("middle", "normed2")), (times[7], 0, keep_half(0)), (times[8], 0, keep_half(1))]
        run_stages(entries)
        cps.start(s.result, o.result)
        for _, drain in plans:
            drain()
        cps.finish()

    sems = [(40,), (len(pieces), 4 * n + 2), (len(pieces), 3 * n + 2)]
    return make_call("first_layer", body, ins, outs, scratch, SMALL + tuple(shards), sems, collective_id=1, has_side_effects=True)


def z_orders(n):
    return ["z%d" % k for k in reversed(range(n.bit_length() - 1))]


def reduce_orders(n):
    z = z_orders(n)[::-1]
    half = len(z) // 2
    first, second = [(b,) + tuple(z[:half]) + (a,) + tuple(z[half:]) for a, b in ("xy", "yx")]
    return ((first, second), (second, first))


REDUCE_WEIGHTS = (1, 4, 0, 2, 3)
REDUCE_PARTS = (2, 1, 3, 3, 3)
REDUCE_TIMES = (0.8, 2.4, 4.2, 6.0, 8.0)
WORK_LEAD, WORK_STEP = 0.77, 0.146


def weight_shards(z, kind):
    names = ("w_qkv_shard", "w_out_shard", "w_gate_shard", "w_up_shard", "w_down_shard")
    return {name: ((rows, z.quarter), kind) for name, rows in zip(names, z.rows_of)}


def add_into(target, extra):
    target[...] = target[...] + extra[...].astype(target.dtype)


def reduce_plan(p, t, from_sibling, bufs, out, k, piece, ss, rs):
    r0, rc, order, _ = piece
    axes, last = p.axes, len(order) - 1
    rows = pl.ds(r0, rc)

    def part(ref, s, other):
        return ref.at[along(p, axes, order[s + 1 :], order[s] if other else None, (rows,))]

    def step(s):
        return pltpu.make_async_remote_copy(
            src_ref=part(t, s, True),
            dst_ref=bufs[s].at[(slice(None),) * (last - s) + (rows,)],
            send_sem=ss.at[k, s],
            recv_sem=rs.at[k, s],
            device_id=p.partner(order[s]),
            device_id_type=MESH,
        )

    def meet():
        add_into(part(t, 0, True), part(from_sibling, 0, True))
        step(0).start()
        add_into(part(t, 0, False), part(from_sibling, 0, False))

    def follow(s):
        step(s - 1).wait_recv()
        left = [a for a in axes if a in order[s:]]
        for other in (True, False):
            side = 1 - p.coordinate(order[s]) if other else p.coordinate(order[s])
            index = tuple(side if a == order[s] else slice(None) for a in left) + (rows,)
            add_into(part(t, s, other), bufs[s - 1].at[index])
            if other:
                step(s).start()

    def finish():
        step(last).wait_recv()
        out[rows, :] = part(t, last, False)[...].astype(F32) + bufs[last][rows, :].astype(F32)

    def drain():
        for s in range(last + 1):
            step(s).wait_send()

    return [meet] + [functools.partial(follow, s) for s in range(1, last + 1)] + [finish], drain


def last_kernel(z):
    t, d, n = z.tokens, z.padded, z.n
    left, right = rows_first(z)
    both = dict(left, **right)
    ins = {m + k: v for m, v in both.items() for k in "12"}
    ins.update(gain=((8, d), F32))
    outs = dict(sums=((z.rows, BLOCK), F32), gain_sums=((8, d), F32))
    two = lambda v: ((2 * t, v[0][1]), BF)
    scratch = {m: two(v) for m, v in both.items() if m not in ("gate", "up")}
    stage = max(z.rows_of)
    scratch.update(
        t=((2, 2, n, z.rows, BLOCK), BF),
        staged=((STAGED, 2, 2, stage, BLOCK), BF),
        from_sibling=((2, 2, n, z.rows, BLOCK), BF),
        gain_sent=((n.bit_length() + 2, 8, d), F32),
        gain_in=((n.bit_length() + 2, 8, d), F32),
    )
    pairs = 2 + n.bit_length() - 1
    for k in range(pairs):
        scratch["step%d" % k] = ((2,) * (pairs - 1 - k) + (z.rows, BLOCK), BF)
    order, parts = REDUCE_WEIGHTS, REDUCE_PARTS
    pieces, starts = [], {}
    slot = 1
    for k in order:
        starts[k] = slot
        for r0, rc, way, part in row_chunks(z.starts[k], z.blocks[k], (1,) * parts[k], reduce_orders(n), slot):
            pieces.append((r0, rc, way, slot + part, k))
        slot += parts[k]

    def body(i, o, s, sems):
        local, ss, rs, sib_s, sib_r, gain_s, gain_r = sems
        cps = Copies(local)
        need = {}

        names = (("qkv_back", "normed"), ("heads", "attn_back"), ("gate", "normed2"), ("up", "normed2"), ("hidden", "ffn_grad"))
        in_hidden = ("hidden", "gate", "up")

        def load(k):
            for m in names[k]:
                if m not in need:
                    target = s.hidden if m in in_hidden else getattr(s, m)
                    need[m] = cps.later([cps.start(getattr(i, m + a), target.at[pl.ds((2 - int(a)) * t, t)]) for a in "12"])

        load(order[0])
        p = Place(n)
        p.greet()
        count = [0]

        def sibling(k, zo, slot):
            rows = pl.ds(z.starts[k], z.blocks[k])
            return pltpu.make_async_remote_copy(
                src_ref=s.staged.at[slot, :, :, pl.ds(0, z.blocks[k])],
                dst_ref=s.from_sibling.at[:, :, zo, rows],
                send_sem=sib_s.at[slot],
                recv_sem=sib_r.at[k, zo],
                device_id=p.partner("c"),
                device_id_type=MESH,
            )

        sent = {}

        def put(k, zo, slot, a, b):
            per = z.rows_of[k]
            own, other = jnp.where(p.c == 0, a, b).astype(BF), jnp.where(p.c == 0, b, a).astype(BF)
            for q in range(4):
                lanes = slice(q * BLOCK, (q + 1) * BLOCK)
                s.t[q // 2, q % 2, zo, z.starts[k] : z.starts[k] + per, :] = own[:, lanes]
                s.staged[slot, q // 2, q % 2, :per, :] = other[:, lanes]

        some = [1, 1] + [z.group // 2] * 3

        def work(k, first):
            per = z.rows_of[k]

            def run():
                if first == 0:
                    load(k)
                    for m in names[k]:
                        need[m]()
                    after = order[order.index(k) + 1 :][:1]
                    if after and not (names[k][0] in in_hidden and names[after[0]][0] in in_hidden):
                        load(after[0])
                m_left = (s.qkv_back, s.heads, s.hidden, s.hidden, s.hidden)[k]
                m_right = (s.normed, s.attn_back, s.normed2, s.normed2, s.ffn_grad)[k]
                width = 2 * per * some[k]
                value = tn(m_left[:, first * 2 * per : first * 2 * per + width], m_right[...])
                for e in range(some[k]):
                    zo = first + e
                    slot = count[0] % STAGED
                    if slot in sent:
                        sent.pop(slot).wait_send()
                    count[0] += 1
                    put(k, zo, slot, value[2 * e * per : (2 * e + 1) * per], value[(2 * e + 1) * per : (2 * e + 2) * per])
                    if count[0] == 1:
                        p.met()
                    sent[slot] = sibling(k, zo, slot)
                    sent[slot].start()

            return run

        latest = REDUCE_TIMES[0] - 0.01
        entries = []
        for k in order:
            for first in range(0, n, some[k]):
                at_time = starts[k] + min(first * 4 / n * WORK_STEP * parts[k] - WORK_LEAD, latest)
                entries.append((at_time, -1, work(k, first)))
        met = set()

        def after_sibling(k, f):
            def run():
                if k not in met:
                    met.add(k)
                    for zo in range(n):
                        sibling(k, zo, 0).wait_recv()
                f()

            return run

        cube = lambda ref: ref.reshape((2,) * pairs + (z.rows, BLOCK))
        bufs = [getattr(s, "step%d" % k) for k in range(pairs)]
        plans = [reduce_plan(p, cube(s.t), cube(s.from_sibling), bufs, o.sums, k, piece[:4], ss, rs) for k, piece in enumerate(pieces)]
        when = stage_times(REDUCE_TIMES, pairs + 1)
        for k, (stages, _) in enumerate(plans):
            stages[0] = after_sibling(pieces[k][4], stages[0])
        entries += [(pieces[k][3] + at_time, k, f) for k, (stages, _) in enumerate(plans) for at_time, f in zip(when, stages)]
        stages, gains_drain = gain_plan(p, i.gain, s, o.gain_sums, gain_s, gain_r)
        entries += [(1 + k, 100, f) for k, f in enumerate(stages)]
        run_stages(entries)
        for _, drain in plans:
            drain()
        for c in sent.values():
            c.wait_send()
        gains_drain()
        cps.finish()

    sems = [(40,), (len(pieces), pairs), (len(pieces), pairs), (STAGED,), (5, n), (pairs + 1,), (pairs + 1,)]
    return make_call("gradients", body, ins, outs, scratch, ("gain", "sums", "gain_sums"), sems, collective_id=2, has_side_effects=True)


STAGED = 4


def gain_plan(p, mine, s, out, ss, rs):
    axes = ["c"] + p.axes

    def exchange(k):
        return pltpu.make_async_remote_copy(
            src_ref=s.gain_sent.at[k], dst_ref=s.gain_in.at[k], send_sem=ss.at[k], recv_sem=rs.at[k], device_id=p.partner(axes[k]), device_id_type=MESH
        )

    def begin():
        s.gain_sent[0] = mine[...]
        exchange(0).start()

    def step(k):
        exchange(k).wait_recv()
        total = s.gain_sent[k] + s.gain_in[k]
        if k + 1 < len(axes):
            s.gain_sent[k + 1] = total
            exchange(k + 1).start()
        else:
            out[...] = total

    def drain():
        for k in range(len(axes)):
            exchange(k).wait_send()

    return [begin] + [functools.partial(step, k) for k in range(len(axes))], drain


def unpack_kernel(z):
    shards = weight_shards(z, F32)
    ins = dict(sums=((z.rows, BLOCK), F32), gain_sums=((8, z.padded), F32))
    outs = dict(shards, gain_grads=((2, z.width), F32))

    def body(i, o, s, sems):
        for k, name in enumerate(shards):
            getattr(o, name)[...] = i.sums[z.starts[k] : z.starts[k] + z.rows_of[k], : z.quarter]
        for q in range(4):
            o.gain_grads[:, q * z.quarter : (q + 1) * z.quarter] = i.gain_sums[:2, q * BLOCK : q * BLOCK + z.quarter]

    return make_call("unpack", body, ins, outs, {}, tuple(ins) + tuple(outs), [])


def rotary_tables(count_of_rows):
    position = np.arange(count_of_rows, dtype=np.float32)
    inverse = np.exp(np.arange(HEAD // 2, dtype=np.float32) * np.float32(-2.0 * math.log(10000.0) / HEAD))
    angle = position[:, None] * inverse[None, :]
    cos, sin = np.cos(angle), np.sin(angle)
    return np.concatenate([cos] * 4, axis=1), np.concatenate([-sin, sin] * 2, axis=1)


def local(wide, tokens, cotangent, norm_gains, w_qkv, w_out, w_gate, w_up, w_down):
    z = Sizes(tokens.shape[0], tokens.shape[1], w_qkv.shape[1] * wide, w_out.shape[0] * wide, w_gate.shape[1] * wide, wide)
    cos, sin = rotary_tables(z.tokens)
    small = dict(gains=norm_gains, cos=jnp.asarray(cos), sin=jnp.asarray(sin))
    shards = dict(zip(weight_shards(z, BF), (w_qkv.T, w_out, w_gate.T, w_up.T, w_down)))
    one = first_kernel(z)(tokens=tokens.T, **small, **shards)
    kept = {"first_" + n: one[n] for n in kept_shapes(z)}
    weights = {n: one[n] for n in ("gathered", "dense_qkv", "dense_out")}
    two = middle_kernel(z)(tokens=one["start"], state=one["result"], cotangent=cotangent.T, **small, **kept, **weights)
    factors = {n + "1": one[n] for n in ("normed", "normed2", "heads", "hidden")}
    out = unpack_kernel(z)(**last_kernel(z)(**factors, **two))
    grads = [out[n] for n in weight_shards(z, F32)]
    return (two["result"].T, two["grad_in"].T, out["gain_grads"], grads[0].T, grads[1], grads[2].T, grads[3].T, grads[4])


def solution(mesh):
    return jax.shard_map(
        functools.partial(local, mesh.shape["wide"]),
        mesh=mesh,
        in_specs=(
            P(("mp", "wide"), None),
            P(("mp", "wide"), None),
            P(),
            P("mp", "wide"),
            P("wide", "mp"),
            P("mp", "wide"),
            P("mp", "wide"),
            P("wide", "mp"),
        ),
        out_specs=(
            P(("mp", "wide"), None),
            P(("mp", "wide"), None),
            P(),
            P("mp", "wide"),
            P("wide", "mp"),
            P("mp", "wide"),
            P("mp", "wide"),
            P("wide", "mp"),
        ),
        check_vma=False,
    )
```

```python
import functools
import math
import types

import jax
import jax.numpy as jnp
import numpy as np
from jax import lax
from jax.experimental import pallas as pl
from jax.experimental.pallas import tpu as pltpu
from jax.sharding import PartitionSpec as P

EPSILON = 1e-05
NEGATIVE = -1e30
HEAD = 64
QUERY_HEADS = 15
KEY_HEADS = 5
GROUP = 3
LANES = 128
BLOCK = 256
BF = jnp.bfloat16
F32 = jnp.float32
MESH = pl.DeviceIdType.MESH
VMEM_BYTES = 62 * 2**20


def dot(a, b, contract):
    return lax.dot_general(a, b, ((contract[:1], contract[1:]), ((), ())), preferred_element_type=F32)


def nn(a, b):
    return dot(a, b, (1, 0))


def nt(a, b):
    return dot(a, b, (1, 1))


def tn(a, b):
    return dot(a, b, (0, 0))


def at(start, size):
    return pl.ds(pl.multiple_of(start, size), size)


def loop(count, body, **kw):
    def step(i, _):
        body(i)
        return 0

    lax.fori_loop(0, count, step, 0, **kw)


class Sizes:
    def __init__(self, tokens, width, qkv, heads, hidden, wide):
        self.tokens, self.width = tokens, width
        self.padded = 4 * BLOCK
        self.quarter = width // 4
        self.qkv, self.heads, self.hidden, self.wide = qkv, heads, hidden, wide
        up = lambda v: -(-v // 16) * 16
        self.rows_of = (qkv // wide, heads // wide, hidden // wide, hidden // wide, hidden // wide)
        self.blocks = tuple(up(v) for v in self.rows_of)
        self.starts = tuple(sum(self.blocks[:k]) for k in range(5))
        self.rows = sum(self.blocks)
        self.qkv_padded = -(-qkv // LANES) * LANES
        self.n = wide // 2
        self.group = 640 // self.rows_of[2]


def normalize(z, state, gain_row, out):
    def body(i):
        rows = at(i * 64, 64)
        s = state[rows, :].astype(F32)
        r = lax.rsqrt(jnp.sum(s * s, axis=1, keepdims=True) * (1.0 / z.width) + EPSILON)
        out[rows, :] = (s * r * gain_row).astype(BF)

    loop(z.tokens // 64, body, unroll=True)


def normalize_back(z, state, gain_row, incoming, passed, out, gain_out):
    def body(i):
        rows = at(i * 64, 64)
        s = state[rows, :].astype(F32)
        g = incoming[rows, :]
        r = lax.rsqrt(jnp.sum(s * s, axis=1, keepdims=True) * (1.0 / z.width) + EPSILON)
        n = s * r
        gn = g * n
        c = g * gain_row
        m = jnp.sum(gn * gain_row, axis=1, keepdims=True) * (1.0 / z.width)
        out[rows, :] = passed[rows, :].astype(F32) + r * (c - n * m)
        gain_out[...] += jnp.sum(gn.reshape(8, 8, z.padded), axis=0)

    loop(z.tokens // 64, body, unroll=True)


def half_mask(rows):
    return lax.broadcasted_iota(jnp.int32, (rows, LANES), 1) < HEAD


def swap_pairs(v):
    lane = lax.rem(lax.broadcasted_iota(jnp.int32, v.shape, 1), HEAD)
    return jnp.where(lane < HEAD // 2, pltpu.roll(v, LANES - HEAD // 2, 1), pltpu.roll(v, HEAD // 2, 1))


def project_qkv(z, r):
    half = 5 * LANES
    for start in (0, half, 2 * half):
        size = min(half, z.qkv - start)
        r.qkv[:, start : start + size] = nt(r.normed[...], r.w_qkv[start : start + size, :])

    def body(i):
        rows = at(i * LANES, LANES)
        lo = half_mask(LANES)
        c, s = r.cos[rows, :], r.sin[rows, :]
        zero = jnp.zeros((LANES, LANES), F32)

        def place(target, turned, v, first, second):
            other, across = pltpu.roll(v, HEAD, 1), v.T.astype(BF)
            if first is not None:
                target[0, first, rows, :] = jnp.where(lo, v, zero).astype(BF)
                target[1, first, rows, :] = jnp.where(lo, zero, other).astype(BF)
                turned[first, :, rows] = across[:HEAD]
            if second is not None:
                target[0, second, rows, :] = jnp.where(lo, other, zero).astype(BF)
                target[1, second, rows, :] = jnp.where(lo, zero, v).astype(BF)
                turned[second, :, rows] = across[HEAD:]

        for m in range(10):
            lanes = slice(m * LANES, (m + 1) * LANES)
            v = r.qkv[rows, lanes]
            v = v * c + swap_pairs(v) * s
            if m < 8:
                q = v * HEAD**-0.5
                r.query[rows, lanes] = (q if m < 7 else jnp.where(lo, q, zero)).astype(BF)
            if m >= 7:
                place(r.keys, r.keys_turned, v, None if m == 7 else 2 * m - 15, 2 * m - 14)
        for m in range(3):
            v = r.qkv[rows, (10 + m) * LANES : (11 + m) * LANES]
            place(r.values, r.values_turned, v, 2 * m, 2 * m + 1 if m < 2 else None)

    loop(z.tokens // LANES, body, unroll=True)


def masked(s):
    rows = lax.broadcasted_iota(jnp.int32, s.shape, 0)
    return jnp.where(rows <= lax.broadcasted_iota(jnp.int32, s.shape, 1), s, NEGATIVE)


def attend(z, r, first, count):
    t = z.tokens // 2

    def one(m, parity):
        h = 2 * m + parity
        g = h // GROUP
        cols = at(m * LANES, LANES)
        early, late = r.query[:t, cols], r.query[t:, cols]
        key, value = r.keys.at[parity, g], r.values_turned.at[g]
        a = masked(nt(key[:t, :], early))
        b, c = nt(key[:t, :], late), masked(nt(key[t:, :], late))
        a = jnp.exp(a - jnp.max(a, axis=0, keepdims=True))
        high = jnp.maximum(jnp.max(b, axis=0, keepdims=True), jnp.max(c, axis=0, keepdims=True))
        b, c = jnp.exp(b - high), jnp.exp(c - high)
        a = (a * (1.0 / jnp.sum(a, axis=0, keepdims=True))).astype(BF)
        inverse = 1.0 / (jnp.sum(b, axis=0, keepdims=True) + jnp.sum(c, axis=0, keepdims=True))
        b, c = (b * inverse).astype(BF), (c * inverse).astype(BF)
        r.weights[h, 0], r.weights[h, 1], r.weights[h, 2] = a, b, c
        return nn(value[:, :t], a), nn(value[:, :t], b) + nn(value[:, t:], c)

    def put(m, low, high):
        cols = at(m * LANES, LANES)
        r.heads[:t, cols] = jnp.concatenate([low[0], high[0]], axis=0).T.astype(BF)
        r.heads[t:, cols] = jnp.concatenate([low[1], high[1]], axis=0).T.astype(BF)

    def pair(i):
        put(first + i, one(first + i, 0), one(first + i, 1))

    last = QUERY_HEADS // 2
    loop(min(first + count, last) - first, pair, unroll=True)
    if first + count > last:
        empty = jnp.zeros((HEAD, t), F32)
        put(last, one(last, 0), (empty, empty))


def forward_steps(z, r):
    chunk = r.chunk

    def start():
        normalize(z, r.state, r.gains[0:1, :], r.normed)

    def qkv():
        r.need_qkv()
        project_qkv(z, r)

    def heads(first):
        return lambda: attend(z, r, first, 2)

    def out():
        r.need_out()
        for n in range(2):
            cols = slice(n * 512, (n + 1) * 512)
            r.middle[:, cols] = r.state[:, cols].astype(F32) + nn(r.heads[:, : z.heads], r.w_out[:, cols])
        normalize(z, r.middle, r.gains[1:2, :], r.normed2)

    def gate_up(i):
        cols = at(i * chunk, chunk)
        gate = nt(r.normed2[...], r.gate_block(i))
        up = nt(r.normed2[...], r.up_block(i))
        r.gate[:, cols] = gate.astype(BF)
        r.up[:, cols] = up.astype(BF)
        r.hidden[:, cols] = (gate * jax.nn.sigmoid(gate) * up).astype(BF)

    def ffn():
        r.need_gate()
        loop(z.hidden // chunk, gate_up, unroll=True)

    def some(first, count):
        return lambda: loop(count, lambda i: gate_up(first + i), unroll=True)

    def down():
        r.need_down()
        r.down()

    if r.halves:
        half = z.hidden // chunk // 2
        return [start, qkv, heads(0), heads(2), heads(4), heads(6), out, some(0, half), some(half, half), down]
    return [start, qkv, lambda: attend(z, r, 0, 8), out, ffn, down]


def forward(z, r):
    for step in forward_steps(z, r):
        step()


def attend_back(z, r):
    t = z.tokens // 2
    r.key_grad[...] = jnp.zeros_like(r.key_grad)
    r.value_grad[...] = jnp.zeros_like(r.value_grad)
    first, second = slice(0, t), slice(t, 2 * t)

    def one(m, parity):
        h = 2 * m + parity
        g = h // GROUP
        cols = at(m * LANES, LANES)
        key, value = r.keys_turned.at[g], r.values.at[parity, g]
        d1, d2 = r.heads_grad[first, cols], r.heads_grad[second, cols]
        q1, q2 = r.query[first, cols], r.query[second, cols]
        a, b, c = r.weights[h, 0], r.weights[h, 1], r.weights[h, 2]
        fa, fb, fc = a.astype(F32), b.astype(F32), c.astype(F32)
        ga, gb, gc = nt(value[first, :], d1), nt(value[first, :], d2), nt(value[second, :], d2)
        ta, tb, tc = fa * ga, fb * gb, fc * gc
        da = jnp.sum(ta, axis=0, keepdims=True)
        db = jnp.sum(tb, axis=0, keepdims=True) + jnp.sum(tc, axis=0, keepdims=True)
        sa, sb, sc = (ta - fa * da).astype(BF), (tb - fb * db).astype(BF), (tc - fc * db).astype(BF)
        r.value_grad[parity, g, first, :] += nn(a, d1) + nn(b, d2)
        r.value_grad[parity, g, second, :] += nn(c, d2)
        r.key_grad[parity, g, first, :] += nn(sa, q1) + nn(sb, q2)
        r.key_grad[parity, g, second, :] += nn(sc, q2)
        return nn(key[:, :t], sa), nn(key[:, :t], sb) + nn(key[:, t:], sc)

    def put(m, low, high):
        cols = at(m * LANES, LANES)
        r.query_grad[first, cols] = jnp.concatenate([low[0], high[0]], axis=0).T
        r.query_grad[second, cols] = jnp.concatenate([low[1], high[1]], axis=0).T

    last = QUERY_HEADS // 2
    loop(last, lambda m: put(m, one(m, 0), one(m, 1)), unroll=True)
    empty = jnp.zeros((HEAD, t), F32)
    put(last, one(last, 0), (empty, empty))


def unrotate_qkv(z, r):
    def unrotate(i):
        rows = at(i * 64, 64)
        lo = half_mask(64)
        c, s = r.cos[rows, :], r.sin[rows, :]

        def turn(v):
            return v * c - swap_pairs(v) * s

        def joined(ref, g):
            a, b = ref[0, g, rows, :], ref[1, g, rows, :]
            return jnp.where(lo, a + pltpu.roll(b, HEAD, 1), 0.0), jnp.where(lo, 0.0, b + pltpu.roll(a, HEAD, 1))

        def put(m, v):
            r.qkv_back[rows, m * LANES : (m + 1) * LANES] = v.astype(BF)

        k = [joined(r.key_grad, g) for g in range(KEY_HEADS)]
        v = [joined(r.value_grad, g) for g in range(KEY_HEADS)]
        scale = HEAD**-0.5
        for m in range(7):
            put(m, turn(r.query_grad[rows, m * LANES : (m + 1) * LANES] * scale))
        last = jnp.where(lo, r.query_grad[rows, 7 * LANES : 8 * LANES] * scale, 0.0)
        put(7, turn(last + k[0][1]))
        put(8, turn(k[1][0] + k[2][1]))
        put(9, turn(k[3][0] + k[4][1]))
        put(10, v[0][0] + v[1][1])
        put(11, v[2][0] + v[3][1])
        put(12, v[4][0])

    loop(z.tokens // 64, unrotate, unroll=True)


def backward_steps(z, r):
    ffn_grad = r.ffn_grad

    def rounded():
        def body(i):
            rows = at(i * 64, 64)
            ffn_grad[rows, :] = r.grad[rows, :].astype(BF)

        if r.grad is not ffn_grad:
            loop(z.tokens // 64, body, unroll=True)

    def ffn():
        r.need_down()
        r.need_kept()

        def body(n):
            cols = at(n * 512, 512)
            back = nt(ffn_grad[...], r.w_down[cols, :])
            gate = r.gate[:, cols].astype(F32)
            up = r.up[:, cols].astype(F32)
            s = jax.nn.sigmoid(gate)
            r.gate[:, cols] = (back * up * s * (1.0 + gate * (1.0 - s))).astype(BF)
            r.up[:, cols] = (back * gate * s).astype(BF)

        loop(z.hidden // 512, body, unroll=True)
        r.ffn_done()

    def into():
        r.need_gate()

        def body(n):
            cols = at(n * 512, 512)
            r.normed_grad[:, cols] = nn(r.gate[...], r.w_gate[:, cols]) + nn(r.up[...], r.w_up[:, cols])

        loop(z.padded // 512, body, unroll=True)

    def norm2():
        r.need_middle()
        normalize_back(z, r.middle, r.gains[1:2, :], r.normed_grad, r.grad, r.middle_grad, r.gain_out.at[1])

        def body(i):
            rows = at(i * 64, 64)
            r.attn_back[rows, :] = r.middle_grad[rows, :].astype(BF)

        loop(z.tokens // 64, body, unroll=True)
        r.norm2_done()

    def out():
        r.need_attention()
        r.need_out()
        w = z.heads
        for start, size in ((0, 512), (512, w - 512)):
            cols = slice(start, start + size)
            back = nt(r.attn_back[...], r.w_out[cols, :])
            r.heads_grad[:, cols] = back.astype(BF)
        r.heads_grad[:, w:] = jnp.zeros((z.tokens, z.padded - w), BF)

    def attention():
        attend_back(z, r)
        r.attention_done()

    def unrotate():
        unrotate_qkv(z, r)
        r.unrotate_done()

    def qkv():
        r.need_qkv()
        for n in range(2):
            cols = slice(n * 512, (n + 1) * 512)
            r.normed_grad[:, cols] = nn(r.qkv_back[:, : z.qkv], r.w_qkv[:, cols])

    def norm1():
        normalize_back(z, r.state, r.gains[0:1, :], r.normed_grad, r.middle_grad, r.grad_in, r.gain_out.at[0])

    return [rounded, ffn, into, norm2, out, attention, unrotate, qkv, norm1]


def backward(z, r):
    for step in backward_steps(z, r):
        step()


def kept_shapes(z):
    t, d, f = z.tokens, z.padded, z.hidden
    return dict(
        query=((t, d), BF),
        keys=((2, KEY_HEADS, t, LANES), BF),
        values=((2, KEY_HEADS, t, LANES), BF),
        keys_turned=((KEY_HEADS, HEAD, t), BF),
        weights=((QUERY_HEADS, 3, t // 2, t // 2), BF),
        heads=((t, d), BF),
        middle=((t, d), F32),
        gate=((t, f), BF),
        up=((t, f), BF),
    )


def layer_shapes(z):
    t, d, f = z.tokens, z.padded, z.hidden
    return dict(kept_shapes(z), normed=((t, d), BF), normed2=((t, d), BF), hidden=((t, f), BF), values_turned=((KEY_HEADS, HEAD, t), BF))


def weight_shapes(z):
    d, f = z.padded, z.hidden
    return dict(w_qkv=((z.qkv, d), BF), w_out=((z.heads, d), BF), w_gate=((f, d), BF), w_up=((f, d), BF), w_down=((f, d), BF))


def tables(z):
    t, d = z.tokens, z.padded
    return dict(gains=((2, z.width), F32), cos=((t, LANES), F32), sin=((t, LANES), F32))


def blocks_shape(z):
    return ((2, 2, z.n, 2, z.rows, BLOCK), BF)


def rows_first(z):
    t, d, f = z.tokens, z.padded, z.hidden
    left = dict(qkv_back=((t, z.qkv_padded), BF), heads=((t, d), BF), gate=((t, f), BF), up=((t, f), BF), hidden=((t, f), BF))
    right = dict(normed=((t, d), BF), attn_back=((t, d), BF), normed2=((t, d), BF), ffn_grad=((t, d), BF))
    return left, right


def make_call(name, body, ins, outs, scratch, in_vmem, sems, **params):
    n_in, n_out, n_s = list(ins), list(outs), list(scratch)

    def kernel(*refs):
        a, b, c = len(n_in), len(n_in) + len(n_out), len(n_in) + len(n_out) + len(n_s)
        group = lambda names, part: types.SimpleNamespace(**dict(zip(names, part)))
        body(group(n_in, refs[:a]), group(n_out, refs[a:b]), group(n_s, refs[b:c]), refs[c:])

    spec = lambda n: pl.BlockSpec(memory_space=pltpu.VMEM if n in in_vmem else pl.ANY)
    call = pl.pallas_call(
        kernel,
        out_shape=[jax.ShapeDtypeStruct(*outs[n]) for n in n_out],
        in_specs=[spec(n) for n in n_in],
        out_specs=[spec(n) for n in n_out],
        scratch_shapes=[pltpu.VMEM(*scratch[n]) for n in n_s] + [pltpu.SemaphoreType.DMA(s) for s in sems],
        compiler_params=pltpu.CompilerParams(vmem_limit_bytes=VMEM_BYTES, **params),
        name=name,
    )
    return lambda **vals: dict(zip(n_out, call(*[vals[n] for n in n_in])))


class Copies:
    def __init__(self, sems):
        self.sems, self.used, self.open = sems, 0, {}

    def start(self, src, dst):
        key = self.used
        self.used += 1
        self.open[key] = pltpu.make_async_copy(src, dst, self.sems.at[key])
        self.open[key].start()
        return key

    def wait(self, keys):
        for key in keys:
            if key in self.open:
                self.open.pop(key).wait()

    def later(self, keys):
        return lambda: self.wait(keys)

    def finish(self):
        self.wait(list(self.open))


SMALL = ("gains", "cos", "sin", "tokens")


def pad_into(z, target, source, turned=True):
    target[...] = jnp.zeros(target.shape, target.dtype)
    for q in range(4):
        part = slice(q * z.quarter, (q + 1) * z.quarter)
        value = source[part, :].astype(F32).T.astype(target.dtype) if turned else source[:, part]
        target[:, q * BLOCK : q * BLOCK + z.quarter] = value


def unpad_into(z, target, value, first=0):
    for q in range(value.shape[1] // BLOCK):
        start = (first + q) * z.quarter
        target[start : start + z.quarter, :] = value[:, q * BLOCK : (q + 1) * BLOCK].T[: z.quarter, :]


def middle_kernel(z):
    t, d = z.tokens, z.padded
    kept = kept_shapes(z)
    ins = dict(tables(z), tokens=((t, d), BF), state=((t, d), F32), cotangent=((z.width, t), BF))
    ins.update(gathered=blocks_shape(z), dense_qkv=((z.qkv, d), BF), dense_out=((z.heads, d), BF))
    ins.update({"first_" + n: v for n, v in kept.items()})
    left, right = rows_first(z)
    both = dict(left, **right)
    outs = dict(result=((z.width, t), F32), grad_in=((z.width, t), F32), gain=((8, d), F32))
    outs.update({n + "2": v for n, v in both.items()})
    outs.update({n + "1": both[n] for n in ("qkv_back", "attn_back", "gate", "up", "ffn_grad")})
    scratch = dict(layer_shapes(z), **weight_shapes(z), state=((t, d), F32), grad=((t, d), BF))
    scratch.update(qkv=((t, z.qkv_padded), F32), plain=((z.width, t), F32), gain_out=((2, 8, d), F32), gains=((2, d), F32))
    scratch.update(key_grad=((2, KEY_HEADS, t, LANES), F32), value_grad=((2, KEY_HEADS, t, LANES), F32))

    def body(i, o, s, sems):
        cps = Copies(sems[0])
        state = cps.start(i.state, s.state)
        qkv = cps.start(i.dense_qkv, s.w_qkv)
        pad_into(z, s.gains, i.gains, False)
        s.gain_out[...] = jnp.zeros_like(s.gain_out)
        none = lambda: None
        r = types.SimpleNamespace(**vars(s))
        vars(r).update(cos=i.cos, sin=i.sin, chunk=512, halves=False)
        r.gate_block = lambda n: s.w_gate[at(n * 512, 512), :]
        r.up_block = lambda n: s.w_up[at(n * 512, 512), :]

        def down():
            for n in range(2):
                cols = slice(n * 512, (n + 1) * 512)
                unpad_into(z, s.plain, s.middle[:, cols] + nn(s.hidden[...], s.w_down[:, cols]), 2 * n)

        r.down = down
        cps.wait([state])

        def need_qkv():
            cps.wait([qkv])
            vars(r).update(start_weights(z, cps, i, s))

        r.need_qkv = need_qkv
        forward(z, r)
        sent = dict(plain=cps.start(s.plain, o.result))
        for n, target in (("normed", o.normed2), ("normed2", o.normed22), ("hidden", o.hidden2), ("heads", o.heads2)):
            sent[n] = cps.start(getattr(s, n), target)
        pad_into(z, s.grad, i.cotangent)
        sent["grad"] = cps.start(s.grad, o.ffn_grad2)
        wait = lambda *names: (lambda: cps.wait([sent[n] for n in names]))

        back = types.SimpleNamespace(**vars(r))
        back.qkv_back = s.hidden.at[:, : z.qkv_padded]
        vars(back).update(heads_grad=s.normed2, attn_back=s.normed, normed_grad=s.qkv.at[:, :d], middle_grad=s.middle, query_grad=s.qkv.at[:, :d], grad_in=s.state)
        vars(back).update(ffn_grad=s.grad, need_kept=none, need_middle=wait("normed"), need_attention=wait("normed2"), need_qkv=none)
        loads = {}

        def send(n, source, target):
            sent[n] = cps.start(source, target)

        def load(n):
            loads[n] = cps.start(getattr(i, "first_" + n), getattr(s, n))

        def ffn_done():
            send("gate", s.gate, o.gate2)
            send("up", s.up, o.up2)

        def attention_done():
            wait("gate", "up", "heads", "hidden")()
            for n in ("gate", "up", "heads", "query", "keys", "values", "keys_turned", "weights"):
                load(n)

        back.ffn_done, back.attention_done = ffn_done, attention_done
        back.norm2_done = lambda: send("attn_back", s.normed, o.attn_back2)
        back.unrotate_done = lambda: send("qkv_back", back.qkv_back, o.qkv_back2)
        backward(z, back)
        load("middle")
        wait("grad")()

        first = types.SimpleNamespace(**vars(back))
        vars(first).update(grad=s.state, state=s.grad)
        first.need_kept = cps.later([loads["gate"], loads["up"]])
        first.need_middle = lambda: (cps.wait([loads["middle"]]), wait("attn_back")())
        first.need_attention = cps.later([loads[n] for n in ("heads", "query", "keys", "values", "keys_turned", "weights")])

        def ffn_done1():
            cps.start(s.gate, o.gate1)
            cps.start(s.up, o.up1)
            send("grad", s.grad, o.ffn_grad1)

        def attention_done1():
            wait("grad", "qkv_back")()
            send("tokens", i.tokens, s.grad)

        first.ffn_done, first.attention_done = ffn_done1, attention_done1
        first.norm2_done = lambda: send("attn_back", s.normed, o.attn_back1)
        first.unrotate_done = lambda: send("qkv_back", back.qkv_back, o.qkv_back1)
        first.need_qkv = lambda: wait("tokens")()
        backward(z, first)
        wait("plain")()
        unpad_into(z, s.plain, s.state[...])
        cps.start(s.plain, o.grad_in)
        o.gain[...] = jnp.zeros_like(o.gain)
        o.gain[0:1, :] = jnp.sum(s.gain_out[0], axis=0, keepdims=True)
        o.gain[1:2, :] = jnp.sum(s.gain_out[1], axis=0, keepdims=True)
        cps.finish()

    return make_call("second_layer", body, ins, outs, scratch, ("gains", "cos", "sin", "cotangent", "gain"), [(80,)])


def start_weights(z, cps, i, s):
    def blocks(w, k):
        w = w.reshape(z.n, 2, z.blocks[k], z.padded)
        rows = pl.ds(z.starts[k], z.blocks[k])
        return [cps.start(i.gathered.at[q // 2, q % 2, :, :, rows], w.at[:, :, :, q * BLOCK : (q + 1) * BLOCK]) for q in range(4)]

    out = [cps.start(i.dense_out, s.w_out)]
    gate = blocks(s.w_gate, 2) + blocks(s.w_up, 3)
    down = blocks(s.w_down, 4)
    return dict(need_out=cps.later(out), need_gate=cps.later(gate), need_down=cps.later(down))


class Place:
    def __init__(self, n):
        mp, w = lax.axis_index("mp"), lax.axis_index("wide")
        self.n = n
        self.x, self.y, self.c, self.z = lax.rem(mp, 2), mp // 2, lax.rem(w, 2), w // 2
        self.axes = ["y", "x"] + z_orders(n)

    def coordinate(self, axis):
        if axis[0] == "z":
            return lax.rem(self.z // 2 ** int(axis[1:]), 2)
        return getattr(self, axis)

    def partner(self, axis):
        away = 1 - 2 * self.coordinate(axis)
        x, y, c, z = self.x, self.y, self.c, self.z
        if axis == "x":
            x = x + away
        elif axis == "y":
            y = y + away
        elif axis == "c":
            c = c + away
        else:
            z = z + away * 2 ** int(axis[1:])
        return {"mp": y * 2 + x, "wide": z * 2 + c}

    def dev(self, z):
        return {"mp": self.y * 2 + self.x, "wide": z * 2 + self.c}

    def signal(self, device):
        pl.semaphore_signal(pltpu.get_barrier_semaphore(), inc=1, device_id=device, device_id_type=MESH)

    def greet_line(self):
        for axis in "xyc":
            self.signal(self.partner(axis))

        @pl.when(self.z > 0)
        def _():
            self.signal(self.dev(self.z - 1))

        @pl.when(self.z < self.n - 1)
        def _():
            self.signal(self.dev(self.z + 1))

    def met_line(self):
        count = 3 + jnp.where(self.z > 0, 1, 0) + jnp.where(self.z < self.n - 1, 1, 0)
        pl.semaphore_wait(pltpu.get_barrier_semaphore(), count)

    def greet(self):
        for axis in self.axes + ["c"]:
            self.signal(self.partner(axis))

    def met(self):
        pl.semaphore_wait(pltpu.get_barrier_semaphore(), len(self.axes) + 1)


def run_stages(entries):
    for entry in sorted(entries, key=lambda e: e[:2]):
        entry[2]()


def shares(units, weights):
    out, done, used = [], 0, 0
    for w in weights:
        done += w
        end = round(units * done / sum(weights))
        out.append(end - used)
        used = end
    return out


def row_chunks(start, rows, parts, orders, first=0):
    out, r = [], start
    for k, units in enumerate(shares(rows // 16, parts)):
        turn = orders[(first + k) % len(orders)]
        for order, u in zip(turn, shares(units, [1] * len(turn))):
            if u:
                out.append((r, 16 * u, order, k))
                r += 16 * u
    return out


GATHER_ORDERS = (("xzy", "yzx"), ("zxy", "zyx"), ("yzx", "xzy"))
GATHER_PARTS = (1,) * 8
GATHER_TIMES = ((-1.57, 1.06, 2.26, 0.735, 0.09, 1.42, 1.91), (-1.17, -0.17, 0.63, 0.84, 2.35, 2.68, 3.05))
STEP_GAP = 0.45


def along(p, axes, free, turned, rows):
    mine = [p.coordinate(a) for a in axes]
    return tuple(slice(None) if a in free else 1 - v if a == turned else v for a, v in zip(axes, mine)) + rows


def gather_plan(p, g, k, piece, ss, rs):
    r0, rc, order, _ = piece
    n, rows = p.n, pl.ds(r0, rc)
    a1, a2 = [a for a in order if a != "z"]
    z_first = order[0] == "z"

    def one(zo, other=False):
        x = 1 - p.x if other and a1 == "x" else p.x
        y = 1 - p.y if other and a1 == "y" else p.y
        return g.at[y, x, zo, p.c, rows]

    def pair(zo, other=False, c=None):
        c = p.c if c is None else c
        if a1 == "x":
            return g.at[1 - p.y if other else p.y, :, zo, c, rows]
        return g.at[:, 1 - p.x if other else p.x, zo, c, rows]

    def copy(ref, dev, s, r):
        return pltpu.make_async_remote_copy(src_ref=ref, dst_ref=ref, send_sem=ss.at[k, s], recv_sem=rs.at[k, r], device_id=dev, device_id_type=MESH)

    along = one if z_first else pair
    up = lambda zo: copy(along(zo), p.dev(p.z + 1), zo, zo)
    down = lambda zo: copy(along(zo), p.dev(p.z - 1), n + zo, zo)
    line_in = lambda zo: copy(along(zo), p.partner("c"), zo, zo)
    first = lambda zo, other=False: copy(one(zo, other), p.partner(a1), 2 * n + zo, n + zo)
    second = lambda zo, other=False: copy(pair(zo, other), p.partner(a2), 3 * n + zo, 2 * n + zo)

    def sibling(other, c=None):
        c = p.c if c is None else c
        if a1 == "x":
            part = g.at[1 - p.y if other else p.y, :, :, c, rows]
        else:
            part = g.at[:, 1 - p.x if other else p.x, :, c, rows]
        o = 1 if other else 0
        return copy(part, p.partner("c"), 4 * n + o, 3 * n + o)

    def line(zo):
        @pl.when((zo <= p.z) & (p.z < n - 1))
        def _():
            up(zo).start()

        @pl.when((zo >= p.z) & (p.z > 0))
        def _():
            down(zo).start()

    def at_distance(d, body):
        @pl.when(p.z - d >= 0)
        def _():
            body(p.z - d)

        @pl.when(p.z + d < n)
        def _():
            body(p.z + d)

    stages = []
    times = GATHER_TIMES[1 if z_first else 0]
    hop_time, step = times[1:3] if z_first else times[2:4]
    last_hop = hop_time + (n - 2) * step
    if z_first:

        def start():
            line(p.z)
            first(p.z).start()

        stages.append((times[0], start))
        for d in range(1, n):

            def hop(d=d):
                def body(zo):
                    line_in(zo).wait_recv()
                    line(zo)
                    first(zo).start()

                at_distance(d, body)

            stages.append((hop_time + (d - 1) * step, hop))

        def cross():
            for zo in range(n):
                first(zo, True).wait_recv()
                second(zo).start()

        stages.append((last_hop + times[3], cross))
    else:

        def start():
            first(p.z).start()

        def meet():
            first(p.z, True).wait_recv()
            line(p.z)
            second(p.z).start()

        stages += [(times[0], start), (times[1], meet)]
        for d in range(1, n):

            def hop(d=d):
                def body(zo):
                    line_in(zo).wait_recv()
                    line(zo)
                    second(zo).start()

                at_distance(d, body)

            stages.append((hop_time + (d - 1) * step, hop))

    def halfway():
        sibling(False).start()

    def arrived():
        for zo in range(n):
            second(zo, True).wait_recv()
        sibling(True).start()

    def done():
        sibling(False, 1 - p.c).wait_recv()
        sibling(True, 1 - p.c).wait_recv()

    def drain():
        for zo in range(n):

            @pl.when((zo <= p.z) & (p.z < n - 1))
            def _():
                up(zo).wait_send()

            @pl.when((zo >= p.z) & (p.z > 0))
            def _():
                down(zo).wait_send()

            second(zo).wait_send()
            if z_first:
                first(zo).wait_send()
        if not z_first:
            first(p.z).wait_send()
        sibling(False).wait_send()
        sibling(True).wait_send()

    return stages + [(last_hop + at_time, f) for at_time, f in zip(times[-3:], (halfway, arrived, done))], drain


def stage_times(table, count):
    more = count - len(table)
    return list(table[:-2]) + [table[-3] + 1 + k for k in range(more)] + [v + more for v in table[-2:]]


def first_kernel(z):
    t, d, n = z.tokens, z.padded, z.n
    pieces = row_chunks(0, z.rows, GATHER_PARTS, GATHER_ORDERS)
    layer = layer_shapes(z)
    shards = weight_shards(z, BF)
    ins = dict(tables(z), tokens=((z.width, t), BF), **shards)
    outs = dict({m: v for m, v in layer.items() if m != "values_turned"}, start=((t, d), BF), result=((t, d), F32), gathered=blocks_shape(z), dense_qkv=((z.qkv, d), BF), dense_out=((z.heads, d), BF))
    scratch = dict(layer, result=((t, d), F32), qkv=((t, z.qkv_padded), F32), blocks=blocks_shape(z))
    scratch.update(w_qkv=((z.qkv, d), BF), w_out=((z.heads, d), BF), start=((t, d), BF), gains=((2, d), F32))

    def body(i, o, s, sems):
        local, ss, rs = sems
        cps = Copies(local)
        p = Place(n)
        p.greet_line()
        for k, name in enumerate(shards):
            w = getattr(i, name)[...]
            rows = z.starts[k]
            s.blocks[p.y, p.x, p.z, p.c, rows : rows + z.blocks[k], :] = jnp.zeros((z.blocks[k], BLOCK), BF)
            s.blocks[p.y, p.x, p.z, p.c, rows : rows + z.rows_of[k], : z.quarter] = w
        p.met_line()

        def dense(k, target):
            per = z.rows_of[k]
            for j in range(z.wide):
                for q in range(4):
                    rows = s.blocks[q // 2, q % 2, j // 2, j % 2, z.starts[k] : z.starts[k] + per, :]
                    target[j * per : (j + 1) * per, q * BLOCK : (q + 1) * BLOCK] = rows

        def block(k):
            start, per, some = z.starts[k], z.rows_of[k], z.group // 2

            def read(j):
                rows = []
                for e in range(z.group):
                    quarters = [s.blocks[q // 2, q % 2, j * some + e // 2, e % 2, start : start + per, :] for q in range(4)]
                    rows.append(jnp.concatenate(quarters, axis=1))
                return jnp.concatenate(rows, axis=0)

            return read

        none = lambda: None
        r = types.SimpleNamespace(**vars(s))
        vars(r).update(cos=i.cos, sin=i.sin, state=s.start, chunk=640, halves=True)
        vars(r).update(gate_block=block(2), up_block=block(3), need_gate=none, need_down=none)

        def need_qkv():
            dense(0, s.w_qkv)
            cps.start(s.w_qkv, o.dense_qkv)

        def need_out():
            dense(1, s.w_out)
            cps.start(s.w_out, o.dense_out)

        def down():
            read = block(4)
            s.result[...] = s.middle[...]

            def add(j):
                s.result[...] += nn(s.hidden[:, at(j * 640, 640)], read(j))

            loop(z.hidden // 640, add)

        vars(r).update(need_qkv=need_qkv, need_out=need_out, down=down)
        steps = forward_steps(z, r)

        def begin():
            pad_into(z, s.gains, i.gains, False)
            pad_into(z, s.start, i.tokens)
            cps.start(s.start, o.start)
            forward_start()

        forward_start, steps[0] = steps[0], begin
        plans = [gather_plan(p, s.blocks, k, piece, ss, rs) for k, piece in enumerate(pieces)]
        entries = [(pieces[k][3] + at_time, k, f) for k, (stages, _) in enumerate(plans) for at_time, f in stages]
        done = [pieces[k][3] + stages[-1][0] for k, (stages, _) in enumerate(plans)]
        ready = [max(at_time for at_time, piece in zip(done, pieces) if piece[0] < e) for e in (z.starts + (z.rows,))[1:]]
        times = [0.5]
        for k in (0, 0, 0, 0, 0, 1, 3, 3, 4):
            times.append(max(ready[k] + 0.5, times[-1] + STEP_GAP))
        entries += [(at_time, -1, f) for at_time, f in zip(times, steps)]

        def out_of(part):
            rows = [p for p in pieces if p[3] == part]
            span = pl.ds(rows[0][0], sum(p[1] for p in rows))
            return lambda: cps.start(s.blocks.at[:, :, :, :, span], o.gathered.at[:, :, :, :, span])

        for part in range(len(GATHER_PARTS)):
            entries.append((max(at_time for at_time, piece in zip(done, pieces) if piece[3] == part), 100 + part, out_of(part)))

        def keep(*names):
            return lambda: [cps.start(getattr(s, m), getattr(o, m)) for m in names]

        def keep_half(k):
            cols = slice(k * z.hidden // 2, (k + 1) * z.hidden // 2)
            return lambda: [cps.start(getattr(s, m).at[:, cols], getattr(o, m).at[:, cols]) for m in ("gate", "up", "hidden")]

        entries += [(times[5], 0, keep("normed", "query", "keys", "values", "keys_turned", "weights", "heads"))]
        entries += [(times[6], 0, keep("middle", "normed2")), (times[7], 0, keep_half(0)), (times[8], 0, keep_half(1))]
        run_stages(entries)
        cps.start(s.result, o.result)
        for _, drain in plans:
            drain()
        cps.finish()

    sems = [(40,), (len(pieces), 4 * n + 2), (len(pieces), 3 * n + 2)]
    return make_call("first_layer", body, ins, outs, scratch, SMALL + tuple(shards), sems, collective_id=1, has_side_effects=True)


def z_orders(n):
    return ["z%d" % k for k in reversed(range(n.bit_length() - 1))]


def reduce_orders(n):
    z = z_orders(n)[::-1]
    half = len(z) // 2
    first, second = [(b,) + tuple(z[:half]) + (a,) + tuple(z[half:]) for a, b in ("xy", "yx")]
    return ((first, second), (second, first))


REDUCE_WEIGHTS = (1, 4, 0, 2, 3)
REDUCE_PARTS = (2, 1, 3, 3, 3)
REDUCE_TIMES = (0.8, 2.4, 4.2, 6.0, 8.0)
WORK_LEAD, WORK_STEP = 0.77, 0.146


def weight_shards(z, kind):
    names = ("w_qkv_shard", "w_out_shard", "w_gate_shard", "w_up_shard", "w_down_shard")
    return {name: ((rows, z.quarter), kind) for name, rows in zip(names, z.rows_of)}


def add_into(target, extra):
    target[...] = target[...] + extra[...].astype(target.dtype)


def reduce_plan(p, t, from_sibling, bufs, out, k, piece, ss, rs):
    r0, rc, order, _ = piece
    axes, last = p.axes, len(order) - 1
    rows = pl.ds(r0, rc)

    def part(ref, s, other):
        return ref.at[along(p, axes, order[s + 1 :], order[s] if other else None, (rows,))]

    def step(s):
        return pltpu.make_async_remote_copy(
            src_ref=part(t, s, True),
            dst_ref=bufs[s].at[(slice(None),) * (last - s) + (rows,)],
            send_sem=ss.at[k, s],
            recv_sem=rs.at[k, s],
            device_id=p.partner(order[s]),
            device_id_type=MESH,
        )

    def meet():
        add_into(part(t, 0, True), part(from_sibling, 0, True))
        step(0).start()
        add_into(part(t, 0, False), part(from_sibling, 0, False))

    def follow(s):
        step(s - 1).wait_recv()
        left = [a for a in axes if a in order[s:]]
        for other in (True, False):
            side = 1 - p.coordinate(order[s]) if other else p.coordinate(order[s])
            index = tuple(side if a == order[s] else slice(None) for a in left) + (rows,)
            add_into(part(t, s, other), bufs[s - 1].at[index])
            if other:
                step(s).start()

    def finish():
        step(last).wait_recv()
        out[rows, :] = part(t, last, False)[...].astype(F32) + bufs[last][rows, :].astype(F32)

    def drain():
        for s in range(last + 1):
            step(s).wait_send()

    return [meet] + [functools.partial(follow, s) for s in range(1, last + 1)] + [finish], drain


def last_kernel(z):
    t, d, n = z.tokens, z.padded, z.n
    left, right = rows_first(z)
    both = dict(left, **right)
    ins = {m + k: v for m, v in both.items() for k in "12"}
    ins.update(gain=((8, d), F32))
    outs = dict(sums=((z.rows, BLOCK), F32), gain_sums=((8, d), F32))
    two = lambda v: ((2 * t, v[0][1]), BF)
    scratch = {m: two(v) for m, v in both.items() if m not in ("gate", "up")}
    stage = max(z.rows_of)
    scratch.update(
        t=((2, 2, n, z.rows, BLOCK), BF),
        staged=((STAGED, 2, 2, stage, BLOCK), BF),
        from_sibling=((2, 2, n, z.rows, BLOCK), BF),
        gain_sent=((n.bit_length() + 2, 8, d), F32),
        gain_in=((n.bit_length() + 2, 8, d), F32),
    )
    pairs = 2 + n.bit_length() - 1
    for k in range(pairs):
        scratch["step%d" % k] = ((2,) * (pairs - 1 - k) + (z.rows, BLOCK), BF)
    order, parts = REDUCE_WEIGHTS, REDUCE_PARTS
    pieces, starts = [], {}
    slot = 1
    for k in order:
        starts[k] = slot
        for r0, rc, way, part in row_chunks(z.starts[k], z.blocks[k], (1,) * parts[k], reduce_orders(n), slot):
            pieces.append((r0, rc, way, slot + part, k))
        slot += parts[k]

    def body(i, o, s, sems):
        local, ss, rs, sib_s, sib_r, gain_s, gain_r = sems
        cps = Copies(local)
        need = {}

        names = (("qkv_back", "normed"), ("heads", "attn_back"), ("gate", "normed2"), ("up", "normed2"), ("hidden", "ffn_grad"))
        in_hidden = ("hidden", "gate", "up")

        def load(k):
            for m in names[k]:
                if m not in need:
                    target = s.hidden if m in in_hidden else getattr(s, m)
                    need[m] = cps.later([cps.start(getattr(i, m + a), target.at[pl.ds((2 - int(a)) * t, t)]) for a in "12"])

        load(order[0])
        p = Place(n)
        p.greet()
        count = [0]

        def sibling(k, zo, slot):
            rows = pl.ds(z.starts[k], z.blocks[k])
            return pltpu.make_async_remote_copy(
                src_ref=s.staged.at[slot, :, :, pl.ds(0, z.blocks[k])],
                dst_ref=s.from_sibling.at[:, :, zo, rows],
                send_sem=sib_s.at[slot],
                recv_sem=sib_r.at[k, zo],
                device_id=p.partner("c"),
                device_id_type=MESH,
            )

        sent = {}

        def put(k, zo, slot, a, b):
            per = z.rows_of[k]
            own, other = jnp.where(p.c == 0, a, b).astype(BF), jnp.where(p.c == 0, b, a).astype(BF)
            for q in range(4):
                lanes = slice(q * BLOCK, (q + 1) * BLOCK)
                s.t[q // 2, q % 2, zo, z.starts[k] : z.starts[k] + per, :] = own[:, lanes]
                s.staged[slot, q // 2, q % 2, :per, :] = other[:, lanes]

        some = [1, 1] + [z.group // 2] * 3

        def work(k, first):
            per = z.rows_of[k]

            def run():
                if first == 0:
                    load(k)
                    for m in names[k]:
                        need[m]()
                    after = order[order.index(k) + 1 :][:1]
                    if after and not (names[k][0] in in_hidden and names[after[0]][0] in in_hidden):
                        load(after[0])
                m_left = (s.qkv_back, s.heads, s.hidden, s.hidden, s.hidden)[k]
                m_right = (s.normed, s.attn_back, s.normed2, s.normed2, s.ffn_grad)[k]
                width = 2 * per * some[k]
                value = tn(m_left[:, first * 2 * per : first * 2 * per + width], m_right[...])
                for e in range(some[k]):
                    zo = first + e
                    slot = count[0] % STAGED
                    if slot in sent:
                        sent.pop(slot).wait_send()
                    count[0] += 1
                    put(k, zo, slot, value[2 * e * per : (2 * e + 1) * per], value[(2 * e + 1) * per : (2 * e + 2) * per])
                    if count[0] == 1:
                        p.met()
                    sent[slot] = sibling(k, zo, slot)
                    sent[slot].start()

            return run

        latest = REDUCE_TIMES[0] - 0.01
        entries = []
        for k in order:
            for first in range(0, n, some[k]):
                at_time = starts[k] + min(first * 4 / n * WORK_STEP * parts[k] - WORK_LEAD, latest)
                entries.append((at_time, -1, work(k, first)))
        met = set()

        def after_sibling(k, f):
            def run():
                if k not in met:
                    met.add(k)
                    for zo in range(n):
                        sibling(k, zo, 0).wait_recv()
                f()

            return run

        cube = lambda ref: ref.reshape((2,) * pairs + (z.rows, BLOCK))
        bufs = [getattr(s, "step%d" % k) for k in range(pairs)]
        plans = [reduce_plan(p, cube(s.t), cube(s.from_sibling), bufs, o.sums, k, piece[:4], ss, rs) for k, piece in enumerate(pieces)]
        when = stage_times(REDUCE_TIMES, pairs + 1)
        for k, (stages, _) in enumerate(plans):
            stages[0] = after_sibling(pieces[k][4], stages[0])
        entries += [(pieces[k][3] + at_time, k, f) for k, (stages, _) in enumerate(plans) for at_time, f in zip(when, stages)]
        stages, gains_drain = gain_plan(p, i.gain, s, o.gain_sums, gain_s, gain_r)
        entries += [(1 + k, 100, f) for k, f in enumerate(stages)]
        run_stages(entries)
        for _, drain in plans:
            drain()
        for c in sent.values():
            c.wait_send()
        gains_drain()
        cps.finish()

    sems = [(40,), (len(pieces), pairs), (len(pieces), pairs), (STAGED,), (5, n), (pairs + 1,), (pairs + 1,)]
    return make_call("gradients", body, ins, outs, scratch, ("gain", "sums", "gain_sums"), sems, collective_id=2, has_side_effects=True)


STAGED = 4


def gain_plan(p, mine, s, out, ss, rs):
    axes = ["c"] + p.axes

    def exchange(k):
        return pltpu.make_async_remote_copy(
            src_ref=s.gain_sent.at[k], dst_ref=s.gain_in.at[k], send_sem=ss.at[k], recv_sem=rs.at[k], device_id=p.partner(axes[k]), device_id_type=MESH
        )

    def begin():
        s.gain_sent[0] = mine[...]
        exchange(0).start()

    def step(k):
        exchange(k).wait_recv()
        total = s.gain_sent[k] + s.gain_in[k]
        if k + 1 < len(axes):
            s.gain_sent[k + 1] = total
            exchange(k + 1).start()
        else:
            out[...] = total

    def drain():
        for k in range(len(axes)):
            exchange(k).wait_send()

    return [begin] + [functools.partial(step, k) for k in range(len(axes))], drain


def unpack_kernel(z):
    shards = weight_shards(z, F32)
    ins = dict(sums=((z.rows, BLOCK), F32), gain_sums=((8, z.padded), F32))
    outs = dict(shards, gain_grads=((2, z.width), F32))

    def body(i, o, s, sems):
        for k, name in enumerate(shards):
            getattr(o, name)[...] = i.sums[z.starts[k] : z.starts[k] + z.rows_of[k], : z.quarter]
        for q in range(4):
            o.gain_grads[:, q * z.quarter : (q + 1) * z.quarter] = i.gain_sums[:2, q * BLOCK : q * BLOCK + z.quarter]

    return make_call("unpack", body, ins, outs, {}, tuple(ins) + tuple(outs), [])


def rotary_tables(count_of_rows):
    position = np.arange(count_of_rows, dtype=np.float32)
    inverse = np.exp(np.arange(HEAD // 2, dtype=np.float32) * np.float32(-2.0 * math.log(10000.0) / HEAD))
    angle = position[:, None] * inverse[None, :]
    cos, sin = np.cos(angle), np.sin(angle)
    return np.concatenate([cos] * 4, axis=1), np.concatenate([-sin, sin] * 2, axis=1)


def local(wide, tokens, cotangent, norm_gains, w_qkv, w_out, w_gate, w_up, w_down):
    z = Sizes(tokens.shape[0], tokens.shape[1], w_qkv.shape[1] * wide, w_out.shape[0] * wide, w_gate.shape[1] * wide, wide)
    cos, sin = rotary_tables(z.tokens)
    small = dict(gains=norm_gains, cos=jnp.asarray(cos), sin=jnp.asarray(sin))
    shards = dict(zip(weight_shards(z, BF), (w_qkv.T, w_out, w_gate.T, w_up.T, w_down)))
    one = first_kernel(z)(tokens=tokens.T, **small, **shards)
    kept = {"first_" + n: one[n] for n in kept_shapes(z)}
    weights = {n: one[n] for n in ("gathered", "dense_qkv", "dense_out")}
    two = middle_kernel(z)(tokens=one["start"], state=one["result"], cotangent=cotangent.T, **small, **kept, **weights)
    factors = {n + "1": one[n] for n in ("normed", "normed2", "heads", "hidden")}
    out = unpack_kernel(z)(**last_kernel(z)(**factors, **two))
    grads = [out[n] for n in weight_shards(z, F32)]
    return (two["result"].T, two["grad_in"].T, out["gain_grads"], grads[0].T, grads[1], grads[2].T, grads[3].T, grads[4])


def solution(mesh):
    return jax.shard_map(
        functools.partial(local, mesh.shape["wide"]),
        mesh=mesh,
        in_specs=(
            P(("mp", "wide"), None),
            P(("mp", "wide"), None),
            P(),
            P("mp", "wide"),
            P("wide", "mp"),
            P("mp", "wide"),
            P("mp", "wide"),
            P("wide", "mp"),
        ),
        out_specs=(
            P(("mp", "wide"), None),
            P(("mp", "wide"), None),
            P(),
            P("mp", "wide"),
            P("wide", "mp"),
            P("mp", "wide"),
            P("mp", "wide"),
            P("wide", "mp"),
        ),
        check_vma=False,
    )
```
